32 devices in a mesh: dp: 8 (over z, x), mp: 4 (over y, core).
Axes of the slice: x: 2, y: 2, z: 4, core: 2. Of those that a mesh axis runs over, the one named last changes fastest.
Arguments:
- clean_mel: bfloat16 [2, 8, 1024, 80], P(None, 'dp'), may hold values from -6 to 6
- noise_mel: bfloat16 [2, 8, 1024, 80], P(None, 'dp'), may hold values from -6 to 6
- lengths: int32 [2, 8], P(None, 'dp'), may hold values from 128 to 1024, as said below
- span_start: int32 [2, 8], P(None, 'dp'), may hold values from 0 to 308, as said below
- span_end: int32 [2, 8], P(None, 'dp'), may hold values from 1 to 1024, as said below
- phone_ids: int32 [2, 8, 1024], P(None, 'dp'), may hold values from 0 to 127
- flow_steps: int32 [2, 8], P(None, 'dp'), may hold values from 0 to 1000
- in_table: float32 [288, 1024], P(None, ('dp', 'mp')), may hold values from -0.5 to 0.5
- channel_rows: float32 [39, 1024], P(None, ('dp', 'mp')), as said below
- attn_qkv: float32 [1024, 3072], P('dp', 'mp'), may hold values from -0.1875 to 0.1875
- attn_out: float32 [1024, 1024], P('mp', 'dp'), may hold values from -0.375 to 0.375
- ffn_up: float32 [1024, 4096], P('dp', 'mp'), may hold values from -0.1875 to 0.1875
- ffn_down: float32 [4096, 1024], P('mp', 'dp'), may hold values from -0.09375 to 0.09375
- mel_head: float32 [1024, 80], P(('dp', 'mp')), may hold values from -0.1875 to 0.1875
- table_first: float32 [288, 1024], P(None, ('dp', 'mp')), may hold values from -1.9073486e-05 to 1.9073486e-05
- channel_first: float32 [39, 1024], P(None, ('dp', 'mp')), may hold values from -1.9073486e-05 to 1.9073486e-05
- qkv_first: float32 [1024, 3072], P('dp', 'mp'), may hold values from -1.9073486e-05 to 1.9073486e-05
- merge_first: float32 [1024, 1024], P('mp', 'dp'), may hold values from -1.9073486e-05 to 1.9073486e-05
- upward_first: float32 [1024, 4096], P('dp', 'mp'), may hold values from -1.9073486e-05 to 1.9073486e-05
- downward_first: float32 [4096, 1024], P('mp', 'dp'), may hold values from -1.9073486e-05 to 1.9073486e-05
- head_first: float32 [1024, 80], P(('dp', 'mp')), may hold values from -1.9073486e-05 to 1.9073486e-05
- table_second: float32 [288, 1024], P(None, ('dp', 'mp')), may hold values from 1.1538745e-13 to 4.615498e-13
- channel_second: float32 [39, 1024], P(None, ('dp', 'mp')), may hold values from 7.692497e-13 to 3.0769987e-12
- qkv_second: float32 [1024, 3072], P('dp', 'mp'), may hold values from 7.692497e-13 to 3.0769987e-12
- merge_second: float32 [1024, 1024], P('mp', 'dp'), may hold values from 7.692497e-13 to 3.0769987e-12
- upward_second: float32 [1024, 4096], P('dp', 'mp'), may hold values from 7.692497e-13 to 3.0769987e-12
- downward_second: float32 [4096, 1024], P('mp', 'dp'), may hold values from 7.692497e-13 to 3.0769987e-12
- head_second: float32 [1024, 80], P(('dp', 'mp')), may hold values from 7.692497e-13 to 3.0769987e-12
Outputs:
- loss: float32 [], replicated
- grad_norm: float32 [], replicated
- table_new: float32 [288, 1024], P(None, ('dp', 'mp'))
- table_first_new: float32 [288, 1024], P(None, ('dp', 'mp'))
- table_second_new: float32 [288, 1024], P(None, ('dp', 'mp'))
- channel_new: float32 [39, 1024], P(None, ('dp', 'mp'))
- channel_first_new: float32 [39, 1024], P(None, ('dp', 'mp'))
- channel_second_new: float32 [39, 1024], P(None, ('dp', 'mp'))
- qkv_new: float32 [1024, 3072], P('dp', 'mp')
- qkv_first_new: float32 [1024, 3072], P('dp', 'mp')
- qkv_second_new: float32 [1024, 3072], P('dp', 'mp')
- merge_new: float32 [1024, 1024], P('mp', 'dp')
- merge_first_new: float32 [1024, 1024], P('mp', 'dp')
- merge_second_new: float32 [1024, 1024], P('mp', 'dp')
- upward_new: float32 [1024, 4096], P('dp', 'mp')
- upward_first_new: float32 [1024, 4096], P('dp', 'mp')
- upward_second_new: float32 [1024, 4096], P('dp', 'mp')
- downward_new: float32 [4096, 1024], P('mp', 'dp')
- downward_first_new: float32 [4096, 1024], P('mp', 'dp')
- downward_second_new: float32 [4096, 1024], P('mp', 'dp')
- head_new: float32 [1024, 80], P(('dp', 'mp'))
- head_first_new: float32 [1024, 80], P(('dp', 'mp'))
- head_second_new: float32 [1024, 80], P(('dp', 'mp'))
The draws below stay inside these ranges and needn't reach their ends.
Inputs may be any that keep to these rules, and one draw needn't show every extreme that they name: `lengths`: in every draw some utterance has exactly 1024 frames. `span_start`: the span lies inside its utterance and covers about 70 to 100 percent of its frames. span_end is greater than span_start and at most the utterance's length. `channel_rows`: taps are of order one over the square root of 31; gains are near one.
All inputs are finite; a program needn't handle non-finite values.
Results may differ from the reference program's by a relative error of at most 0.015.
Values may be sent and summed in bfloat16 or wider, within the bound.
A program may use at most 512 MiB of HBM per device.

```python
import math
import jax
import jax.numpy as jnp
from jax import lax

D = 1024
HEADS = 16
HEAD_DIM = 64
FF = 4096
MEL = 80
PHONES = 128
KERNEL = 31
LEN = 1024
MICRO = 2
TSTEPS = 1000
STEP = 10
UTTS = 8
INPUTS = 288
NCH = 39
PTOTAL = 12999680
N_MP = 4


def lengths_from(key):
    inner = jax.random.fold_in(key, 11)
    first, second = jax.random.split(inner)
    base = jax.random.randint(first, (MICRO * UTTS,), LEN // 8, LEN + 1)
    pick = jax.random.randint(second, (), 0, MICRO * UTTS)
    base = jnp.where(jnp.arange(MICRO * UTTS) == pick, LEN, base)
    return base.reshape(MICRO, UTTS)


def spans_from(key):
    sizes = lengths_from(key)
    inner = jax.random.fold_in(key, 23)
    first, second = jax.random.split(inner)
    full = sizes == LEN
    share = jax.random.randint(first, (MICRO, UTTS), 70, 101)
    share = jnp.where(full, 70, share)
    width = jnp.maximum(sizes * share // 100, 1)
    begin = jax.random.randint(second, (MICRO, UTTS), 0, sizes - width + 1)
    begin = jnp.where(full, sizes - width, begin)
    return (begin, begin + width)


def draw_lengths(key, part):
    return lengths_from(key).astype(jnp.int32)


def draw_span_start(key, part):
    return spans_from(key)[0].astype(jnp.int32)


def draw_span_end(key, part):
    return spans_from(key)[1].astype(jnp.int32)


def draw_channel_rows(key, part):
    inner = jax.random.fold_in(key, 5)
    first, second = jax.random.split(inner)
    taps = jax.random.normal(first, (KERNEL, D), jnp.float32) * KERNEL ** (-0.5)
    noise = jax.random.normal(second, (8, D), jnp.float32)
    scales = jnp.array([0.15, 0.3, 0.15, 0.3, 0.15, 0.3, 0.3, 0.3], jnp.float32)
    offsets = jnp.array([1.0, 0.0, 1.0, 0.0, 1.0, 0.0, 0.0, 0.0], jnp.float32)
    vecs = offsets[:, None] + scales[:, None] * noise
    return jnp.concatenate([taps, vecs], axis=0).astype(jnp.float32)


def touch_ends(entries, rng, smallest, largest):
    extent = entries.shape
    spot = [jax.random.randint(jax.random.fold_in(rng, axis), (), 0, extent[axis]) for axis in range(len(extent))]
    entries = entries.at[tuple(spot)].set(smallest)
    longest = extent.index(max(extent))
    spot[longest] = (spot[longest] + 1) % extent[longest]
    return entries.at[tuple(spot)].set(largest)


def levels(own_key, extent, shards, low, high):
    def one(axis_at, parts):
        draws = jax.random.uniform(jax.random.fold_in(jax.random.fold_in(own_key, 6), axis_at), (parts,), jnp.float32, low / len(shards), high / len(shards))
        return jnp.repeat(jnp.exp(draws), extent[axis_at] // parts).reshape((-1,) + (1,) * (len(extent) - axis_at - 1))

    loudness = one(*shards[0])
    for cut in shards[1:]:
        loudness = loudness * one(*cut)
    return loudness


def bell_draw(rng, dims, scale, limit, cuts=(), kind=jnp.bfloat16):
    entries = jax.random.normal(rng, dims, jnp.float32) * scale
    if len(cuts) > 0:
        entries = levels(rng, dims, cuts, -0.22, 0.18) * entries
    return jnp.clip(entries, min=-limit, max=limit).astype(kind)


def setup_inputs(seed: int = 0) -> dict:
    streams_of = jax.random.split(jax.random.key(seed), 29)
    clean_mel = bell_draw(streams_of[0], (MICRO, UTTS, LEN, MEL), 1.0, 6.0, ((1, 8),))
    noise_mel = bell_draw(streams_of[1], (MICRO, UTTS, LEN, MEL), 1.0, 6.0, ((1, 8),))
    lengths = draw_lengths(jax.random.fold_in(streams_of[28], 71), 0)
    span_start = draw_span_start(jax.random.fold_in(streams_of[28], 71), 0)
    span_end = draw_span_end(jax.random.fold_in(streams_of[28], 71), 0)
    phone_ids = touch_ends(jax.random.randint(streams_of[5], (MICRO, UTTS, LEN), 0, PHONES), jax.random.fold_in(streams_of[5], 1), 0, PHONES - 1).astype(jnp.int32)
    flow_steps = touch_ends(jax.random.randint(streams_of[6], (MICRO, UTTS), 0, TSTEPS + 1), jax.random.fold_in(streams_of[6], 1), 0, TSTEPS).astype(jnp.int32)
    in_table = bell_draw(streams_of[7], (INPUTS, D), (2 * MEL) ** -0.5, 0.5, ((1, 32),), jnp.float32)
    channel_rows = draw_channel_rows(jax.random.fold_in(streams_of[28], 71), 0)
    attn_qkv = bell_draw(streams_of[9], (D, 3 * D), D ** -0.5, 0.1875, ((0, 8), (1, 4)), jnp.float32)
    attn_out = bell_draw(streams_of[10], (D, D), (D // 4) ** -0.5, 0.375, ((0, 4), (1, 8)), jnp.float32)
    ffn_up = bell_draw(streams_of[11], (D, FF), D ** -0.5, 0.1875, ((0, 8), (1, 4)), jnp.float32)
    ffn_down = bell_draw(streams_of[12], (FF, D), FF ** -0.5, 0.09375, ((0, 4), (1, 8)), jnp.float32)
    mel_head = bell_draw(streams_of[13], (D, MEL), D ** -0.5, 0.1875, ((0, 32),), jnp.float32)
    table_first = bell_draw(streams_of[14], (INPUTS, D), (0.011 * PTOTAL ** -0.5), 1.9073486328125e-05, ((1, 32),), jnp.float32)
    channel_first = bell_draw(streams_of[15], (NCH, D), (0.011 * PTOTAL ** -0.5), 1.9073486328125e-05, ((1, 32),), jnp.float32)
    qkv_first = bell_draw(streams_of[16], (D, 3 * D), (0.011 * PTOTAL ** -0.5), 1.9073486328125e-05, ((0, 8), (1, 4)), jnp.float32)
    merge_first = bell_draw(streams_of[17], (D, D), (0.011 * PTOTAL ** -0.5), 1.9073486328125e-05, ((0, 4), (1, 8)), jnp.float32)
    upward_first = bell_draw(streams_of[18], (D, FF), (0.011 * PTOTAL ** -0.5), 1.9073486328125e-05, ((0, 8), (1, 4)), jnp.float32)
    downward_first = bell_draw(streams_of[19], (FF, D), (0.011 * PTOTAL ** -0.5), 1.9073486328125e-05, ((0, 4), (1, 8)), jnp.float32)
    head_first = bell_draw(streams_of[20], (D, MEL), (0.011 * PTOTAL ** -0.5), 1.9073486328125e-05, ((0, 32),), jnp.float32)
    table_second = jnp.clip(jnp.exp(math.log(4.61549797946964e-13) - 1.3862944 * jax.random.uniform(streams_of[21], (INPUTS, D), jnp.float32) ** levels(streams_of[21], (INPUTS, D), ((1, 32),), -0.2, 0.2)), 1.15387449486741e-13, 4.61549797946964e-13)
    channel_second = jnp.clip(jnp.exp(math.log(3.076998725259905e-12) - 1.3862944 * jax.random.uniform(streams_of[22], (NCH, D), jnp.float32) ** levels(streams_of[22], (NCH, D), ((1, 32),), -0.2, 0.2)), 7.692496813149763e-13, 3.076998725259905e-12)
    qkv_second = jnp.clip(jnp.exp(math.log(3.076998725259905e-12) - 1.3862944 * jax.random.uniform(streams_of[23], (D, 3 * D), jnp.float32) ** levels(streams_of[23], (D, 3 * D), ((0, 8), (1, 4)), -0.2, 0.2)), 7.692496813149763e-13, 3.076998725259905e-12)
    merge_second = jnp.clip(jnp.exp(math.log(3.076998725259905e-12) - 1.3862944 * jax.random.uniform(streams_of[24], (D, D), jnp.float32) ** levels(streams_of[24], (D, D), ((0, 4), (1, 8)), -0.2, 0.2)), 7.692496813149763e-13, 3.076998725259905e-12)
    upward_second = jnp.clip(jnp.exp(math.log(3.076998725259905e-12) - 1.3862944 * jax.random.uniform(streams_of[25], (D, FF), jnp.float32) ** levels(streams_of[25], (D, FF), ((0, 8), (1, 4)), -0.2, 0.2)), 7.692496813149763e-13, 3.076998725259905e-12)
    downward_second = jnp.clip(jnp.exp(math.log(3.076998725259905e-12) - 1.3862944 * jax.random.uniform(streams_of[26], (FF, D), jnp.float32) ** levels(streams_of[26], (FF, D), ((0, 4), (1, 8)), -0.2, 0.2)), 7.692496813149763e-13, 3.076998725259905e-12)
    head_second = jnp.clip(jnp.exp(math.log(3.076998725259905e-12) - 1.3862944 * jax.random.uniform(streams_of[27], (D, MEL), jnp.float32) ** levels(streams_of[27], (D, MEL), ((0, 32),), -0.2, 0.2)), 7.692496813149763e-13, 3.076998725259905e-12)
    return {"clean_mel": clean_mel, "noise_mel": noise_mel, "lengths": lengths, "span_start": span_start, "span_end": span_end, "phone_ids": phone_ids, "flow_steps": flow_steps, "in_table": in_table, "channel_rows": channel_rows, "attn_qkv": attn_qkv, "attn_out": attn_out, "ffn_up": ffn_up, "ffn_down": ffn_down, "mel_head": mel_head, "table_first": table_first, "channel_first": channel_first, "qkv_first": qkv_first, "merge_first": merge_first, "upward_first": upward_first, "downward_first": downward_first, "head_first": head_first, "table_second": table_second, "channel_second": channel_second, "qkv_second": qkv_second, "merge_second": merge_second, "upward_second": upward_second, "downward_second": downward_second, "head_second": head_second}


@jax.custom_vjp
def low(v):
    return lax.optimization_barrier(v.astype(jnp.bfloat16)).astype(jnp.float32)

@jax.custom_vjp
def low_back(v):
    return v

def low_keep(v):
    return (low(v), None)

def low_pass(kept, grad):
    return (grad,)

def back_keep(v):
    return (v, None)

def back_low(kept, grad):
    return (low(grad),)
low.defvjp(low_keep, low_pass)
low_back.defvjp(back_keep, back_low)
SIGMA = 1e-05
BETA_ONE = 0.9
BETA_TWO = 0.999
EPSILON = 1e-08
DECAY = 0.01
RATE = 0.15
CLIP_AT = 0.1
NORM_EPS = 1e-05
HIGH = lax.Precision.HIGHEST

def matmul(left, right):
    return jnp.dot(left, right, precision=HIGH, preferred_element_type=jnp.float32)

def gelu(v):
    return jax.nn.gelu(v, approximate=True)

def layer_norm(v, gain, bias):
    centered = v - lax.optimization_barrier(jnp.mean(v, axis=-1, keepdims=True))
    spread = lax.optimization_barrier(jnp.mean(centered * centered, axis=-1, keepdims=True))
    return centered * lax.rsqrt(spread + NORM_EPS) * gain + bias

def conv_mix(hidden, taps, bias, valid):
    masked = hidden * valid[..., None]
    half = taps.shape[0] // 2
    length = hidden.shape[-2]
    widths = [(0, 0)] * (hidden.ndim - 2) + [(half, half), (0, 0)]
    padded = jnp.pad(masked, widths)
    total = jnp.zeros_like(hidden) + bias
    for offset in range(taps.shape[0]):
        total = total + taps[offset] * padded[..., offset:offset + length, :]
    return total

def front(hidden, channel, valid):
    vecs = channel[KERNEL:]
    inner = hidden + gelu(conv_mix(hidden, channel[:KERNEL], vecs[7], valid))
    return (inner, layer_norm(inner, vecs[0], vecs[1]))

def adam_update(weight, first, second, grad, factor):
    clipped = grad * factor
    first_new = BETA_ONE * first + (1.0 - BETA_ONE) * clipped
    second_new = BETA_TWO * second + (1.0 - BETA_TWO) * clipped * clipped
    first_hat = first_new / (1.0 - BETA_ONE ** STEP)
    second_hat = second_new / (1.0 - BETA_TWO ** STEP)
    weight_new = weight - RATE * (first_hat / (jnp.sqrt(second_hat) + EPSILON) + DECAY * weight)
    return (weight_new, first_new, second_new)

def utterance_loss(weights, features, valid, masked, target, scale):
    w_in, channel, w_qkv, w_out, w_up, w_down, w_head = weights
    start = low_back(matmul(features, w_in)) + channel[KERNEL + 6]
    inner, normed = front(start, channel, valid)
    act_one = low(normed)
    heads_dev = HEADS // N_MP
    cols = 3 * heads_dev * HEAD_DIM
    rows_head = heads_dev * HEAD_DIM
    width = FF // N_MP
    place = jnp.arange(LEN)
    distance = jnp.abs(place[:, None] - place[None, :]).astype(jnp.float32)
    attn = jnp.zeros((LEN, D), jnp.float32)
    for shard in range(N_MP):
        packed = matmul(low_back(act_one), w_qkv[:, shard * cols:(shard + 1) * cols])
        packed = low(low_back(packed)).reshape(LEN, heads_dev, 3, HEAD_DIM)
        query, key, value = (packed[:, :, 0], packed[:, :, 1], packed[:, :, 2])
        slopes = jnp.exp2(-8.0 * (shard * heads_dev + jnp.arange(heads_dev) + 1).astype(jnp.float32) / HEADS)
        raw = low_back(jnp.einsum('qhd,khd->hqk', query, key, precision=HIGH))
        score = raw * HEAD_DIM ** (-0.5) - slopes[:, None, None] * distance
        score = jnp.where(valid[None, None, :] > 0, score, -1000000000.0)
        prob = jax.nn.softmax(score, axis=-1)
        mixed = jnp.einsum('hqk,khd->qhd', low(prob), value, precision=HIGH)
        mixed = low(low_back(mixed)).reshape(LEN, rows_head)
        attn = attn + low(matmul(mixed, w_out[shard * rows_head:(shard + 1) * rows_head]))
    second = inner + low_back(attn)
    act_two = low(layer_norm(second, channel[KERNEL + 2], channel[KERNEL + 3]))
    ffn = jnp.zeros((LEN, D), jnp.float32)
    for shard in range(N_MP):
        hidden = low_back(matmul(low_back(act_two), w_up[:, shard * width:(shard + 1) * width]))
        activated = low(gelu(hidden))
        ffn = ffn + low(matmul(activated, w_down[shard * width:(shard + 1) * width]))
    third = second + low_back(ffn)
    act_three = low(layer_norm(third, channel[KERNEL + 4], channel[KERNEL + 5]))
    pred = low_back(matmul(act_three, w_head))
    error = pred - target
    return jnp.sum(masked[:, None] * error * error) * scale

def reference(clean_mel, noise_mel, lengths, span_start, span_end, phone_ids, flow_steps, in_table, channel_rows, attn_qkv, attn_out, ffn_up, ffn_down, mel_head, table_first, channel_first, qkv_first, merge_first, upward_first, downward_first, head_first, table_second, channel_second, qkv_second, merge_second, upward_second, downward_second, head_second):
    place = jnp.arange(LEN)
    valid = (place[None, None, :] < lengths[:, :, None]).astype(jnp.float32)
    masked = ((place[None, None, :] >= span_start[:, :, None]) & (place[None, None, :] < span_end[:, :, None])).astype(jnp.float32)
    counts = lax.optimization_barrier(jnp.sum(masked, axis=(1, 2)))
    scale = jnp.broadcast_to((1.0 / counts)[:, None], (MICRO, UTTS)).reshape(-1)
    tau = (flow_steps.astype(jnp.float32) / TSTEPS)[:, :, None, None]
    clean = clean_mel.astype(jnp.float32)
    noise = noise_mel.astype(jnp.float32)
    noisy = (1.0 - (1.0 - SIGMA) * tau) * noise + tau * clean
    context = clean * (valid * (1.0 - masked))[..., None]
    target = clean - (1.0 - SIGMA) * noise
    onehot = (phone_ids[..., None] == jnp.arange(PHONES)).astype(jnp.float32)
    features = jnp.concatenate([low(noisy), low(context), onehot], axis=-1).reshape(MICRO * UTTS, LEN, INPUTS)
    data = (features, valid.reshape(-1, LEN), masked.reshape(-1, LEN), target.reshape(-1, LEN, MEL), scale)
    masters = (in_table, channel_rows, attn_qkv, attn_out, ffn_up, ffn_down, mel_head)

    def total_loss(params):
        weights = tuple((low(w) for w in params))
        checked = jax.checkpoint(utterance_loss)
        return jnp.sum(lax.map(lambda item: checked(weights, *item), data))
    loss, pull = jax.vjp(total_loss, masters)
    grads = pull(jnp.ones_like(loss))[0]
    grad_norm = jnp.sqrt(sum((jnp.sum(g * g) for g in grads)))
    factor = CLIP_AT / jnp.maximum(grad_norm, CLIP_AT)
    firsts = (table_first, channel_first, qkv_first, merge_first, upward_first, downward_first, head_first)
    seconds = (table_second, channel_second, qkv_second, merge_second, upward_second, downward_second, head_second)
    tw, tm, tv = adam_update(masters[0], firsts[0], seconds[0], grads[0], factor)
    cw, cm, cv = adam_update(masters[1], firsts[1], seconds[1], grads[1], factor)
    qw, qm, qv = adam_update(masters[2], firsts[2], seconds[2], grads[2], factor)
    ow, om, ov = adam_update(masters[3], firsts[3], seconds[3], grads[3], factor)
    uw, um, uv = adam_update(masters[4], firsts[4], seconds[4], grads[4], factor)
    dw, dm, dv = adam_update(masters[5], firsts[5], seconds[5], grads[5], factor)
    hw, hm, hv = adam_update(masters[6], firsts[6], seconds[6], grads[6], factor)
    return (loss, grad_norm, tw, tm, tv, cw, cm, cv, qw, qm, qv, ow, om, ov, uw, um, uv, dw, dm, dv, hw, hm, hv)
```

```python
import jax
import jax.numpy as jnp
from jax import lax
from jax.sharding import PartitionSpec as P

HEADS = 16
HEAD_DIM = 64
PHONES = 128
KERNEL = 31
HALF = 15
PAD = 16
TSTEPS = 1000
STEP = 10

SIGMA = 1e-05
BETA_ONE = 0.9
BETA_TWO = 0.999
EPSILON = 1e-08
DECAY = 0.01
RATE = 0.15
CLIP_AT = 0.1
NORM_EPS = 1e-05
SCALE = HEAD_DIM**-0.5
bf = jnp.bfloat16
f32 = jnp.float32


def gelu(v):
    return jax.nn.gelu(v, approximate=True)


def gelu_back(v, dv):
    return jax.vjp(gelu, v)[1](dv)[0]


def dot(left, right):
    return jnp.dot(left, right, preferred_element_type=f32)


def tdot(left, right):
    return lax.dot_general(
        left, right, (((0,), (0,)), ((), ())), preferred_element_type=f32
    )


def rdot(left, right):
    return lax.dot_general(
        left, right, (((1,), (1,)), ((), ())), preferred_element_type=f32
    )


def norm_parts(v):
    centered = v - jnp.mean(v, axis=-1, keepdims=True)
    spread = jnp.mean(centered * centered, axis=-1, keepdims=True)
    r = lax.rsqrt(spread + NORM_EPS)
    return centered * r, r


def norm_back(da, xhat, r, gain):
    dgain = jnp.sum(da * xhat, axis=0)
    dbias = jnp.sum(da, axis=0)
    dx = da * gain
    dv = r * (
        dx
        - jnp.mean(dx, axis=-1, keepdims=True)
        - xhat * jnp.mean(dx * xhat, axis=-1, keepdims=True)
    )
    return dv, dgain, dbias


def adam_update(weight, first, second, grad, factor):
    clipped = grad * factor
    first_new = BETA_ONE * first + (1.0 - BETA_ONE) * clipped
    second_new = BETA_TWO * second + (1.0 - BETA_TWO) * clipped * clipped
    first_hat = first_new / (1.0 - BETA_ONE**STEP)
    second_hat = second_new / (1.0 - BETA_TWO**STEP)
    weight_new = weight - RATE * (first_hat / (jnp.sqrt(second_hat) + EPSILON) + DECAY * weight)
    return (weight_new, first_new, second_new)


def shards(
    clean_mel,
    noise_mel,
    lengths,
    span_start,
    span_end,
    phone_ids,
    flow_steps,
    in_table,
    channel_rows,
    attn_qkv,
    attn_out,
    ffn_up,
    ffn_down,
    mel_head,
    table_first,
    channel_first,
    qkv_first,
    merge_first,
    upward_first,
    downward_first,
    head_first,
    table_second,
    channel_second,
    qkv_second,
    merge_second,
    upward_second,
    downward_second,
    head_second,
):
    micro, units, length, mel = clean_mel.shape
    nmp = lax.axis_size("mp")
    seqs = nmp // micro
    rows = length // seqs
    mp = lax.axis_index("mp")
    batch = mp // seqs
    seq = mp % seqs
    base = seq * rows
    width = in_table.shape[0]
    nch = channel_rows.shape[0]

    c_qkv = attn_qkv.shape[1]
    c_out = attn_out.shape[0]
    c_up = ffn_up.shape[1]
    cuts = (c_qkv, c_qkv + c_out, c_qkv + c_out + c_up)

    thin = jnp.concatenate([in_table.T, channel_rows.T, mel_head], axis=1).astype(bf)
    thin = lax.all_gather(thin, ("dp", "mp"), axis=0, tiled=True)
    model = thin.shape[0]
    w_qkv = lax.all_gather(attn_qkv.astype(bf), ("mp", "dp"), axis=0, tiled=True)
    w_qkv = w_qkv.reshape(nmp, model, c_qkv)
    rest = jnp.concatenate([attn_out.T, ffn_up, ffn_down.T], axis=1).astype(bf)
    rest = lax.all_gather(rest, ("mp", "dp"), axis=0, tiled=True).reshape(nmp, model, -1)
    w_out = rest[:, :, :c_out]
    w_up = rest[:, :, c_out : c_out + c_up]
    w_down = rest[:, :, c_out + c_up :]
    w_in = thin[:, :width]
    channel = thin[:, width : width + nch].T.astype(f32)
    w_head = thin[:, width + nch :]
    taps = channel[:KERNEL]
    vecs = channel[KERNEL:]

    counts = lax.psum(jnp.sum((span_end - span_start).astype(f32), axis=1), "dp")
    count = lax.dynamic_index_in_dim(counts, batch, 0, keepdims=False)

    def mine(x):
        return lax.dynamic_index_in_dim(x, batch, 0, keepdims=False)[0]

    def widen(x):
        x = jnp.pad(mine(x), [(PAD, PAD)] + [(0, 0)] * (x.ndim - 3))
        return lax.dynamic_slice_in_dim(x, base, rows + 2 * PAD, 0)

    size = mine(lengths)
    first_frame = mine(span_start)
    last_frame = mine(span_end)
    place = base - PAD + jnp.arange(rows + 2 * PAD)
    valid_ext = ((place >= 0) & (place < size)).astype(f32)[:, None]
    masked_ext = ((place >= first_frame) & (place < last_frame)).astype(f32)[:, None]
    inside = slice(PAD, PAD + rows)
    valid = valid_ext[inside]
    masked = masked_ext[inside]
    tau = mine(flow_steps).astype(f32) / TSTEPS
    clean = widen(clean_mel).astype(f32)
    noise = widen(noise_mel).astype(f32)
    noisy = (1.0 - (1.0 - SIGMA) * tau) * noise + tau * clean
    context = clean * (valid_ext * (1.0 - masked_ext))
    target = (clean - (1.0 - SIGMA) * noise)[inside]
    onehot = (widen(phone_ids)[:, None] == jnp.arange(PHONES)).astype(bf)
    features_ext = jnp.concatenate([noisy.astype(bf), context.astype(bf), onehot], axis=-1)
    features = features_ext[inside]

    start_ext = rdot(features_ext, w_in) + vecs[6]
    hm = start_ext * valid_ext
    conv = jnp.zeros((rows, model), f32) + vecs[7]
    for k in range(KERNEL):
        conv = conv + taps[k] * hm[k + 1 : k + 1 + rows]
    first = start_ext[inside] + gelu(conv)
    x_one, r_one = norm_parts(first)
    act_one = (x_one * vecs[0] + vecs[1]).astype(bf)

    packed = jnp.einsum("rd,mdc->rmc", act_one, w_qkv, preferred_element_type=f32).astype(bf)
    packed = packed.reshape(rows, HEADS, 3, HEAD_DIM)
    query, key, value = packed[:, :, 0], packed[:, :, 1], packed[:, :, 2]
    groups = [[g * seqs + s for s in range(seqs)] for g in range(micro)]

    def shift(x, i):
        pairs = [(g[(s + i) % seqs], g[s]) for g in groups for s in range(seqs)]
        return lax.ppermute(x, "mp", pairs)

    def unshift(x, i):
        pairs = [(g[s], g[(s + i) % seqs]) for g in groups for s in range(seqs)]
        return lax.ppermute(x, "mp", pairs)

    both = jnp.stack([key, value])
    both = jnp.concatenate([both] + [shift(both, i) for i in range(1, seqs)], axis=1)
    keys, values = both[0], both[1]
    blocks = (seq + jnp.arange(seqs)) % seqs
    key_place = (blocks[:, None] * rows + jnp.arange(rows)).reshape(-1)
    query_place = base + jnp.arange(rows)
    slopes = jnp.exp2(-8.0 * (jnp.arange(HEADS) + 1).astype(f32) / HEADS)
    distance = jnp.abs(query_place[:, None] - key_place[None, :]).astype(f32)
    raw = jnp.einsum("qhd,khd->hqk", query, keys, preferred_element_type=f32)
    score = raw * SCALE - slopes[:, None, None] * distance
    score = jnp.where((key_place < size)[None, None, :], score, -1000000000.0)
    top = jnp.max(score, axis=-1, keepdims=True)
    prob = jnp.exp(score - top)
    prob = prob / jnp.sum(prob, axis=-1, keepdims=True)
    prob_low = prob.astype(bf)
    mixed = jnp.einsum("hqk,khd->qhd", prob_low, values, preferred_element_type=f32)
    mixed = mixed.astype(bf).reshape(rows, nmp, c_out)
    attn = jnp.zeros((rows, model), f32)
    for m in range(nmp):
        attn = attn + rdot(mixed[:, m], w_out[m])
    second = first + attn

    x_two, r_two = norm_parts(second)
    act_two = (x_two * vecs[2] + vecs[3]).astype(bf)
    ffn = jnp.zeros((rows, model), f32)
    hidden = []
    active = []
    for m in range(nmp):
        hidden.append(dot(act_two, w_up[m]))
        active.append(gelu(hidden[m]).astype(bf))
        ffn = ffn + rdot(active[m], w_down[m])
    third = second + ffn

    x_three, r_three = norm_parts(third)
    act_three = (x_three * vecs[4] + vecs[5]).astype(bf)
    error = dot(act_three, w_head) - target
    weight_rows = masked / count
    loss_local = jnp.sum(weight_rows * error * error)
    dpred = (2.0 * weight_rows * error).astype(bf)
    g_head = tdot(act_three, dpred)
    dthird, dg3, db3 = norm_back(rdot(dpred, w_head), x_three, r_three, vecs[4])

    dffn = dthird.astype(bf)
    da2 = jnp.zeros((rows, model), f32)
    g_up, g_down = [], []
    for m in range(nmp):
        dhid = gelu_back(hidden[m], dot(dffn, w_down[m])).astype(bf)
        g_down.append(tdot(dffn, active[m]).astype(bf))
        g_up.append(tdot(act_two, dhid).astype(bf))
        da2 = da2 + rdot(dhid, w_up[m])
    dnorm, dg2, db2 = norm_back(da2, x_two, r_two, vecs[2])
    dsecond = dthird + dnorm

    dattn = dsecond.astype(bf)
    g_out = [tdot(dattn, mixed[:, m]).astype(bf) for m in range(nmp)]
    dmixed = jnp.stack([dot(dattn, w_out[m]) for m in range(nmp)], axis=1)
    dmixed = dmixed.astype(bf).reshape(rows, HEADS, HEAD_DIM)
    dvalues = jnp.einsum("hqk,qhd->khd", prob_low, dmixed, preferred_element_type=f32)
    dprob = jnp.einsum("qhd,khd->hqk", dmixed, values, preferred_element_type=f32)
    dscore = prob * (dprob - jnp.sum(prob * dprob, axis=-1, keepdims=True))
    draw = (dscore * SCALE).astype(bf)
    dquery = jnp.einsum("hqk,khd->qhd", draw, keys, preferred_element_type=f32)
    dkeys = jnp.einsum("hqk,qhd->khd", draw, query, preferred_element_type=f32)
    dboth = jnp.stack([dkeys, dvalues])
    total = dboth[:, :rows]
    for i in range(1, seqs):
        total = total + unshift(dboth[:, i * rows : (i + 1) * rows].astype(bf), i).astype(f32)
    dpacked = jnp.stack([dquery, total[0], total[1]], axis=2).astype(bf)
    dpacked = dpacked.reshape(rows, nmp, c_qkv)
    g_qkv = [tdot(act_one, dpacked[:, m]).astype(bf) for m in range(nmp)]
    da1 = jnp.zeros((rows, model), f32)
    for m in range(nmp):
        da1 = da1 + rdot(dpacked[:, m], w_qkv[m])

    dnorm, dg1, db1 = norm_back(da1, x_one, r_one, vecs[0])
    dfirst = dsecond + dnorm
    dconv = gelu_back(conv, dfirst)
    right = lax.ppermute(
        dconv[:PAD], "mp", [(g[s + 1], g[s]) for g in groups for s in range(seqs - 1)]
    )
    left = lax.ppermute(
        dconv[rows - PAD :], "mp", [(g[s], g[s + 1]) for g in groups for s in range(seqs - 1)]
    )
    dconv_ext = jnp.concatenate([left, dconv, right], axis=0)
    back = jnp.zeros((rows, model), f32)
    g_taps = []
    for k in range(KERNEL):
        back = back + taps[k] * dconv_ext[2 * PAD - 1 - k : 2 * PAD - 1 - k + rows]
        g_taps.append(jnp.sum(dconv * hm[k + 1 : k + 1 + rows], axis=0))
    dstart = dfirst + valid * back
    g_in = tdot(dstart.astype(bf), features)
    g_rows = g_taps + [dg1, db1, dg2, db2, dg3, db3, jnp.sum(dstart, axis=0), jnp.sum(dconv, axis=0)]
    g_chan = jnp.stack(g_rows, axis=1)

    g_thin = jnp.concatenate([g_in, g_chan, g_head], axis=1).astype(bf)
    g_rest = jnp.stack(
        [jnp.concatenate([g_up[m], g_down[m]], axis=1) for m in range(nmp)]
    ).reshape(nmp * model, -1)
    g_near = jnp.stack(
        [jnp.concatenate([g_qkv[m], g_out[m]], axis=1) for m in range(nmp)]
    ).reshape(nmp * model, -1)
    g_rest = lax.psum_scatter(g_rest, ("mp", "dp"), scatter_dimension=0, tiled=True).astype(f32)
    g_near = lax.psum_scatter(g_near, ("mp", "dp"), scatter_dimension=0, tiled=True).astype(f32)
    g_thin = lax.psum_scatter(g_thin, ("dp", "mp"), scatter_dimension=0, tiled=True).astype(f32)
    squares = jnp.sum(g_rest * g_rest) + jnp.sum(g_near * g_near) + jnp.sum(g_thin * g_thin)
    sums = lax.psum(jnp.stack([loss_local, squares]), ("dp", "mp"))
    loss = sums[0]
    grad_norm = jnp.sqrt(sums[1])
    factor = CLIP_AT / jnp.maximum(grad_norm, CLIP_AT)

    tw, tm, tv = adam_update(in_table, table_first, table_second, g_thin[:, :width].T, factor)
    cw, cm, cv = adam_update(
        channel_rows, channel_first, channel_second, g_thin[:, width : width + nch].T, factor
    )
    hw, hm_, hv = adam_update(mel_head, head_first, head_second, g_thin[:, width + nch :], factor)
    qw, qm, qv = adam_update(attn_qkv, qkv_first, qkv_second, g_near[:, :c_qkv], factor)
    ow, om, ov = adam_update(attn_out, merge_first, merge_second, g_near[:, c_qkv:].T, factor)
    uw, um, uv = adam_update(ffn_up, upward_first, upward_second, g_rest[:, :c_up], factor)
    dw, dm, dv = adam_update(ffn_down, downward_first, downward_second, g_rest[:, c_up:].T, factor)
    return (
        loss, grad_norm,
        tw, tm, tv, cw, cm, cv, qw, qm, qv, ow, om, ov, uw, um, uv, dw, dm, dv, hw, hm_, hv,
    )


def solution(mesh):
    wide = P(None, ("dp", "mp"))
    tall = P(("dp", "mp"), None)
    down = P("dp", "mp")
    flat = P("mp", "dp")
    weights = (wide, wide, down, flat, down, flat, tall)
    pair = P(None, "dp")
    data = (P(None, "dp", None, None), P(None, "dp", None, None), pair, pair, pair)
    data = data + (P(None, "dp", None), pair)
    return jax.shard_map(
        shards,
        mesh=mesh,
        in_specs=data + weights * 3,
        out_specs=(P(), P()) + tuple(w for w in weights for _ in range(3)),
        check_vma=False,
    )
```

```python
import functools

import jax
import jax.numpy as jnp
from jax import lax
from jax.experimental import pallas as pl
from jax.experimental.pallas import tpu as pltpu
from jax.sharding import PartitionSpec as P

HEADS = 16
HEAD_DIM = 64
PHONES = 128
KERNEL = 31
HALF = 15
PAD = 16
TSTEPS = 1000
STEP = 10

SIGMA = 1e-05
BETA_ONE = 0.9
BETA_TWO = 0.999
EPSILON = 1e-08
DECAY = 0.01
RATE = 0.15
CLIP_AT = 0.1
NORM_EPS = 1e-05
SCALE = HEAD_DIM**-0.5
bf = jnp.bfloat16
f32 = jnp.float32


def gelu(v):
    return jax.nn.gelu(v, approximate=True)


def gelu_back(v, dv):
    return jax.vjp(gelu, v)[1](dv)[0]


def dot(left, right):
    return jnp.dot(left, right, preferred_element_type=f32)


def tdot(left, right):
    return lax.dot_general(
        left, right, (((0,), (0,)), ((), ())), preferred_element_type=f32
    )


def rdot(left, right):
    return lax.dot_general(
        left, right, (((1,), (1,)), ((), ())), preferred_element_type=f32
    )


def norm_parts(v):
    centered = v - jnp.mean(v, axis=-1, keepdims=True)
    spread = jnp.mean(centered * centered, axis=-1, keepdims=True)
    r = lax.rsqrt(spread + NORM_EPS)
    return centered * r, r


def norm_back(da, xhat, r, gain):
    dgain = jnp.sum(da * xhat, axis=0)
    dbias = jnp.sum(da, axis=0)
    dx = da * gain
    dv = r * (
        dx
        - jnp.mean(dx, axis=-1, keepdims=True)
        - xhat * jnp.mean(dx * xhat, axis=-1, keepdims=True)
    )
    return dv, dgain, dbias


def adam_update(weight, first, second, grad, factor):
    clipped = grad * factor
    first_new = BETA_ONE * first + (1.0 - BETA_ONE) * clipped
    second_new = BETA_TWO * second + (1.0 - BETA_TWO) * clipped * clipped
    first_hat = first_new / (1.0 - BETA_ONE**STEP)
    second_hat = second_new / (1.0 - BETA_TWO**STEP)
    weight_new = weight - RATE * (first_hat / (jnp.sqrt(second_hat) + EPSILON) + DECAY * weight)
    return (weight_new, first_new, second_new)


MESH = pl.DeviceIdType.MESH
AXES = ("z", "x", "y", "c")


class Wires:
    def __init__(self, ndp, nmp):
        self.sizes = {"z": ndp // 2, "x": 2, "y": nmp // 2, "c": 2}
        dp = lax.axis_index("dp")
        mp = lax.axis_index("mp")
        self.at = {"z": dp // 2, "x": dp % 2, "y": mp // 2, "c": mp % 2}

    def peer(self, axis, k):
        at = dict(self.at)
        at[axis] = lax.rem(at[axis] + k, self.sizes[axis])
        return (at["z"] * 2 + at["x"], at["y"] * 2 + at["c"])

    def owner_mp(self, ky, kc):
        ny = self.sizes["y"]
        return lax.rem(self.at["y"] + ny - ky, ny) * 2 + lax.rem(self.at["c"] + 2 - kc, 2)

    def ring(self):
        return [self.peer(a, k) for a in AXES for k in range(1, self.sizes[a])]

    def near(self, k):
        nmp = self.sizes["y"] * self.sizes["c"]
        return (lax.axis_index("dp"), lax.rem(lax.axis_index("mp") + k, nmp))

    def far(self, k):
        ndp = self.sizes["z"] * self.sizes["x"]
        return (lax.rem(lax.axis_index("dp") + k, ndp), lax.axis_index("mp"))

    def greet(self, peers):
        barrier = pltpu.get_barrier_semaphore()
        for p in peers:
            pl.semaphore_signal(barrier, inc=1, device_id=p, device_id_type=MESH)
        pl.semaphore_wait(barrier, len(peers))


def slot_number(sizes, k):
    return ((k["z"] * sizes["x"] + k["x"]) * sizes["y"] + k["y"]) * sizes["c"] + k["c"]


def spread(sizes, order):
    slots = [(dict.fromkeys(AXES, 0), -1)]
    for stage, axis in enumerate(order):
        slots += [
            ({**k, axis: n}, stage) for n in range(1, sizes[axis]) for k, _ in list(slots)
        ]
    return slots


class Gather:
    def __init__(self, wires, order, own, slot, send, recv):
        self.wires, self.order, self.own, self.slot = wires, order, own, slot
        self.send, self.recv = send, recv
        self.slots = spread(wires.sizes, order)
        self.started = []

    def forward(self, source, k, stage):
        for later in range(stage + 1, len(self.order)):
            axis = self.order[later]
            for n in range(1, self.wires.sizes[axis]):
                there = {**k, axis: n}
                number = slot_number(self.wires.sizes, there)
                copy = pltpu.make_async_remote_copy(
                    source, self.slot(there, k), self.send.at[number], self.recv.at[number],
                    device_id=self.wires.peer(axis, n), device_id_type=MESH,
                )
                copy.start()
                self.started.append((copy, number))

    def begin(self):
        k, stage = self.slots[0]
        self.forward(self.own, k, stage)

    def arrive(self, index):
        k, stage = self.slots[index]
        number = slot_number(self.wires.sizes, k)
        here = self.slot(k, k)
        pltpu.make_async_remote_copy(
            here, here, self.send.at[number], self.recv.at[number],
            device_id=self.wires.peer("c", 1), device_id_type=MESH,
        ).wait_recv()
        self.forward(here, k, stage)

    def finish(self):
        for copy, _ in self.started:
            copy.wait_send()


class Reduce:
    def __init__(self, wires, order, source, landing, add, send, recv):
        self.wires, self.order = wires, order
        self.source, self.landing, self.add = source, landing, add
        self.send, self.recv = send, recv
        self.started = []
        slots = [k for k, _ in spread(wires.sizes, order[::-1])]
        self.stages = []
        for stage, axis in enumerate(order):
            self.stages.append([k for k in slots if k[axis]])
            slots = [k for k in slots if not k[axis]]

    def copy(self, stage, k):
        axis = self.order[stage]
        number = slot_number(self.wires.sizes, k)
        n = self.wires.sizes[axis]
        return pltpu.make_async_remote_copy(
            self.source(k, stage), self.landing(k, stage),
            self.send.at[number], self.recv.at[number],
            device_id=self.wires.peer(axis, (n - k[axis]) % n), device_id_type=MESH,
        )

    def leave(self, stage, k):
        copy = self.copy(stage, k)
        copy.start()
        self.started.append(copy)

    def begin(self):
        for k in self.stages[0]:
            self.leave(0, k)

    def arrive(self, stage, k):
        self.copy(stage, k).wait_recv()
        kept = {**k, self.order[stage]: 0}
        self.add(k, kept)
        last = k[self.order[stage]] == self.wires.sizes[self.order[stage]] - 1
        if last and stage + 1 < len(self.order) and kept[self.order[stage + 1]]:
            self.leave(stage + 1, kept)

    def finish(self):
        for copy in self.started:
            copy.wait_send()


FIRST = ("z", "x", "y", "c")
OTHER = ("z", "y", "x", "c")


def gather_kernel(ndp, nmp, *refs):
    owns, outs = refs[:3], refs[3:6]
    send, recv, local = refs[6:]
    wires = Wires(ndp, nmp)
    wires.greet(wires.ring())
    sizes = wires.sizes
    thin_rows = owns[0].shape[0]

    def thin_slot(k, sent):
        block = (k["z"] * sizes["x"] + k["x"]) * nmp + wires.owner_mp(sent["y"], sent["c"])
        return outs[0].at[pl.ds(pl.multiple_of(block * thin_rows, thin_rows), thin_rows)]

    def wide_slot(ref, rows, half):
        def slot(k, sent):
            start = (k["z"] * sizes["x"] + k["x"]) * 2 * rows + half * rows
            return ref.at[k["y"] * sizes["c"] + k["c"], pl.ds(start, rows)]

        return slot

    flows = [Gather(wires, FIRST, owns[0], thin_slot, send.at[0], recv.at[0])]
    for ref, out in zip(owns[1:], outs[1:]):
        rows = ref.shape[0] // 2
        for half, order in enumerate((FIRST, OTHER)):
            number = len(flows)
            own = ref.at[pl.ds(half * rows, rows)]
            slot = wide_slot(out, rows, half)
            flows.append(Gather(wires, order, own, slot, send.at[number], recv.at[number]))
    zero = dict.fromkeys(AXES, 0)
    kept = [pltpu.make_async_copy(f.own, f.slot(zero, zero), local.at[i]) for i, f in enumerate(flows)]
    for copy in kept:
        copy.start()
    for f in flows:
        f.begin()
    count = len(flows[0].slots)
    for group in (flows[:1], flows[1:3], flows[3:]):
        for index in range(1, count):
            for f in group:
                f.arrive(index)
    for copy in kept:
        copy.wait()
    for f in flows:
        f.finish()


def gather_all(thin, near, rest, ndp, nmp):
    model = near.shape[0] * ndp
    outs = (
        jax.ShapeDtypeStruct((model, thin.shape[1]), bf),
        jax.ShapeDtypeStruct((nmp, model, near.shape[1]), bf),
        jax.ShapeDtypeStruct((nmp, model, rest.shape[1]), bf),
    )
    return pl.pallas_call(
        functools.partial(gather_kernel, ndp, nmp),
        name="gather",
        out_shape=outs,
        in_specs=[pl.BlockSpec(memory_space=pl.ANY)] * 3,
        out_specs=[pl.BlockSpec(memory_space=pl.ANY)] * 3,
        scratch_shapes=[
            pltpu.SemaphoreType.DMA((5, ndp * nmp)),
            pltpu.SemaphoreType.DMA((5, ndp * nmp)),
            pltpu.SemaphoreType.DMA((5,)),
        ],
        compiler_params=pltpu.CompilerParams(collective_id=0, has_side_effects=True),
    )(thin, near, rest)


def total(ref):
    rows = 8

    def body(i, part):
        x = ref[pl.ds(i * rows, rows)]
        return part + x * x

    part = lax.fori_loop(0, ref.shape[0] // rows, body, jnp.zeros((rows, ref.shape[1]), f32))
    return jnp.sum(part)


def reduce_kernel(ndp, nmp, wide, *refs):
    count = wide + 1
    terms, loss = refs[:count], refs[count]
    outs, sums = refs[count + 1 : 2 * count + 1], refs[2 * count + 1]
    rest = refs[2 * count + 2 :]
    held, land = rest[:count], rest[count : 2 * count + wide]
    parts, send, recv, local, near_send, near_recv, far_send, far_recv = rest[2 * count + wide :]
    wires = Wires(ndp, nmp)
    sizes = wires.sizes
    nears = [wires.near(k) for k in range(1, nmp)]
    fars = [wires.far(k) for k in range(1, ndp)]
    wires.greet(nears + fars)
    flows = []
    loads = []

    def tile_add(out, target, source, rows):
        step = 16

        def body(i, _):
            here = pl.ds(pl.multiple_of(i * step, step), step)
            target_rows = target[here].astype(f32) + source[here].astype(f32)
            out[here] = target_rows.astype(out.dtype)
            return 0

        lax.fori_loop(0, rows // step, body, 0)

    def wide_flow(i, half, order):
        term, keep, out = terms[i], held[i], outs[i]
        rows = term.shape[1] // ndp // 2
        box = land[1 + 2 * (i - 1) + half]

        def place(k):
            return pl.ds((k["z"] * sizes["x"] + k["x"]) * 2 * rows + half * rows, rows)

        def source(k, stage):
            if stage == 0:
                return term.at[k["y"] * sizes["c"] + k["c"], place(k)]
            return keep.at[k["y"], place(k)]

        def landing(k, stage):
            return box.at[slot_number(sizes, k) - 1]

        def add(k, kept):
            target = keep.at[kept["y"], place(kept)]
            if any(kept.values()):
                tile_add(target, target, landing(k, 0), rows)
            else:
                target = out.at[pl.ds(half * rows, rows)]
                tile_add(target, target, landing(k, 0), rows)

        n = len(flows)
        flows.append(Reduce(wires, order, source, landing, add, send.at[n], recv.at[n]))

    def thin_flow(order):
        term, keep, out, box = terms[0], held[0], outs[0], land[0]
        rows = out.shape[0]

        def source(k, stage):
            block = (k["z"] * sizes["x"] + k["x"]) * nmp + wires.owner_mp(k["y"], k["c"])
            ref = term if stage == 0 else keep
            return ref.at[pl.ds(pl.multiple_of(block * rows, rows), rows)]

        def landing(k, stage):
            return box.at[slot_number(sizes, k) - 1]

        def add(k, kept):
            target = source(kept, 1)
            if any(kept.values()):
                tile_add(target, target, landing(k, 0), rows)
            else:
                tile_add(out, out, landing(k, 0), rows)

        n = len(flows)
        flows.append(Reduce(wires, order, source, landing, add, send.at[n], recv.at[n]))

    thin_flow(FIRST[::-1])
    for i in range(1, count):
        for half, order in enumerate((FIRST[::-1], OTHER[::-1])):
            wide_flow(i, half, order)
    for i in range(count):
        if i == 0:
            loads.append(pltpu.make_async_copy(terms[0], held[0], local.at[0]))
        else:
            for ky in range(sizes["y"]):
                loads.append(
                    pltpu.make_async_copy(
                        terms[i].at[ky * sizes["c"]], held[i].at[ky], local.at[len(loads)]
                    )
                )
    for copy in loads:
        copy.start()
    for f in flows[1:] + flows[:1]:
        f.begin()
    for copy in loads:
        copy.wait()
    zero = dict.fromkeys(AXES, 0)
    for i in range(count):
        if i == 0:
            rows = outs[0].shape[0]
            block = wires.owner_mp(0, 0)
            outs[0][...] = held[0][pl.ds(pl.multiple_of(block * rows, rows), rows)].astype(f32)
        else:
            outs[i][...] = held[i][0, : outs[i].shape[0]].astype(f32)
    for stage in range(len(FIRST)):
        for pos in range(len(flows[0].stages[stage])):
            for f in flows[1:] + flows[:1]:
                f.arrive(stage, f.stages[stage][pos])
    for f in flows:
        f.finish()

    squares = total(outs[0])
    for out in outs[1:]:
        squares = squares + total(out)
    lanes = lax.broadcasted_iota(jnp.int32, (8, 128), 1)
    block = jnp.where(lanes == 1, squares, loss[...])
    for peers, sends, recvs, lower in (
        (nears, near_send, near_recv, 0),
        (fars, far_send, far_recv, nmp),
    ):
        parts[lower] = block
        copies = []
        for i, p in enumerate(peers):
            copy = pltpu.make_async_remote_copy(
                parts.at[lower], parts.at[lower + 1 + i], sends.at[i], recvs.at[i],
                device_id=p, device_id_type=MESH,
            )
            copy.start()
            copies.append(copy)
        for copy in copies:
            copy.wait()
        for i in range(len(peers)):
            block = block + parts[lower + 1 + i]
    sums[...] = block


def reduce_all(terms, loss, ndp, nmp):
    wide = len(terms) - 1
    thin = terms[0]
    slots = ndp * nmp - 1
    outs = [jax.ShapeDtypeStruct((thin.shape[0] // (ndp * nmp), thin.shape[1]), f32)]
    held = [pltpu.VMEM(thin.shape, bf)]
    land = [pltpu.VMEM((slots, thin.shape[0] // (ndp * nmp), thin.shape[1]), bf)]
    for t in terms[1:]:
        rows = t.shape[1] // ndp
        outs.append(jax.ShapeDtypeStruct((rows, t.shape[2]), f32))
        held.append(pltpu.VMEM((nmp // 2, t.shape[1], t.shape[2]), bf))
        land += [pltpu.VMEM((slots, rows // 2, t.shape[2]), bf)] * 2
    outs.append(jax.ShapeDtypeStruct((8, 128), f32))
    flows = 1 + 2 * wide
    dma = pltpu.SemaphoreType.DMA
    vmem = pl.BlockSpec(memory_space=pltpu.VMEM)
    return pl.pallas_call(
        functools.partial(reduce_kernel, ndp, nmp, wide),
        name="reduce",
        out_shape=outs,
        in_specs=[pl.BlockSpec(memory_space=pl.ANY)] * (wide + 1) + [vmem],
        out_specs=[vmem] * len(outs),
        scratch_shapes=held
        + land
        + [
            pltpu.VMEM((nmp + ndp, 8, 128), f32),
            dma((flows, ndp * nmp)),
            dma((flows, ndp * nmp)),
            dma((1 + wide * (nmp // 2),)),
            dma((nmp - 1,)),
            dma((nmp - 1,)),
            dma((ndp - 1,)),
            dma((ndp - 1,)),
        ],
        compiler_params=pltpu.CompilerParams(
            collective_id=1, has_side_effects=True, vmem_limit_bytes=60 << 20
        ),
    )(*terms, loss)


def shards(
    clean_mel,
    noise_mel,
    lengths,
    span_start,
    span_end,
    phone_ids,
    flow_steps,
    in_table,
    channel_rows,
    attn_qkv,
    attn_out,
    ffn_up,
    ffn_down,
    mel_head,
    table_first,
    channel_first,
    qkv_first,
    merge_first,
    upward_first,
    downward_first,
    head_first,
    table_second,
    channel_second,
    qkv_second,
    merge_second,
    upward_second,
    downward_second,
    head_second,
):
    micro, units, length, mel = clean_mel.shape
    nmp = lax.axis_size("mp")
    seqs = nmp // micro
    rows = length // seqs
    mp = lax.axis_index("mp")
    batch = mp // seqs
    seq = mp % seqs
    base = seq * rows
    width = in_table.shape[0]
    nch = channel_rows.shape[0]

    c_qkv = attn_qkv.shape[1]
    c_out = attn_out.shape[0]
    c_up = ffn_up.shape[1]

    ndp = lax.axis_size("dp")
    thin = jnp.concatenate([in_table.T, channel_rows.T, mel_head], axis=1).astype(bf)
    extra = -thin.shape[1] % 128
    thin = jnp.pad(thin, ((0, 0), (0, extra)))
    rest = jnp.concatenate([attn_out.T, ffn_up, ffn_down.T], axis=1).astype(bf)
    own = ndp * nmp <= 32 and seqs == 2
    if own:
        thin, w_qkv, rest = gather_all(thin, attn_qkv.astype(bf), rest, ndp, nmp)
        wires = Wires(ndp, nmp)
        owners = jnp.stack([wires.owner_mp(m // 2, m % 2) for m in range(nmp)])
    else:
        thin = lax.all_gather(thin, ("dp", "mp"), axis=0, tiled=True)
        w_qkv = lax.all_gather(attn_qkv.astype(bf), ("mp", "dp"), axis=0, tiled=True)
        w_qkv = w_qkv.reshape(nmp, -1, c_qkv)
        rest = lax.all_gather(rest, ("mp", "dp"), axis=0, tiled=True)
        rest = rest.reshape(nmp, -1, rest.shape[1])
        owners = jnp.arange(nmp)
    model = thin.shape[0]
    w_out = rest[:, :, :c_out]
    w_up = rest[:, :, c_out : c_out + c_up]
    w_down = rest[:, :, c_out + c_up :]
    w_in = thin[:, :width]
    channel = thin[:, width : width + nch].T.astype(f32)
    w_head = thin[:, width + nch : width + nch + mel]
    taps = channel[:KERNEL]
    vecs = channel[KERNEL:]

    counts = lax.psum(jnp.sum((span_end - span_start).astype(f32), axis=1), "dp")
    count = lax.dynamic_index_in_dim(counts, batch, 0, keepdims=False)

    def mine(x):
        return lax.dynamic_index_in_dim(x, batch, 0, keepdims=False)[0]

    def widen(x):
        x = jnp.pad(mine(x), [(PAD, PAD)] + [(0, 0)] * (x.ndim - 3))
        return lax.dynamic_slice_in_dim(x, base, rows + 2 * PAD, 0)

    size = mine(lengths)
    first_frame = mine(span_start)
    last_frame = mine(span_end)
    place = base - PAD + jnp.arange(rows + 2 * PAD)
    valid_ext = ((place >= 0) & (place < size)).astype(f32)[:, None]
    masked_ext = ((place >= first_frame) & (place < last_frame)).astype(f32)[:, None]
    inside = slice(PAD, PAD + rows)
    valid = valid_ext[inside]
    masked = masked_ext[inside]
    tau = mine(flow_steps).astype(f32) / TSTEPS
    clean = widen(clean_mel).astype(f32)
    noise = widen(noise_mel).astype(f32)
    noisy = (1.0 - (1.0 - SIGMA) * tau) * noise + tau * clean
    context = clean * (valid_ext * (1.0 - masked_ext))
    target = (clean - (1.0 - SIGMA) * noise)[inside]
    onehot = (widen(phone_ids)[:, None] == jnp.arange(PHONES)).astype(bf)
    features_ext = jnp.concatenate([noisy.astype(bf), context.astype(bf), onehot], axis=-1)
    features = features_ext[inside]

    start_ext = rdot(features_ext, w_in) + vecs[6]
    hm = start_ext * valid_ext
    conv = jnp.zeros((rows, model), f32) + vecs[7]
    for k in range(KERNEL):
        conv = conv + taps[k] * hm[k + 1 : k + 1 + rows]
    first = start_ext[inside] + gelu(conv)
    x_one, r_one = norm_parts(first)
    act_one = (x_one * vecs[0] + vecs[1]).astype(bf)

    packed = jnp.einsum("rd,mdc->rmc", act_one, w_qkv, preferred_element_type=f32).astype(bf)
    packed = packed.reshape(rows, HEADS, 3, HEAD_DIM)
    query, key, value = packed[:, :, 0], packed[:, :, 1], packed[:, :, 2]
    groups = [[g * seqs + s for s in range(seqs)] for g in range(micro)]

    def shift(x, i):
        pairs = [(g[(s + i) % seqs], g[s]) for g in groups for s in range(seqs)]
        return lax.ppermute(x, "mp", pairs)

    def unshift(x, i):
        pairs = [(g[s], g[(s + i) % seqs]) for g in groups for s in range(seqs)]
        return lax.ppermute(x, "mp", pairs)

    def swap(x):
        if not own:
            return x
        x = x.reshape(2, rows, nmp // 2, 2, -1)[:, :, :, ::-1]
        return x.reshape(2, rows, HEADS, HEAD_DIM)

    both = jnp.stack([key, value])
    both = jnp.concatenate([both] + [swap(shift(both, i)) for i in range(1, seqs)], axis=1)
    keys, values = both[0], both[1]
    blocks = (seq + jnp.arange(seqs)) % seqs
    key_place = (blocks[:, None] * rows + jnp.arange(rows)).reshape(-1)
    query_place = base + jnp.arange(rows)
    heads = (owners[:, None] * (HEADS // nmp) + jnp.arange(HEADS // nmp)).reshape(-1)
    slopes = jnp.exp2(-8.0 * (heads + 1).astype(f32) / HEADS)
    distance = jnp.abs(query_place[:, None] - key_place[None, :]).astype(f32)
    raw = jnp.einsum("qhd,khd->hqk", query, keys, preferred_element_type=f32)
    score = raw * SCALE - slopes[:, None, None] * distance
    score = jnp.where((key_place < size)[None, None, :], score, -1000000000.0)
    top = jnp.max(score, axis=-1, keepdims=True)
    prob = jnp.exp(score - top)
    prob = prob / jnp.sum(prob, axis=-1, keepdims=True)
    prob_low = prob.astype(bf)
    mixed = jnp.einsum("hqk,khd->qhd", prob_low, values, preferred_element_type=f32)
    mixed = mixed.astype(bf).reshape(rows, nmp, c_out)
    attn = jnp.zeros((rows, model), f32)
    for m in range(nmp):
        attn = attn + rdot(mixed[:, m], w_out[m])
    second = first + attn

    x_two, r_two = norm_parts(second)
    act_two = (x_two * vecs[2] + vecs[3]).astype(bf)
    ffn = jnp.zeros((rows, model), f32)
    hidden = []
    active = []
    for m in range(nmp):
        hidden.append(dot(act_two, w_up[m]))
        active.append(gelu(hidden[m]).astype(bf))
        ffn = ffn + rdot(active[m], w_down[m])
    third = second + ffn

    x_three, r_three = norm_parts(third)
    act_three = (x_three * vecs[4] + vecs[5]).astype(bf)
    error = dot(act_three, w_head) - target
    weight_rows = masked / count
    loss_local = jnp.sum(weight_rows * error * error)
    dpred = (2.0 * weight_rows * error).astype(bf)
    g_head = tdot(act_three, dpred)
    dthird, dg3, db3 = norm_back(rdot(dpred, w_head), x_three, r_three, vecs[4])

    dffn = dthird.astype(bf)
    da2 = jnp.zeros((rows, model), f32)
    g_up, g_down = [], []
    for m in range(nmp):
        dhid = gelu_back(hidden[m], dot(dffn, w_down[m])).astype(bf)
        g_down.append(tdot(dffn, active[m]).astype(bf))
        g_up.append(tdot(act_two, dhid).astype(bf))
        da2 = da2 + rdot(dhid, w_up[m])
    dnorm, dg2, db2 = norm_back(da2, x_two, r_two, vecs[2])
    dsecond = dthird + dnorm

    dattn = dsecond.astype(bf)
    g_out = [tdot(dattn, mixed[:, m]).astype(bf) for m in range(nmp)]
    dmixed = jnp.stack([dot(dattn, w_out[m]) for m in range(nmp)], axis=1)
    dmixed = dmixed.astype(bf).reshape(rows, HEADS, HEAD_DIM)
    dvalues = jnp.einsum("hqk,qhd->khd", prob_low, dmixed, preferred_element_type=f32)
    dprob = jnp.einsum("qhd,khd->hqk", dmixed, values, preferred_element_type=f32)
    dscore = prob * (dprob - jnp.sum(prob * dprob, axis=-1, keepdims=True))
    draw = (dscore * SCALE).astype(bf)
    dquery = jnp.einsum("hqk,khd->qhd", draw, keys, preferred_element_type=f32)
    dkeys = jnp.einsum("hqk,qhd->khd", draw, query, preferred_element_type=f32)
    dboth = jnp.stack([dkeys, dvalues])
    parts = [dboth[:, i * rows : (i + 1) * rows] for i in range(seqs)]
    dboth = parts[0]
    for i in range(1, seqs):
        dboth = dboth + swap(unshift(parts[i].astype(bf), i).astype(f32))
    dpacked = jnp.stack([dquery, dboth[0], dboth[1]], axis=2).astype(bf)
    dpacked = dpacked.reshape(rows, nmp, c_qkv)
    g_qkv = [tdot(act_one, dpacked[:, m]).astype(bf) for m in range(nmp)]
    da1 = jnp.zeros((rows, model), f32)
    for m in range(nmp):
        da1 = da1 + rdot(dpacked[:, m], w_qkv[m])

    dnorm, dg1, db1 = norm_back(da1, x_one, r_one, vecs[0])
    dfirst = dsecond + dnorm
    dconv = gelu_back(conv, dfirst)
    right = lax.ppermute(
        dconv[:PAD], "mp", [(g[s + 1], g[s]) for g in groups for s in range(seqs - 1)]
    )
    left = lax.ppermute(
        dconv[rows - PAD :], "mp", [(g[s], g[s + 1]) for g in groups for s in range(seqs - 1)]
    )
    dconv_ext = jnp.concatenate([left, dconv, right], axis=0)
    back = jnp.zeros((rows, model), f32)
    g_taps = []
    for k in range(KERNEL):
        back = back + taps[k] * dconv_ext[2 * PAD - 1 - k : 2 * PAD - 1 - k + rows]
        g_taps.append(jnp.sum(dconv * hm[k + 1 : k + 1 + rows], axis=0))
    dstart = dfirst + valid * back
    g_in = tdot(dstart.astype(bf), features)
    g_rows = g_taps + [dg1, db1, dg2, db2, dg3, db3, jnp.sum(dstart, axis=0), jnp.sum(dconv, axis=0)]
    g_chan = jnp.stack(g_rows, axis=1)

    g_thin = jnp.concatenate([g_in, g_chan, g_head], axis=1).astype(bf)
    g_thin = jnp.pad(g_thin, ((0, 0), (0, extra)))
    lanes = lax.broadcasted_iota(jnp.int32, (8, 128), 1)
    loss_block = jnp.where(lanes == 0, loss_local, 0.0)
    terms = [g_thin, jnp.stack(g_up), jnp.stack(g_down), jnp.stack(g_qkv), jnp.stack(g_out)]
    if own:
        g_thin, g_up, g_down, g_qkv, g_out, sums = reduce_all(terms, loss_block, ndp, nmp)
    else:
        g_thin = lax.psum_scatter(g_thin, ("dp", "mp"), scatter_dimension=0, tiled=True)
        sums = [g_thin.astype(f32)] + [
            lax.psum_scatter(
                t.reshape(-1, t.shape[2]), ("mp", "dp"), scatter_dimension=0, tiled=True
            ).astype(f32)
            for t in terms[1:]
        ]
        g_thin, g_up, g_down, g_qkv, g_out = sums
        squares = sum(jnp.sum(g * g) for g in sums)
        sums = lax.psum(jnp.stack([loss_local, squares])[None], ("dp", "mp"))
    sums = sums[0]
    loss = sums[0]
    grad_norm = jnp.sqrt(sums[1])
    factor = CLIP_AT / jnp.maximum(grad_norm, CLIP_AT)

    tw, tm, tv = adam_update(in_table, table_first, table_second, g_thin[:, :width].T, factor)
    cw, cm, cv = adam_update(
        channel_rows, channel_first, channel_second, g_thin[:, width : width + nch].T, factor
    )
    hw, hm_, hv = adam_update(mel_head, head_first, head_second, g_thin[:, width + nch : width + nch + mel], factor)
    qw, qm, qv = adam_update(attn_qkv, qkv_first, qkv_second, g_qkv, factor)
    ow, om, ov = adam_update(attn_out, merge_first, merge_second, g_out.T, factor)
    uw, um, uv = adam_update(ffn_up, upward_first, upward_second, g_up, factor)
    dw, dm, dv = adam_update(ffn_down, downward_first, downward_second, g_down.T, factor)
    return (
        loss, grad_norm,
        tw, tm, tv, cw, cm, cv, qw, qm, qv, ow, om, ov, uw, um, uv, dw, dm, dv, hw, hm_, hv,
    )


def solution(mesh):
    wide = P(None, ("dp", "mp"))
    tall = P(("dp", "mp"), None)
    down = P("dp", "mp")
    flat = P("mp", "dp")
    weights = (wide, wide, down, flat, down, flat, tall)
    pair = P(None, "dp")
    data = (P(None, "dp", None, None), P(None, "dp", None, None), pair, pair, pair)
    data = data + (P(None, "dp", None), pair)
    return jax.shard_map(
        shards,
        mesh=mesh,
        in_specs=data + weights * 3,
        out_specs=(P(), P()) + tuple(w for w in weights for _ in range(3)),
        check_vma=False,
    )
```

```python
import functools
from typing import Any, NamedTuple

import jax
import jax.numpy as jnp
from jax import lax
from jax.experimental import pallas as pl
from jax.experimental.pallas import tpu as pltpu
from jax.sharding import PartitionSpec as P

HEADS = 16
HEAD_DIM = 64
PHONES = 128
KERNEL = 31
HALF = 15
PAD = 16
TSTEPS = 1000
STEP = 10

SIGMA = 1e-05
BETA_ONE = 0.9
BETA_TWO = 0.999
EPSILON = 1e-08
DECAY = 0.01
RATE = 0.15
CLIP_AT = 0.1
NORM_EPS = 1e-05
SCALE = HEAD_DIM**-0.5
bf = jnp.bfloat16
f32 = jnp.float32


def gelu(v):
    return jax.nn.gelu(v, approximate=True)


def gelu_back(v, dv):
    return jax.vjp(gelu, v)[1](dv)[0]


def dot(left, right):
    return jnp.dot(left, right, preferred_element_type=f32)


def tdot(left, right):
    return lax.dot_general(
        left, right, (((0,), (0,)), ((), ())), preferred_element_type=f32
    )


def rdot(left, right):
    return lax.dot_general(
        left, right, (((1,), (1,)), ((), ())), preferred_element_type=f32
    )


def norm_parts(v):
    centered = v - jnp.mean(v, axis=-1, keepdims=True)
    spread = jnp.mean(centered * centered, axis=-1, keepdims=True)
    r = lax.rsqrt(spread + NORM_EPS)
    return centered * r, r


def norm_back(da, xhat, r, gain):
    dgain = jnp.sum(da * xhat, axis=0)
    dbias = jnp.sum(da, axis=0)
    dx = da * gain
    dv = r * (
        dx
        - jnp.mean(dx, axis=-1, keepdims=True)
        - xhat * jnp.mean(dx * xhat, axis=-1, keepdims=True)
    )
    return dv, dgain, dbias


def adam_update(weight, first, second, grad, factor):
    clipped = grad * factor
    first_new = BETA_ONE * first + (1.0 - BETA_ONE) * clipped
    second_new = BETA_TWO * second + (1.0 - BETA_TWO) * clipped * clipped
    first_hat = first_new / (1.0 - BETA_ONE**STEP)
    second_hat = second_new / (1.0 - BETA_TWO**STEP)
    weight_new = weight - RATE * (first_hat / (jnp.sqrt(second_hat) + EPSILON) + DECAY * weight)
    return (weight_new, first_new, second_new)


MESH = pl.DeviceIdType.MESH
AXES = ("z", "x", "y", "c")


class Wires:
    def __init__(self, ndp, nmp):
        self.sizes = {"z": ndp // 2, "x": 2, "y": nmp // 2, "c": 2}
        dp = lax.axis_index("dp")
        mp = lax.axis_index("mp")
        self.at = {"z": dp // 2, "x": dp % 2, "y": mp // 2, "c": mp % 2}

    def peer(self, axis, k):
        at = dict(self.at)
        at[axis] = lax.rem(at[axis] + k, self.sizes[axis])
        return (at["z"] * 2 + at["x"], at["y"] * 2 + at["c"])

    def owner_mp(self, ky, kc):
        ny = self.sizes["y"]
        return lax.rem(self.at["y"] + ny - ky, ny) * 2 + lax.rem(self.at["c"] + 2 - kc, 2)

    def near(self, k):
        nmp = self.sizes["y"] * self.sizes["c"]
        return (lax.axis_index("dp"), lax.rem(lax.axis_index("mp") + k, nmp))

    def far(self, k):
        ndp = self.sizes["z"] * self.sizes["x"]
        return (lax.rem(lax.axis_index("dp") + k, ndp), lax.axis_index("mp"))

    def align(self, again):
        fars = [self.far(k) for k in range(1, self.sizes["z"] * self.sizes["x"])]
        self.greet([self.near(k) for k in range(1, self.sizes["y"] * self.sizes["c"])] + fars)
        for p in fars:
            pl.semaphore_signal(again, inc=1, device_id=p, device_id_type=MESH)
        pl.semaphore_wait(again, len(fars))

    def greet(self, peers):
        barrier = pltpu.get_barrier_semaphore()
        for p in peers:
            pl.semaphore_signal(barrier, inc=1, device_id=p, device_id_type=MESH)
        pl.semaphore_wait(barrier, len(peers))


def slot_number(sizes, k):
    return ((k["z"] * sizes["x"] + k["x"]) * sizes["y"] + k["y"]) * sizes["c"] + k["c"]


def spread(sizes, order):
    slots = [(dict.fromkeys(AXES, 0), -1)]
    for stage, axis in enumerate(order):
        slots += [
            ({**k, axis: n}, stage) for n in range(1, sizes[axis]) for k, _ in list(slots)
        ]
    return slots


class Gather:
    def __init__(self, wires, order, own, slot, send, recv):
        self.wires, self.order, self.own, self.slot = wires, order, own, slot
        self.send, self.recv = send, recv
        self.slots = spread(wires.sizes, order)
        self.by_number = {slot_number(wires.sizes, k): i for i, (k, _) in enumerate(self.slots)}
        self.started = []

    def forward(self, source, k, stage):
        for later in range(stage + 1, len(self.order)):
            axis = self.order[later]
            for n in range(1, self.wires.sizes[axis]):
                there = {**k, axis: n}
                number = slot_number(self.wires.sizes, there)
                copy = pltpu.make_async_remote_copy(
                    source, self.slot(there, k), self.send.at[number], self.recv.at[number],
                    device_id=self.wires.peer(axis, n), device_id_type=MESH,
                )
                copy.start()
                self.started.append((copy, number))

    def begin(self):
        k, stage = self.slots[0]
        self.forward(self.own, k, stage)

    def arrive(self, number):
        k, stage = self.slots[self.by_number[number]]
        here = self.slot(k, k)
        pltpu.make_async_remote_copy(
            here, here, self.send.at[number], self.recv.at[number],
            device_id=self.wires.peer("c", 1), device_id_type=MESH,
        ).wait_recv()
        self.forward(here, k, stage)

    def finish(self):
        for copy, _ in self.started:
            copy.wait_send()


FIRST = ("z", "x", "y", "c")
OTHER = ("z", "y", "x", "c")


def total(ref):
    rows = 8

    def body(i, part):
        x = ref[pl.ds(i * rows, rows)]
        return part + x * x

    part = lax.fori_loop(0, ref.shape[0] // rows, body, jnp.zeros((rows, ref.shape[1]), f32))
    return jnp.sum(part)


BLOCK = 256
TILE = 64
FAR = 1e12


def distances(dist, base, other_base, size):
    rows = dist.shape[1]

    def body(i, _):
        here = pl.ds(pl.multiple_of(i * TILE, TILE), TILE)
        down = lax.broadcasted_iota(jnp.int32, (TILE, rows), 0) + i * TILE
        key = jnp.where(down < rows, base + down, other_base + down - rows)
        query = base + lax.broadcasted_iota(jnp.int32, (TILE, rows), 1)
        dist[here] = jnp.where(key < size, jnp.abs(key - query).astype(f32), FAR)
        return 0

    lax.fori_loop(0, dist.shape[0] // TILE, body, 0)


def key_blocks(packed, other, m, col):
    rows = packed.shape[1]
    twin = m + 1 - 2 * (m % 2)
    for part, (ref, index) in enumerate(((packed, m), (other, twin))):
        for start in range(0, rows, BLOCK):
            k = ref[index, start : start + BLOCK, col + HEAD_DIM : col + 2 * HEAD_DIM]
            v = ref[index, start : start + BLOCK, col + 2 * HEAD_DIM : col + 3 * HEAD_DIM]
            yield part, start, part * rows + start, k, v


def attend(packed, other, dist, slopes, mixed, mixed_t, lse, score, m):
    heads = packed.shape[2] // (3 * HEAD_DIM)
    for j in range(heads):
        col = j * 3 * HEAD_DIM
        q = packed[m, :, col : col + HEAD_DIM] * bf(SCALE)
        slope = slopes[m * heads + j]
        top = None
        for _, _, at, k, _ in key_blocks(packed, other, m, col):
            s = rdot(k, q) - slope * dist[at : at + BLOCK]
            score[at : at + BLOCK] = s
            peak = jnp.max(s, axis=0, keepdims=True)
            top = peak if top is None else jnp.maximum(top, peak)
        total_e = jnp.zeros_like(top)
        acc = None
        for _, _, at, _, v in key_blocks(packed, other, m, col):
            e = jnp.exp(score[at : at + BLOCK] - top)
            total_e = total_e + jnp.sum(e, axis=0, keepdims=True)
            part = tdot(v, e.astype(bf))
            acc = part if acc is None else acc + part
        out = acc / total_e
        row = (m * heads + j) * HEAD_DIM
        mixed_t[pl.ds(pl.multiple_of(row, HEAD_DIM), HEAD_DIM)] = out
        mixed[m, :, j * HEAD_DIM : (j + 1) * HEAD_DIM] = out.T.astype(bf)
        lse[m * heads + j] = top + jnp.log(total_e)
        yield


def attend_back(packed, other, dist, slopes, mixed_t, lse, dmixed, down, dother, m):
    heads = packed.shape[2] // (3 * HEAD_DIM)
    for j in range(heads):
        col = j * 3 * HEAD_DIM
        q = packed[m, :, col : col + HEAD_DIM] * bf(SCALE)
        slope = slopes[m * heads + j]
        row = (m * heads + j) * HEAD_DIM
        mt = mixed_t[pl.ds(pl.multiple_of(row, HEAD_DIM), HEAD_DIM)]
        dm = dmixed[m, :, j * HEAD_DIM : (j + 1) * HEAD_DIM]
        delta = jnp.sum(dm.astype(f32).T * mt, axis=0, keepdims=True)
        level = lse[m * heads + j]
        dq = None
        for part, start, at, k, v in key_blocks(packed, other, m, col):
            p = jnp.exp(rdot(k, q) - slope * dist[at : at + BLOCK] - level)
            dv = dot(p.astype(bf), dm)
            t = (p * (rdot(v, dm) - delta)).astype(bf)
            dk = dot(t, q)
            more = tdot(k, t)
            dq = more if dq is None else dq + more
            here = slice(start, start + BLOCK)
            ref = dother if part else down.at[m]
            ref[here, col + HEAD_DIM : col + 2 * HEAD_DIM] = dk.astype(ref.dtype)
            ref[here, col + 2 * HEAD_DIM : col + 3 * HEAD_DIM] = dv.astype(ref.dtype)
        down[m, :, col : col + HEAD_DIM] = (dq * SCALE).T.astype(down.dtype)
        yield


def windows(x, count):
    for j in range(8):
        moved = x if j == 0 else pltpu.roll(x, x.shape[0] - j, 0)
        for far in range(0, count + 1, 8):
            if 1 <= far + j <= count:
                yield far + j, moved[far : far + TILE]


def convolve(hm, chan, conv, column):
    lanes = slice(column, column + 128)

    def body(r, _):
        start = pl.multiple_of(r * TILE, TILE)
        x = hm[pl.ds(start, TILE + 2 * PAD), lanes]
        acc = jnp.broadcast_to(chan[KERNEL + 7, lanes][None], (TILE, 128))
        for offset, moved in windows(x, KERNEL):
            acc = acc + chan[offset - 1, lanes][None] * moved
        conv[pl.ds(start, TILE), lanes] = acc
        return 0

    lax.fori_loop(0, conv.shape[0] // TILE, body, 0)


def convolve_back(dconv, hm, chan, back, gtaps, column):
    lanes = slice(column, column + 128)

    def body(r, _):
        start = pl.multiple_of(r * TILE, TILE)
        x = dconv[pl.ds(start, TILE + 2 * PAD), lanes]
        acc = jnp.zeros((TILE, 128), f32)
        for offset, moved in windows(x, KERNEL):
            acc = acc + chan[KERNEL - offset, lanes][None] * moved
        back[pl.ds(start, TILE), lanes] = acc
        here = x[PAD : PAD + TILE]
        y = hm[pl.ds(start, TILE + 2 * PAD), lanes]
        for offset, moved in windows(y, KERNEL):
            part = here * moved
            part = sum(part[i : i + 8] for i in range(8, TILE, 8)) + part[:8]
            rows_at = slice((offset - 1) * 8, offset * 8)
            gtaps[rows_at, lanes] = gtaps[rows_at, lanes] + part
        return 0

    lax.fori_loop(0, back.shape[0] // TILE, body, 0)


VMEM = pl.BlockSpec(memory_space=pltpu.VMEM)
SMEM = pl.BlockSpec(memory_space=pltpu.SMEM)


class Reduce:
    def __init__(self, wires, order, source, landing, out, send, recv):
        self.wires, self.order, self.source, self.landing = wires, order, source, landing
        self.out, self.send, self.recv = out, send, recv
        self.where = {}
        self.started = []
        sizes = {a: wires.sizes[a] if a in order else 1 for a in AXES}
        slots = [k for k, _ in spread(sizes, order[::-1])]
        self.stages = []
        for axis in order:
            self.stages.append([k for k in slots if k[axis]])
            slots = [k for k in slots if not k[axis]]
        self.by_number = {
            self.number(k): (stage, k) for stage, ks in enumerate(self.stages) for k in ks
        }
        self.summed = set()

    def number(self, k):
        return slot_number(self.wires.sizes, k)

    def now(self, k):
        n = self.number(k)
        return self.landing(self.where[n]) if n in self.where else self.source(k)

    def leave(self, stage, k):
        axis = self.order[stage]
        n = self.wires.sizes[axis]
        number = self.number(k)
        source = self.now(k)
        pltpu.make_async_remote_copy(
            source, self.landing(k), self.send.at[number], self.recv.at[number],
            device_id=self.wires.peer(axis, (n - k[axis]) % n), device_id_type=MESH,
        ).start()
        self.started.append((k, number))

    def keep(self):
        add_rows(self.out, self.source(dict.fromkeys(AXES, 0)), None)

    def depart(self, number):
        self.leave(0, self.by_number[number][1])

    def terms(self, stage, kept):
        return {
            self.number({**kept, axis: n})
            for axis in self.order[: stage + 1]
            for n in range(1, self.wires.sizes[axis])
        }

    def arrive(self, number):
        stage, k = self.by_number[number]
        self.summed.add(number)
        here = self.landing(k)
        axis = self.order[stage]
        pltpu.make_async_remote_copy(
            here, here, self.send.at[number], self.recv.at[number],
            device_id=self.wires.peer(axis, 1), device_id_type=MESH,
        ).wait_recv()
        kept = {**k, axis: 0}
        if not any(kept.values()):
            add_rows(self.out, self.out, here)
            return
        add_rows(here, self.now(kept), here)
        self.where[self.number(kept)] = k
        last = k[axis] == self.wires.sizes[axis] - 1
        if last and stage + 1 < len(self.order) and kept[self.order[stage + 1]]:
            assert self.terms(stage, kept) <= self.summed
            self.leave(stage + 1, kept)

    def finish(self):
        for k, number in self.started:
            here = self.landing(k)
            pltpu.make_async_remote_copy(
                here, here, self.send.at[number], self.recv.at[number],
                device_id=self.wires.peer("c", 1), device_id_type=MESH,
            ).wait_send()


class Crossing:
    def __init__(self, *parts):
        self.parts = parts

    def make(self):
        (src, *s), (dst, *d), send, recv, i, wires = self.parts
        return pltpu.make_async_remote_copy(
            src.at[s[0]] if s else src, dst.at[d[0]] if d else dst, send.at[i], recv.at[i],
            device_id=wires.peer("c", 1), device_id_type=MESH,
        )

    def wait_send(self):
        self.make().wait_send()

    def wait_recv(self):
        self.make().wait_recv()


def add_rows(out, left, right):
    step = 16

    def body(i, _):
        here = pl.ds(pl.multiple_of(i * step, step), step)
        value = left[here].astype(f32)
        if right is not None:
            value = value + right[here].astype(f32)
        out[here] = value.astype(out.dtype)
        return 0

    lax.fori_loop(0, out.shape[0] // step, body, 0)


def gelu_slope(v):
    cube = 0.044715 * v * v * v
    t = jnp.tanh(0.7978845608028654 * (v + cube))
    inner = 0.7978845608028654 * (1.0 + 3.0 * 0.044715 * v * v)
    return 0.5 * (1.0 + t) + 0.5 * v * (1.0 - t * t) * inner


THIN_CHAN = 384
THIN_HEAD = 512
THIN = 640


class BackIn(NamedTuple):
    places: Any
    slopes: Any
    loss: Any
    g_up: Any
    g_down: Any
    dattn: Any
    mixed: Any
    extra: Any
    g_head: Any
    chan: Any
    packed: Any
    other: Any
    mixed_t: Any
    lse: Any
    dmixed: Any
    w_qkv: Any
    first: Any
    conv: Any
    dsecond: Any
    hm: Any
    features: Any


class BackRefs(NamedTuple):
    places: Any
    slopes: Any
    loss: Any
    g_up: Any
    g_down: Any
    dattn: Any
    mixed: Any
    extra: Any
    g_head: Any
    chan: Any
    packed: Any
    other: Any
    mixed_t: Any
    lse: Any
    dmixed: Any
    w_qkv: Any
    first: Any
    conv: Any
    dsecond: Any
    hm: Any
    features: Any
    o_thin: Any
    o_up: Any
    o_down: Any
    o_qkv: Any
    o_out: Any
    sums: Any
    g_qkv: Any
    g_out: Any
    thin: Any
    l_up0: Any
    l_up1: Any
    l_down0: Any
    l_down1: Any
    l_qkv0: Any
    l_qkv1: Any
    l_out0: Any
    l_out1: Any
    l_thin: Any
    down: Any
    dother: Any
    l_other: Any
    a1: Any
    l_a1: Any
    l_dattn: Any
    l_mixed: Any
    l_dpack: Any
    halo: Any
    edge: Any
    parts: Any
    w_buf: Any
    rows_buf: Any
    send: Any
    recv: Any
    c_send: Any
    c_recv: Any
    local: Any
    near_send: Any
    near_recv: Any
    far_send: Any
    far_recv: Any
    again: Any


COLS = 256


def by_tiles(count, size, body):
    def step(i, _):
        body(pl.ds(pl.multiple_of(i * size, size), size))
        return 0

    lax.fori_loop(0, count // size, step, 0)


def fold(x):
    return jnp.sum(x, axis=0, keepdims=True)


def norm_turn(da, xhat, scale, gain):
    dx = da * gain
    return scale * (
        dx
        - jnp.mean(dx, axis=-1, keepdims=True)
        - xhat * jnp.mean(dx * xhat, axis=-1, keepdims=True)
    )


FORE_TURNS = (
    (
        1, 8, 4, 2, 9, 16, 5, 3, 24, 17, 25, 12, 10, 6, 20, 13, 11, 28, 18, 7, 21, 26, 29, 19, 14, 27, 22,
        15, 30, 23, 31, 33, 65, 36, 34, 68, 66, 40, 48,
    ),
    (56,),
    (),
    (72,),
    (37, 35),
    (69, 67),
    (41,),
    (49,),
    (38,),
    (97, 70),
    (129,),
    (80, 42, 44, 57),
    (73, 88, 50, 52),
    (),
    (39, 71),
    (98,),
    (100, 81, 43, 45),
    (),
    (89, 51, 53),
    (130,),
    (132,),
    (104, 58),
    (
        60, 74, 76, 82, 84, 59, 61, 75, 77, 83, 46, 85, 92, 90, 47, 93, 91, 54, 55, 78, 86, 79, 87, 62, 94,
        63, 95, 99, 101, 112, 131, 120, 133, 105, 134, 108, 136, 102, 144, 106, 152,
    ),
    (),
    (),
    (),
    (113,),
    (121, 135, 109, 137, 103, 145, 107, 116, 153, 114),
    (),
    (124,),
    (122, 161, 193),
    (140,),
    (117, 115, 110),
    (),
    (148, 125, 138, 168, 123),
    (141,),
    (156, 176, 146, 111),
    (184, 164),
    (149, 154, 139, 169),
    (196,),
    (162, 157, 177, 147),
    (142, 200, 185, 194, 165),
    (155, 172, 208),
    (118, 143, 126, 150, 119, 127, 151, 158, 159, 197, 163, 180, 216, 201, 195, 173, 209, 170, 188),
    (178,),
    (186,),
    (204, 181, 166, 217, 171, 189),
    (198, 202, 179),
    (212, 174, 187),
    (
        220, 205, 210, 167, 199, 182, 203, 206, 213, 218, 175, 221, 211, 183, 207, 219, 214, 190, 215, 222,
        191, 223,
    ),
)
BACK_TURNS = (
    (34, 100, 42, 108, 50, 116, 58, 124, 38, 102, 46, 110),
    (54, 118),
    (62, 126, 162, 228, 2, 68),
    (170, 236, 10, 76),
    (178, 244, 18, 84),
    (186, 252, 26, 92, 166, 230, 6, 70),
    (14, 78),
    (22, 86),
    (30, 94),
    (130, 196),
    (174, 238, 138, 204, 182, 246, 146, 212),
    (190, 254, 154, 220),
    (290, 356, 298, 364, 306, 372, 134, 198),
    (314, 380, 66, 4, 294, 358, 74, 12, 302, 366),
    (310, 374, 318, 382, 82, 20),
    (90, 28),
    (72, 142, 206, 8, 150, 214),
    (158, 222, 258, 324, 266, 332),
    (274, 340, 80),
    (194, 132, 282, 348),
    (262, 326, 270, 334, 278, 342, 16, 286, 350),
    (88, 202, 140),
    (418, 484, 426, 492, 434, 500, 442, 508, 422, 486, 430, 494, 438, 502, 446, 510, 24, 210, 148),
    (218, 156, 322, 260),
    (330, 268, 338, 276, 346, 284, 200),
    (),
    (386, 452, 136, 394, 460),
    (402, 468),
    (410, 476, 208),
    (390, 454),
    (398, 462, 144, 406, 470),
    (414, 478, 216),
    (388, 450, 152),
    (328, 264, 396, 458),
    (336, 404, 466, 272, 344),
    (
        545, 553, 561, 569, 549, 557, 565, 573, 547, 555, 563, 571, 551, 559, 567, 575, 280, 412, 474, 392,
        456, 513, 521, 529, 537, 517, 525, 533, 541, 515, 523, 531, 539, 519, 527, 535, 543, 400, 514, 522,
        530, 464, 538, 518, 408, 526, 534, 516, 542, 472, 524, 532, 540, 520, 528, 536,
    ),
)


class ForeIn(NamedTuple):
    places: Any
    slopes: Any
    thin_own: Any
    near_own: Any
    mid_own: Any
    down_own: Any
    features: Any


class ForeOut(NamedTuple):
    thin: Any
    near: Any
    mid: Any
    down: Any
    hm: Any
    conv: Any
    first: Any
    packed: Any
    other: Any
    mixed: Any
    mixed_t: Any
    lse: Any
    chan: Any
    second: Any
    a2: Any
    active: Any
    slope: Any


class ForeRefs(NamedTuple):
    places: Any
    slopes: Any
    thin_own: Any
    near_own: Any
    mid_own: Any
    down_own: Any
    features: Any
    o_thin: Any
    o_near: Any
    mid: Any
    down: Any
    o_hm: Any
    o_conv: Any
    o_first: Any
    o_packed: Any
    o_other: Any
    o_mixed: Any
    o_mixed_t: Any
    o_lse: Any
    o_chan: Any
    o_second: Any
    o_a2: Any
    o_active: Any
    o_slope: Any
    thin: Any
    near: Any
    hm: Any
    conv: Any
    first: Any
    packed: Any
    other: Any
    mixed: Any
    mixed_t: Any
    lse: Any
    chan: Any
    second: Any
    a2: Any
    active: Any
    slope: Any
    a1: Any
    dist: Any
    score: Any
    w: Any
    send: Any
    recv: Any
    local: Any
    c_send: Any
    c_recv: Any
    again: Any


def fore_kernel(ndp, nmp, *refs):
    r = ForeRefs(*refs)
    wires = Wires(ndp, nmp)
    wires.align(r.again)
    sizes = wires.sizes
    thin_rows = r.thin_own.shape[0]
    rows, model = r.first.shape
    size = r.places[2]

    def thin_slot(k, sent):
        block = (k["z"] * sizes["x"] + k["x"]) * nmp + wires.owner_mp(sent["y"], sent["c"])
        return r.thin.at[pl.ds(pl.multiple_of(block * thin_rows, thin_rows), thin_rows)]

    flows = [Gather(wires, FIRST, r.thin_own, thin_slot, r.send.at[0], r.recv.at[0])]

    def wide_flow(own, out, half, order):
        height = own.shape[0] // 2

        def slot(k, sent):
            start = (k["z"] * sizes["x"] + k["x"]) * 2 * height + half * height
            return out.at[k["y"] * sizes["c"] + k["c"], pl.ds(start, height)]

        n = len(flows)
        part = own.at[pl.ds(half * height, height)]
        flows.append(Gather(wires, order, part, slot, r.send.at[n], r.recv.at[n]))
        return flows[-1]

    near = [wide_flow(r.near_own, r.near, h, o) for h, o in enumerate((FIRST, OTHER))]
    mid = [wide_flow(r.mid_own, r.mid, h, o) for h, o in enumerate((FIRST, OTHER))]
    down = [wide_flow(r.down_own, r.down, h, o) for h, o in enumerate((FIRST, OTHER))]
    zero = dict.fromkeys(AXES, 0)
    kept = [
        pltpu.make_async_copy(f.own, f.slot(zero, zero), r.local.at[i])
        for i, f in enumerate(flows)
    ]
    for copy in kept:
        copy.start()
    for f in flows[:1] + near:
        f.begin()
    turns = iter(FORE_TURNS)
    slots = ndp * nmp
    saves = []

    def save(src, dst):
        copy = pltpu.make_async_copy(src, dst, r.local.at[len(flows) + nmp + len(saves)])
        copy.start()
        saves.append(copy)

    def turn():
        for code in next(turns):
            flows[code // slots].arrive(code % slots)

    turn()
    for f in mid:
        f.begin()
    for copy in kept:
        copy.wait()

    for i in range(0, model, 128):
        cols = r.thin[i : i + 128, THIN_CHAN:THIN_HEAD].astype(f32)
        r.chan[:, i : i + 128] = cols.T
    save(r.chan, r.o_chan)
    save(r.thin, r.o_thin)
    distances(r.dist, r.places[0], r.places[1], size)
    turn()

    for column in range(0, model, 128):
        cols = slice(column, column + 128)
        h = rdot(r.features[...], r.thin[cols, :THIN_CHAN])
        h = h + r.chan[KERNEL + 6, cols][None]
        place = r.places[0] - PAD + lax.broadcasted_iota(jnp.int32, (h.shape[0], 1), 0)
        r.first[:, cols] = h[PAD : PAD + rows]
        r.hm[:, cols] = jnp.where((place >= 0) & (place < size), h, 0.0)
        turn()
    for c in range(0, model, 128):
        convolve(r.hm, r.chan, r.conv, c)
        turn()

    def norm(i, _):
        here = pl.ds(pl.multiple_of(i * TILE, TILE), TILE)
        v = r.conv[here]
        inner = 0.7978845608028654 * v * (1.0 + 0.044715 * v * v)
        first = r.first[here] + v * (0.5 + 0.5 * jnp.tanh(inner))
        r.first[here] = first
        xhat, _ = norm_parts(first)
        r.a1[here] = (xhat * r.chan[KERNEL][None] + r.chan[KERNEL + 1][None]).astype(bf)

        return 0

    save(r.hm, r.o_hm)
    save(r.conv, r.o_conv)
    for i in range(0, rows // TILE, 2):
        lax.fori_loop(i, i + 2, norm, 0)
        turn()
    save(r.first, r.o_first)
    turn()
    crossings = []
    width = r.packed.shape[2]
    for m in range(nmp):
        def expand(cols):
            r.packed[m, :, cols] = dot(r.a1[...], r.near[m, :, cols]).astype(bf)

        by_tiles(width, COLS, expand)
        copy = pltpu.make_async_remote_copy(
            r.packed.at[m], r.other.at[m], r.c_send.at[m], r.c_recv.at[m],
            device_id=wires.peer("c", 1), device_id_type=MESH,
        )
        copy.start()
        crossings.append(copy)
        turn()
    for f in down:
        f.begin()
    save(r.near, r.o_near)
    save(r.packed, r.o_packed)
    for m in range(nmp):
        crossings[m + 1 - 2 * (m % 2)].wait_recv()
        for _ in attend(
            r.packed, r.other, r.dist, r.slopes, r.mixed, r.mixed_t, r.lse,
            r.score, m,
        ):
            turn()
    turn()
    for src, dst in (
        (r.other, r.o_other), (r.mixed, r.o_mixed), (r.mixed_t, r.o_mixed_t), (r.lse, r.o_lse)
    ):
        save(src, dst)
    loads = [
        pltpu.make_async_copy(r.mid.at[m], r.w.at[m], r.local.at[len(flows) + m])
        for m in range(nmp)
    ]
    for copy in loads:
        copy.start()
    c_out = r.mixed.shape[2]
    hid = r.active.shape[2]
    w_out = [r.w.at[m, :, pl.ds(0, c_out)] for m in range(nmp)]
    w_up = [r.w.at[m, :, pl.ds(c_out, hid)] for m in range(nmp)]
    for copy in loads:
        copy.wait()

    def project(cols):
        acc = r.first[:, cols]
        for m in range(nmp):
            acc = acc + rdot(r.mixed[m], w_out[m][cols, :])
        r.second[:, cols] = acc

    by_tiles(model, COLS, project)

    def second_norm(here):
        xhat, _ = norm_parts(r.second[here])
        gain, bias = r.chan[KERNEL + 2][None], r.chan[KERNEL + 3][None]
        r.a2[here] = (xhat * gain + bias).astype(bf)

    by_tiles(rows, TILE, second_norm)
    save(r.second, r.o_second)
    save(r.a2, r.o_a2)
    turn()
    for m in range(nmp):

        def gelu_pair(v, cols):
            square = v * v
            t = jnp.tanh(0.7978845608028654 * v * (1.0 + 0.044715 * square))
            half = 0.5 + 0.5 * t
            r.active[m, :, cols] = (v * half).astype(bf)
            inner = 0.3989422804014327 * (1.0 + 0.134145 * square)
            r.slope[m, :, cols] = (half + v * (1.0 - t * t) * inner).astype(bf)

        def expand(i, _):
            cols = [pl.ds(pl.multiple_of((2 * i + n) * COLS, COLS), COLS) for n in range(2)]
            values = [dot(r.a2[...], w_up[m][:, c]) for c in cols]
            for v, c in zip(values, cols):
                gelu_pair(v, c)
            return 0

        lax.fori_loop(0, hid // COLS // 2, expand, 0)
        save(r.active.at[m], r.o_active.at[m])
        save(r.slope.at[m], r.o_slope.at[m])
        turn()
    turn()
    assert next(turns, None) is None
    for copy in saves:
        copy.wait()
    for f in flows:
        f.finish()
    for copy in crossings:
        copy.wait_send()


def fore_all(ndp, nmp, given):
    model = given.near_own.shape[0] * ndp
    width = given.near_own.shape[1]
    hid = given.down_own.shape[1]
    wide = HEADS * HEAD_DIM
    rows = given.features.shape[0] - 2 * PAD
    struct = jax.ShapeDtypeStruct
    dma = pltpu.SemaphoreType.DMA
    anywhere = pl.BlockSpec(memory_space=pl.ANY)
    outs = [
        struct((model, THIN), bf),
        struct((nmp, model, width), bf),
        struct((nmp, model, given.mid_own.shape[1]), bf),
        struct((nmp, model, hid), bf),
        struct((rows + 2 * PAD, model), f32),
        struct((rows, model), f32),
        struct((rows, model), f32),
        struct((nmp, rows, width), bf),
        struct((nmp, rows, width), bf),
        struct((nmp, rows, wide // nmp), bf),
        struct((wide, rows), f32),
        struct((HEADS, 1, rows), f32),
        struct((128, model), f32),
        struct((rows, model), f32),
        struct((rows, model), bf),
        struct((nmp, rows, hid), bf),
        struct((nmp, rows, hid), bf),
    ]
    outs = pl.pallas_call(
        functools.partial(fore_kernel, ndp, nmp),
        name="fore",
        out_shape=outs,
        in_specs=[SMEM] * 2 + [anywhere] * 4 + [VMEM],
        out_specs=[anywhere] * len(outs),
        scratch_shapes=[pltpu.VMEM(o.shape, o.dtype) for o in outs[:2] + outs[4:]]
        + [
            pltpu.VMEM((rows, model), bf),
            pltpu.VMEM((2 * rows, rows), f32),
            pltpu.VMEM((2 * rows, rows), f32),
            pltpu.VMEM((nmp, model, given.mid_own.shape[1]), bf),
            dma((7, ndp * nmp)),
            dma((7, ndp * nmp)),
            dma((7 + nmp + 13 + 2 * nmp,)),
            dma((nmp,)),
            dma((nmp,)),
            pltpu.SemaphoreType.REGULAR,
        ],
        compiler_params=pltpu.CompilerParams(
            collective_id=0, has_side_effects=True, vmem_limit_bytes=62 << 20
        ),
    )(*given)
    return ForeOut(*outs)


class MiddleIn(NamedTuple):
    second: Any
    a2: Any
    active: Any
    slope: Any
    chan: Any
    w_head: Any
    target: Any
    weights: Any
    mid: Any
    down: Any


class MiddleOut(NamedTuple):
    g_up: Any
    g_down: Any
    dsecond: Any
    dattn: Any
    dmixed: Any
    extra: Any
    g_head: Any
    loss: Any


class MiddleRefs(NamedTuple):
    second: Any
    a2: Any
    active: Any
    slope: Any
    chan: Any
    w_head: Any
    target: Any
    weights: Any
    mid: Any
    down: Any
    g_up: Any
    g_down: Any
    dsecond: Any
    dattn: Any
    dmixed: Any
    extra: Any
    g_head: Any
    loss: Any
    ffn: Any
    l_a2: Any
    dffn: Any
    l_dffn: Any
    l_active: Any
    l_dhid: Any
    dhid: Any
    a3: Any
    stage: Any
    w: Any
    w_down: Any
    c_send: Any
    c_recv: Any
    local: Any


def middle_kernel(ndp, nmp, *refs):
    r = MiddleRefs(*refs)
    wires = Wires(ndp, nmp)
    partner = wires.peer("c", 1)
    wires.greet([partner])
    rows, model = r.second.shape
    ny = nmp // 2
    theirs = list(range(1, nmp, 2))
    mine = list(range(0, nmp, 2))
    hid = r.active.shape[2]
    c_out = r.mid.shape[2] - hid
    w_out = [r.w.at[m, :, pl.ds(0, c_out)] for m in range(nmp)]
    w_up = [r.w.at[m, :, pl.ds(c_out, hid)] for m in range(nmp)]
    loads = [
        [
            pltpu.make_async_copy(src.at[m], dst.at[m], r.local.at[i * nmp + m])
            for m in range(nmp)
        ]
        for i, (src, dst) in enumerate(((r.down, r.w_down), (r.mid, r.w)))
    ]
    for group in loads:
        for m in theirs + mine:
            group[m].start()
    w_down = [r.w_down.at[m] for m in range(nmp)]
    crossings = []

    def cross(src, dst):
        i = len(crossings)
        copy = pltpu.make_async_remote_copy(
            src, dst, r.c_send.at[i], r.c_recv.at[i],
            device_id=partner, device_id_type=MESH,
        )
        copy.start()
        crossings.append(copy)
        return copy

    def row(i):
        return r.chan[KERNEL + i][None]

    got_a2 = cross(r.a2, r.l_a2)
    got_active = [cross(r.active.at[m], r.l_active.at[m // 2]) for m in theirs]
    for m in theirs + mine:
        loads[0][m].wait()

        def shrink(cols):
            part = rdot(r.active[m], w_down[m][cols, :])
            r.ffn[:, cols] = part if m == theirs[0] else r.ffn[:, cols] + part

        by_tiles(model, COLS, shrink)

    def third_norm(here):
        xhat, _ = norm_parts(r.second[here] + r.ffn[here])
        r.a3[here] = (xhat * row(4) + row(5)).astype(bf)

    by_tiles(rows, TILE, third_norm)
    error = dot(r.a3[...], r.w_head[...]) - r.target[...]
    weighted = r.weights[...] * error
    lanes = lax.broadcasted_iota(jnp.int32, (8, 128), 1)
    r.loss[...] = jnp.where(lanes == 0, jnp.sum(weighted * error), 0.0)
    dpred = (2.0 * weighted).astype(bf)
    r.g_head[...] = tdot(r.a3[...], dpred).astype(bf)
    r.dsecond[...] = rdot(dpred, r.w_head[...])

    zero = jnp.zeros((1, model), f32)

    def third_back(i, acc):
        here = pl.ds(pl.multiple_of(i * TILE, TILE), TILE)
        xhat, scale = norm_parts(r.second[here] + r.ffn[here])
        da = r.dsecond[here]
        dv = norm_turn(da, xhat, scale, row(4))
        r.ffn[here] = dv
        r.dffn[here] = dv.astype(bf)
        return acc[0] + fold(da * xhat), acc[1] + fold(da)

    dgain, dbias = lax.fori_loop(0, rows // TILE, third_back, (zero, zero))
    r.extra[...] = jnp.zeros_like(r.extra)
    r.extra[2:3] = dgain
    r.extra[3:4] = dbias
    got_dffn = cross(r.dffn, r.l_dffn)
    got_dhid = []
    stored = []

    def store(out, y, left, right, left_other, right_other):
        slot = len(stored) % 2
        if len(stored) >= 2:
            stored[-2].wait()

        def body(cols):
            part = tdot(left[:, cols], right[...]) + tdot(left_other[:, cols], right_other[...])
            r.stage[slot, cols] = part.astype(bf)

        by_tiles(model, COLS, body)
        copy = pltpu.make_async_copy(r.stage.at[slot], out.at[y], r.local.at[2 * nmp + len(stored)])
        copy.start()
        stored.append(copy)

    got_a2.wait_recv()
    for m in theirs + mine:
        loads[1][m].wait()

        def contract(cols):
            dact = dot(r.dffn[...], w_down[m][:, cols])
            r.dhid[m, :, cols] = (dact * r.slope[m, :, cols].astype(f32)).astype(bf)

        by_tiles(hid, COLS, contract)
        if m in theirs:
            got_dhid.append(cross(r.dhid.at[m], r.l_dhid.at[m // 2]))

        def gather_da2(cols):
            part = rdot(r.dhid[m], w_up[m][cols, :])
            r.dsecond[:, cols] = part if m == theirs[0] else r.dsecond[:, cols] + part

        by_tiles(model, COLS, gather_da2)
    got_dffn.wait_recv()
    for y in range(ny):
        got_active[y].wait_recv()
        store(r.g_down, y, r.dffn, r.active.at[2 * y], r.l_dffn, r.l_active.at[y])
    for y in range(ny):
        got_dhid[y].wait_recv()
        store(r.g_up, y, r.a2, r.dhid.at[2 * y], r.l_a2, r.l_dhid.at[y])

    def second_back(i, acc):
        here = pl.ds(pl.multiple_of(i * TILE, TILE), TILE)
        xhat, scale = norm_parts(r.second[here])
        da = r.dsecond[here]
        dsecond = r.ffn[here] + norm_turn(da, xhat, scale, row(2))
        r.dsecond[here] = dsecond
        r.dattn[here] = dsecond.astype(bf)
        return acc[0] + fold(da * xhat), acc[1] + fold(da)

    dgain, dbias = lax.fori_loop(0, rows // TILE, second_back, (zero, zero))
    r.extra[0:1] = dgain
    r.extra[1:2] = dbias
    for m in range(nmp):
        r.dmixed[m] = dot(r.dattn[...], w_out[m][...]).astype(bf)
    for copy in stored[-2:]:
        copy.wait()
    for copy in crossings:
        copy.wait_send()


def middle_all(ndp, nmp, given):
    rows, model = given.second.shape
    ny = nmp // 2
    hid = given.active.shape[2]
    c_out = given.mid.shape[2] - hid
    dma = pltpu.SemaphoreType.DMA
    anywhere = pl.BlockSpec(memory_space=pl.ANY)
    struct = jax.ShapeDtypeStruct
    outs = [
        struct((ny, model, hid), bf),
        struct((ny, model, hid), bf),
        struct((rows, model), f32),
        struct((rows, model), bf),
        struct((nmp, rows, c_out), bf),
        struct((8, model), f32),
        struct((model, 128), bf),
        struct((8, 128), f32),
    ]
    flat, tall = pltpu.VMEM((rows, model), f32), pltpu.VMEM((rows, model), bf)
    scratch = [
        flat,
        tall,
        tall,
        tall,
        pltpu.VMEM((ny, rows, hid), bf),
        pltpu.VMEM((ny, rows, hid), bf),
        pltpu.VMEM((nmp, rows, hid), bf),
        tall,
        pltpu.VMEM((2, model, hid), bf),
        pltpu.VMEM(given.mid.shape, bf),
        pltpu.VMEM(given.down.shape, bf),
        dma((8,)),
        dma((8,)),
        dma((2 * nmp + 2 * ny,)),
    ]
    outs = pl.pallas_call(
        functools.partial(middle_kernel, ndp, nmp),
        name="middle",
        out_shape=outs,
        in_specs=[VMEM] * 8 + [anywhere] * 2,
        out_specs=[anywhere] * 2 + [VMEM] * 6,
        scratch_shapes=scratch,
        compiler_params=pltpu.CompilerParams(
            collective_id=2, has_side_effects=True, vmem_limit_bytes=62 << 20
        ),
    )(*given)
    return MiddleOut(*outs)


def back_kernel(ndp, nmp, *refs):
    r = BackRefs(*refs)
    wires = Wires(ndp, nmp)
    sizes = wires.sizes
    rows, model = r.dattn.shape
    ny = sizes["y"]
    seq = wires.at["c"]
    nears = [wires.near(k) for k in range(1, nmp)]
    fars = [wires.far(k) for k in range(1, ndp)]
    wires.align(r.again)
    pending = []
    size = r.places[2]

    count = iter(range(16))

    def cross(src, dst):
        i = next(count)
        copy = Crossing(src, dst, r.c_send, r.c_recv, i, wires)
        copy.make().start()
        pending.append(copy)
        return copy

    def sent(copy):
        copy.wait_send()
        pending[:] = [c for c in pending if c is not copy]

    locals_used = []

    def fetch(src, dst):
        copy = pltpu.make_async_copy(src, dst, r.local.at[len(locals_used)])
        copy.start()
        locals_used.append(copy)
        return copy

    flows = []

    def wide_flow(term, out, box, half, order):
        height = term.shape[1] // ndp // 2
        n = len(flows)

        def source(k):
            start = (k["z"] * sizes["x"] + k["x"]) * 2 * height + half * height
            return term.at[k["y"], pl.ds(start, height)]

        def landing(k):
            return box.at[slot_number(sizes, k) // sizes["c"] - 1]

        here = out.at[pl.ds(half * height, height)]
        flows.append(
            Reduce(wires, order, source, landing, here, r.send.at[n], r.recv.at[n])
        )
        return flows[-1]

    def both(term, out, *boxes):
        orders = (("y", "x", "z"), ("x", "y", "z"))
        return [wide_flow(term, out, boxes[h], h, order) for h, order in enumerate(orders)]

    def thin_source(k):
        height = r.o_thin.shape[0]
        block = (k["z"] * sizes["x"] + k["x"]) * nmp + wires.owner_mp(k["y"], k["c"])
        return r.thin.at[pl.ds(pl.multiple_of(block * height, height), height)]

    down_flows = both(r.g_down, r.o_down, r.l_down0, r.l_down1)
    up_flows = both(r.g_up, r.o_up, r.l_up0, r.l_up1)
    out_flows = both(r.g_out, r.o_out, r.l_out0, r.l_out1)
    qkv_flows = both(r.g_qkv, r.o_qkv, r.l_qkv0, r.l_qkv1)
    n = len(flows)
    thin_flow = Reduce(
        wires, ("c", "y", "x", "z"), thin_source,
        lambda k: r.l_thin.at[slot_number(sizes, k) - 1],
        r.o_thin, r.send.at[n], r.recv.at[n],
    )
    flows.append(thin_flow)
    turns = iter(BACK_TURNS)
    slots = ndp * nmp

    def turn():
        for code in next(turns):
            flow = flows[code // (2 * slots)]
            if code // slots % 2:
                flow.depart(code % slots)
            else:
                flow.arrive(code % slots)

    mine = [m for m in range(nmp) if m % 2 == 0]
    theirs = [m for m in range(nmp) if m % 2]
    for f in down_flows + up_flows:
        f.keep()
    turn()
    got_dattn = cross((r.dattn,), (r.l_dattn,))
    got_mixed = [cross((r.mixed, m), (r.l_mixed, m // 2)) for m in theirs]

    got_other = {}
    loads = {m: fetch(r.w_qkv.at[m], r.w_buf.at[m]) for m in range(2)}

    def attention(packed, other, mixed_t, dmixed, dist):
        copies = [
            fetch(src, ref)
            for src, ref in (
                (r.packed, packed), (r.other, other), (r.mixed_t, mixed_t), (r.dmixed, dmixed)
            )
        ]
        distances(dist, r.places[0], r.places[1], size)
        turn()
        got_dattn.wait_recv()
        for copy in got_mixed:
            copy.wait_recv()
        for y in range(ny):
            g = tdot(r.dattn[...], r.mixed[2 * y])
            r.g_out[y] = (g + tdot(r.l_dattn[...], r.l_mixed[y])).astype(bf)
        for f in out_flows:
            f.keep()
        for copy in copies:
            copy.wait()
        leaving = []
        for m in theirs + mine:
            slot = len(leaving) % 2
            if len(leaving) >= 2:
                sent(leaving[-2])
            for _ in attend_back(
                packed, other, dist, r.slopes, mixed_t, r.lse, dmixed,
                r.down, r.dother.at[slot], m,
            ):
                turn()
            twin = m + 1 - 2 * (m % 2)
            leaving.append(cross((r.dother, slot), (r.l_other, twin)))
            got_other[twin] = leaving[-1]

    chunks, _, width = r.packed.shape
    pl.run_scoped(
        attention,
        pltpu.VMEM(r.packed.shape, bf),
        pltpu.VMEM(r.other.shape, bf),
        pltpu.VMEM(r.mixed_t.shape, f32),
        pltpu.VMEM(r.dmixed.shape, bf),
        pltpu.VMEM((2 * rows, rows), f32),
    )

    lane = lax.broadcasted_iota(jnp.int32, (TILE, width), 1)
    is_query = lax.rem(lane, 3 * HEAD_DIM) < HEAD_DIM

    def front(first, conv, back, hm, features, dconv, gtaps):
        copies = [
            fetch(src, ref)
            for src, ref in (
                (r.first, first), (r.conv, conv), (r.dsecond, back), (r.hm, hm), (r.features, features)
            )
        ]
        copies[0].wait()
        gain = r.chan[KERNEL][None]
        bias = r.chan[KERNEL + 1][None]

        def act(i, _):
            here = pl.ds(pl.multiple_of(i * TILE, TILE), TILE)
            xhat, _ = norm_parts(first[here])
            r.a1[here] = (xhat * gain + bias).astype(bf)
            return 0

        lax.fori_loop(0, rows // TILE, act, 0)
        got_a1 = cross((r.a1,), (r.l_a1,))
        turn()

        def combine(m):
            got_other[m].wait_recv()

            def body(i, _):
                here = pl.ds(pl.multiple_of(i * TILE, TILE), TILE)
                own = r.down[m, here].astype(f32)
                more = own + r.l_other[m, here].astype(f32)
                r.down[m, here] = jnp.where(is_query, own, more).astype(bf)
                return 0

            lax.fori_loop(0, rows // TILE, body, 0)

        got_pack = []
        for m in theirs:
            combine(m)
            got_pack.append(cross((r.down, m), (r.l_dpack, m // 2)))
        for m in mine:
            combine(m)
        turn()
        got_a1.wait_recv()
        for y in range(ny):
            got_pack[y].wait_recv()
            g = tdot(r.a1[...], r.down[2 * y])
            r.g_qkv[y] = (g + tdot(r.l_a1[...], r.l_dpack[y])).astype(bf)
            turn()
        for f in qkv_flows:
            f.keep()
        inner = pl.ds(PAD, rows)
        for m in range(chunks):
            loads[m].wait()
            part = rdot(r.down[m], r.w_buf[m % 2])
            dconv[inner] = part if m == 0 else dconv[inner] + part
            if m + 2 < chunks:
                loads[m + 2] = fetch(r.w_qkv.at[m + 2], r.w_buf.at[m % 2])
            turn()
        for copy in copies[1:]:
            copy.wait()
        r.rows_buf[...] = jnp.zeros_like(r.rows_buf)
        r.rows_buf[KERNEL + 2 : KERNEL + 6] = r.extra[0:4]

        def norm(i, sums_in):
            here = pl.ds(pl.multiple_of(i * TILE, TILE), TILE)
            xhat, scale = norm_parts(first[here])
            shifted = pl.ds(pl.multiple_of(i * TILE + PAD, PAD), TILE)
            da = dconv[shifted]
            dx = da * gain
            dv = scale * (
                dx
                - jnp.mean(dx, axis=-1, keepdims=True)
                - xhat * jnp.mean(dx * xhat, axis=-1, keepdims=True)
            )
            dfirst = back[here] + dv
            first[here] = dfirst
            dc = dfirst * gelu_slope(conv[here])
            dconv[shifted] = dc
            return tuple(a + fold(b) for a, b in zip(sums_in, (da * xhat, da, dc)))

        zero = jnp.zeros((1, model), f32)
        dgain, dbias, dcsum = lax.fori_loop(0, rows // TILE, norm, (zero, zero, zero))
        r.rows_buf[KERNEL : KERNEL + 1] = dgain
        r.rows_buf[KERNEL + 1 : KERNEL + 2] = dbias
        r.rows_buf[KERNEL + 7 : KERNEL + 8] = dcsum
        r.edge[0] = dconv[PAD : 2 * PAD]
        r.edge[1] = dconv[rows : rows + PAD]
        got_edge = cross((r.edge,), (r.halo,))
        turn()
        got_edge.wait_recv()
        dconv[0:PAD] = jnp.where(seq == 0, 0.0, r.halo[1])
        dconv[rows + PAD :] = jnp.where(seq == 0, r.halo[0], 0.0)
        gtaps[...] = jnp.zeros_like(gtaps)
        for c in range(0, model, 128):
            convolve_back(dconv, hm, r.chan, back, gtaps, c)
            turn()

        def finish(i, acc):
            here = pl.ds(pl.multiple_of(i * TILE, TILE), TILE)
            place = r.places[0] + i * TILE + lax.broadcasted_iota(jnp.int32, (TILE, 1), 0)
            dstart = first[here] + jnp.where(place < size, back[here], 0.0)
            r.a1[here] = dstart.astype(bf)
            return acc + fold(dstart)

        sent(got_a1)
        r.rows_buf[KERNEL + 6 : KERNEL + 7] = lax.fori_loop(0, rows // TILE, finish, zero)
        for k in range(KERNEL):
            r.rows_buf[k : k + 1] = fold(gtaps[8 * k : 8 * k + 8])
        r.thin[:, :THIN_CHAN] = tdot(r.a1[...], features[...]).astype(bf)
        for i in range(0, model, 128):
            r.thin[i : i + 128, THIN_CHAN:THIN_HEAD] = r.rows_buf[:, i : i + 128].T.astype(bf)
        r.thin[:, THIN_HEAD:] = r.g_head[...]

    pl.run_scoped(
        front,
        pltpu.VMEM((rows, model), f32),
        pltpu.VMEM((rows, model), f32),
        pltpu.VMEM((rows, model), f32),
        pltpu.VMEM((rows + 2 * PAD, model), f32),
        pltpu.VMEM(r.features.shape, bf),
        pltpu.VMEM((rows + 2 * PAD, model), f32),
        pltpu.VMEM((8 * KERNEL, model), f32),
    )
    thin_flow.keep()
    turn()
    assert next(turns, None) is None
    for f in flows:
        f.finish()
    for copy in pending:
        copy.wait_send()

    squares = None
    for out in (r.o_thin, r.o_up, r.o_down, r.o_qkv, r.o_out):
        part = total(out)
        squares = part if squares is None else squares + part
    lanes = lax.broadcasted_iota(jnp.int32, (8, 128), 1)
    block = jnp.where(lanes == 1, squares, r.loss[...])
    parts = r.parts
    for peers, sends, recvs, lower in (
        (nears, r.near_send, r.near_recv, 0),
        (fars, r.far_send, r.far_recv, nmp),
    ):
        parts[lower] = block
        copies = []
        for i, p in enumerate(peers):
            copy = pltpu.make_async_remote_copy(
                parts.at[lower], parts.at[lower + 1 + i], sends.at[i], recvs.at[i],
                device_id=p, device_id_type=MESH,
            )
            copy.start()
            copies.append(copy)
        for copy in copies:
            copy.wait()
        for i in range(len(peers)):
            block = block + parts[lower + 1 + i]
    r.sums[...] = block


def back_all(ndp, nmp, given):
    rows, model = given.dattn.shape
    ny = nmp // 2
    width = given.packed.shape[2]
    c_out = given.mixed.shape[2]
    c_up = given.g_up.shape[2]
    height = model // ndp
    pairs = (ndp * ny - 1, height // 2)
    dma = pltpu.SemaphoreType.DMA
    wide = (c_up, given.g_down.shape[2], width, c_out)
    outs = [jax.ShapeDtypeStruct((height // nmp, THIN), f32)]
    outs += [jax.ShapeDtypeStruct((height, n), f32) for n in wide]
    outs += [jax.ShapeDtypeStruct((8, 128), f32)]
    scratch = [
        pltpu.VMEM((ny, model, width), bf),
        pltpu.VMEM((ny, model, c_out), bf),
        pltpu.VMEM((model, THIN), bf),
    ]
    for n in wide:
        scratch += [pltpu.VMEM((*pairs, n), bf)] * 2
    scratch += [
        pltpu.VMEM((ndp * nmp - 1, height // nmp, THIN), bf),
        pltpu.VMEM((nmp, rows, width), bf),
        pltpu.VMEM((2, rows, width), bf),
        pltpu.VMEM((nmp, rows, width), bf),
        pltpu.VMEM((rows, model), bf),
        pltpu.VMEM((rows, model), bf),
        pltpu.VMEM((rows, model), bf),
        pltpu.VMEM((ny, rows, c_out), bf),
        pltpu.VMEM((ny, rows, width), bf),
        pltpu.VMEM((2, PAD, model), f32),
        pltpu.VMEM((2, PAD, model), f32),
        pltpu.VMEM((nmp + ndp, 8, 128), f32),
        pltpu.VMEM((2, model, width), bf),
        pltpu.VMEM((128, model), f32),
        dma((9, ndp * nmp)),
        dma((9, ndp * nmp)),
        dma((16,)),
        dma((16,)),
        dma((16,)),
        dma((nmp - 1,)),
        dma((nmp - 1,)),
        dma((ndp - 1,)),
        dma((ndp - 1,)),
        pltpu.SemaphoreType.REGULAR,
    ]
    anywhere = pl.BlockSpec(memory_space=pl.ANY)
    specs = [SMEM] * 2 + [VMEM] * 8 + [anywhere] * 3 + [VMEM] * 1 + [anywhere] * 7
    return pl.pallas_call(
        functools.partial(back_kernel, ndp, nmp),
        name="back",
        out_shape=outs,
        in_specs=specs,
        out_specs=[VMEM] * len(outs),
        scratch_shapes=scratch,
        compiler_params=pltpu.CompilerParams(
            collective_id=1, has_side_effects=True, vmem_limit_bytes=62 << 20
        ),
    )(*given)


def shards(
    clean_mel,
    noise_mel,
    lengths,
    span_start,
    span_end,
    phone_ids,
    flow_steps,
    in_table,
    channel_rows,
    attn_qkv,
    attn_out,
    ffn_up,
    ffn_down,
    mel_head,
    table_first,
    channel_first,
    qkv_first,
    merge_first,
    upward_first,
    downward_first,
    head_first,
    table_second,
    channel_second,
    qkv_second,
    merge_second,
    upward_second,
    downward_second,
    head_second,
):
    micro, units, length, mel = clean_mel.shape
    nmp = lax.axis_size("mp")
    seqs = nmp // micro
    rows = length // seqs
    mp = lax.axis_index("mp")
    batch = mp // seqs
    seq = mp % seqs
    base = seq * rows
    width = in_table.shape[0]
    nch = channel_rows.shape[0]

    c_qkv = attn_qkv.shape[1]
    c_out = attn_out.shape[0]
    c_up = ffn_up.shape[1]

    ndp = lax.axis_size("dp")
    spans = jnp.sum(span_end - span_start, axis=1)
    digits = jnp.stack([spans // 32, spans % 32], axis=1).reshape(1, -1)
    digits = jnp.broadcast_to(digits, (mel_head.shape[0], 2 * micro))

    def columns(x, size):
        return jnp.pad(x.astype(bf), ((0, 0), (0, size - x.shape[1])))

    thin = jnp.concatenate(
        [
            columns(in_table.T, THIN_CHAN),
            columns(channel_rows.T, THIN_HEAD - THIN_CHAN),
            columns(jnp.concatenate([mel_head, digits.astype(f32)], axis=1), THIN - THIN_HEAD),
        ],
        axis=1,
    )
    mid = jnp.concatenate([attn_out.T, ffn_up], axis=1).astype(bf)
    own = (ndp, nmp, seqs) == (8, 4, 2)
    def mine(x):
        return lax.dynamic_index_in_dim(x, batch, 0, keepdims=False)[0]

    def widen(x):
        x = jnp.pad(mine(x), [(PAD, PAD)] + [(0, 0)] * (x.ndim - 3))
        return lax.dynamic_slice_in_dim(x, base, rows + 2 * PAD, 0)

    size = mine(lengths)
    first_frame = mine(span_start)
    last_frame = mine(span_end)
    place = base - PAD + jnp.arange(rows + 2 * PAD)
    valid_ext = ((place >= 0) & (place < size)).astype(f32)[:, None]
    masked_ext = ((place >= first_frame) & (place < last_frame)).astype(f32)[:, None]
    inside = slice(PAD, PAD + rows)
    valid = valid_ext[inside]
    masked = masked_ext[inside]
    tau = mine(flow_steps).astype(f32) / TSTEPS
    clean = widen(clean_mel).astype(f32)
    noise = widen(noise_mel).astype(f32)
    noisy = (1.0 - (1.0 - SIGMA) * tau) * noise + tau * clean
    context = clean * (valid_ext * (1.0 - masked_ext))
    target = (clean - (1.0 - SIGMA) * noise)[inside]
    onehot = (widen(phone_ids)[:, None] == jnp.arange(PHONES)).astype(bf)
    features_ext = jnp.concatenate([noisy.astype(bf), context.astype(bf), onehot], axis=-1)
    features = features_ext[inside]

    wires = Wires(ndp, nmp)
    owners = [wires.owner_mp(m // 2, m % 2) if own else m for m in range(nmp)]
    owners = jnp.stack(owners) if own else jnp.arange(nmp)
    heads = (owners[:, None] * (HEADS // nmp) + jnp.arange(HEADS // nmp)).reshape(-1)
    slopes = jnp.exp2(-8.0 * (heads + 1).astype(f32) / HEADS)
    if own:
        places = jnp.stack([base, (1 - seq) * rows, size]).astype(jnp.int32)
        fore = fore_all(
            ndp,
            nmp,
            ForeIn(
                places=places,
                slopes=slopes,
                thin_own=thin,
                near_own=attn_qkv.astype(bf),
                mid_own=mid,
                down_own=ffn_down.T.astype(bf),
                features=columns(features_ext, THIN_CHAN),
            ),
        )
        thin = fore.thin
    else:
        thin = lax.all_gather(thin, ("dp", "mp"), axis=0, tiled=True)
        w_qkv = lax.all_gather(attn_qkv.astype(bf), ("mp", "dp"), axis=0, tiled=True)
        w_qkv = w_qkv.reshape(nmp, -1, c_qkv)
        rest = jnp.concatenate([mid, ffn_down.T.astype(bf)], axis=1)
        rest = lax.all_gather(rest, ("mp", "dp"), axis=0, tiled=True)
        rest = rest.reshape(nmp, -1, rest.shape[1])
        owners = jnp.arange(nmp)
    model = thin.shape[0]
    digits = thin[:, THIN_HEAD + mel : THIN_HEAD + mel + 2 * micro]
    digits = jnp.sum(digits.reshape(ndp, -1, 2 * micro)[:, 0].astype(f32), axis=0)
    count = lax.dynamic_slice_in_dim(digits, 2 * batch, 2, 0)
    count = count[0] * 32.0 + count[1]

    if own:
        lanes = jnp.arange(128) < mel
        middle = middle_all(
            ndp,
            nmp,
            MiddleIn(
                second=fore.second,
                a2=fore.a2,
                active=fore.active,
                slope=fore.slope,
                chan=fore.chan,
                w_head=jnp.where(lanes, thin[:, THIN_HEAD:], 0),
                target=jnp.pad(target, ((0, 0), (0, 128 - mel))),
                weights=jnp.broadcast_to(masked / count, (rows, 128)),
                mid=fore.mid,
                down=fore.down,
            ),
        )
        given = BackIn(
            places=places,
            slopes=slopes,
            loss=middle.loss,
            g_up=middle.g_up,
            g_down=middle.g_down,
            dattn=middle.dattn,
            mixed=fore.mixed,
            extra=middle.extra,
            g_head=middle.g_head,
            chan=fore.chan,
            packed=fore.packed,
            other=fore.other,
            mixed_t=fore.mixed_t,
            lse=fore.lse,
            dmixed=middle.dmixed,
            w_qkv=fore.near,
            first=fore.first,
            conv=fore.conv,
            dsecond=middle.dsecond,
            hm=fore.hm,
            features=columns(features, THIN_CHAN),
        )
        g_thin, g_up, g_down, g_qkv, g_out, sums = back_all(ndp, nmp, given)
    else:
        w_out = rest[:, :, :c_out]
        w_up = rest[:, :, c_out : c_out + c_up]
        w_down = rest[:, :, c_out + c_up :]
        w_in = thin[:, :width]
        channel = thin[:, THIN_CHAN : THIN_CHAN + nch].T.astype(f32)
        w_head = thin[:, THIN_HEAD : THIN_HEAD + mel]
        taps = channel[:KERNEL]
        vecs = channel[KERNEL:]

        start_ext = rdot(features_ext, w_in) + vecs[6]
        hm = start_ext * valid_ext
        conv = jnp.zeros((rows, model), f32) + vecs[7]
        for k in range(KERNEL):
            conv = conv + taps[k] * hm[k + 1 : k + 1 + rows]
        first = start_ext[inside] + gelu(conv)
        x_one, r_one = norm_parts(first)
        act_one = (x_one * vecs[0] + vecs[1]).astype(bf)

        groups = [[g * seqs + s for s in range(seqs)] for g in range(micro)]

        def shift(x, i):
            pairs = [(g[(s + i) % seqs], g[s]) for g in groups for s in range(seqs)]
            return lax.ppermute(x, "mp", pairs)

        def unshift(x, i):
            pairs = [(g[s], g[(s + i) % seqs]) for g in groups for s in range(seqs)]
            return lax.ppermute(x, "mp", pairs)

        packed = jnp.einsum("rd,mdc->rmc", act_one, w_qkv, preferred_element_type=f32).astype(bf)
        packed = packed.reshape(rows, HEADS, 3, HEAD_DIM)
        query, key, value = packed[:, :, 0], packed[:, :, 1], packed[:, :, 2]
        both = jnp.stack([key, value])
        both = jnp.concatenate([both] + [shift(both, i) for i in range(1, seqs)], axis=1)
        keys, values = both[0], both[1]
        blocks = (seq + jnp.arange(seqs)) % seqs
        key_place = (blocks[:, None] * rows + jnp.arange(rows)).reshape(-1)
        query_place = base + jnp.arange(rows)
        distance = jnp.abs(query_place[:, None] - key_place[None, :]).astype(f32)
        raw = jnp.einsum("qhd,khd->hqk", query, keys, preferred_element_type=f32)
        score = raw * SCALE - slopes[:, None, None] * distance
        score = jnp.where((key_place < size)[None, None, :], score, -1000000000.0)
        top = jnp.max(score, axis=-1, keepdims=True)
        prob = jnp.exp(score - top)
        prob = prob / jnp.sum(prob, axis=-1, keepdims=True)
        prob_low = prob.astype(bf)
        mixed = jnp.einsum("hqk,khd->qhd", prob_low, values, preferred_element_type=f32)
        mixed = mixed.astype(bf).reshape(rows, nmp, c_out)
        mixed = [mixed[:, m] for m in range(nmp)]
        attn = jnp.zeros((rows, model), f32)
        for m in range(nmp):
            attn = attn + rdot(mixed[m], w_out[m])
        second = first + attn

        x_two, r_two = norm_parts(second)
        act_two = (x_two * vecs[2] + vecs[3]).astype(bf)
        ffn = jnp.zeros((rows, model), f32)
        hidden = []
        active = []
        for m in range(nmp):
            hidden.append(dot(act_two, w_up[m]))
            active.append(gelu(hidden[m]).astype(bf))
            ffn = ffn + rdot(active[m], w_down[m])
        third = second + ffn

        x_three, r_three = norm_parts(third)
        act_three = (x_three * vecs[4] + vecs[5]).astype(bf)
        error = dot(act_three, w_head) - target
        weight_rows = masked / count
        loss_local = jnp.sum(weight_rows * error * error)
        dpred = (2.0 * weight_rows * error).astype(bf)
        g_head = tdot(act_three, dpred)
        dthird, dg3, db3 = norm_back(rdot(dpred, w_head), x_three, r_three, vecs[4])

        dffn = dthird.astype(bf)
        da2 = jnp.zeros((rows, model), f32)
        dhids = []
        for m in range(nmp):
            dhid = gelu_back(hidden[m], dot(dffn, w_down[m])).astype(bf)
            dhids.append(dhid)
            da2 = da2 + rdot(dhid, w_up[m])
        dnorm, dg2, db2 = norm_back(da2, x_two, r_two, vecs[2])
        dsecond = dthird + dnorm

        dattn = dsecond.astype(bf)
        g_out = [tdot(dattn, mixed[m]).astype(bf) for m in range(nmp)]
        dmixed = [dot(dattn, w_out[m]).astype(bf) for m in range(nmp)]
        dmixed = jnp.stack(dmixed, axis=1).reshape(rows, HEADS, HEAD_DIM)
        dvalues = jnp.einsum("hqk,qhd->khd", prob_low, dmixed, preferred_element_type=f32)
        dprob = jnp.einsum("qhd,khd->hqk", dmixed, values, preferred_element_type=f32)
        dscore = prob * (dprob - jnp.sum(prob * dprob, axis=-1, keepdims=True))
        draw = (dscore * SCALE).astype(bf)
        dquery = jnp.einsum("hqk,khd->qhd", draw, keys, preferred_element_type=f32)
        dkeys = jnp.einsum("hqk,qhd->khd", draw, query, preferred_element_type=f32)
        dboth = jnp.stack([dkeys, dvalues])
        parts = [dboth[:, i * rows : (i + 1) * rows] for i in range(seqs)]
        dboth = parts[0]
        for i in range(1, seqs):
            dboth = dboth + unshift(parts[i].astype(bf), i).astype(f32)
        dpacked = jnp.stack([dquery, dboth[0], dboth[1]], axis=2).astype(bf)
        dpacked = dpacked.reshape(rows, nmp, c_qkv)
        dpacked = [dpacked[:, m] for m in range(nmp)]
        g_qkv = [tdot(act_one, dpacked[m]).astype(bf) for m in range(nmp)]
        da1 = jnp.zeros((rows, model), f32)
        for m in range(nmp):
            da1 = da1 + rdot(dpacked[m], w_qkv[m])

        dnorm, dg1, db1 = norm_back(da1, x_one, r_one, vecs[0])
        dfirst = dsecond + dnorm
        dconv = gelu_back(conv, dfirst)
        right = lax.ppermute(
            dconv[:PAD], "mp", [(g[s + 1], g[s]) for g in groups for s in range(seqs - 1)]
        )
        left = lax.ppermute(
            dconv[rows - PAD :], "mp", [(g[s], g[s + 1]) for g in groups for s in range(seqs - 1)]
        )
        dconv_ext = jnp.concatenate([left, dconv, right], axis=0)
        back = jnp.zeros((rows, model), f32)
        g_taps = []
        for k in range(KERNEL):
            back = back + taps[k] * dconv_ext[2 * PAD - 1 - k : 2 * PAD - 1 - k + rows]
            g_taps.append(jnp.sum(dconv * hm[k + 1 : k + 1 + rows], axis=0))
        dstart = dfirst + valid * back
        g_in = tdot(dstart.astype(bf), features)
        g_rows = g_taps + [dg1, db1, dg2, db2, dg3, db3, jnp.sum(dstart, axis=0), jnp.sum(dconv, axis=0)]
        g_chan = jnp.stack(g_rows, axis=1)

        g_thin = jnp.concatenate(
            [
                columns(g_in, THIN_CHAN),
                columns(g_chan, THIN_HEAD - THIN_CHAN),
                columns(g_head, THIN - THIN_HEAD),
            ],
            axis=1,
        )
        g_up = [tdot(act_two, dhids[m]).astype(bf) for m in range(nmp)]
        g_down = [tdot(dffn, active[m]).astype(bf) for m in range(nmp)]
        terms = [g_thin, jnp.stack(g_up), jnp.stack(g_down), jnp.stack(g_qkv), jnp.stack(g_out)]
        g_thin = lax.psum_scatter(g_thin, ("dp", "mp"), scatter_dimension=0, tiled=True)
        sums = [g_thin.astype(f32)] + [
            lax.psum_scatter(
                t.reshape(-1, t.shape[2]), ("mp", "dp"), scatter_dimension=0, tiled=True
            ).astype(f32)
            for t in terms[1:]
        ]
        g_thin, g_up, g_down, g_qkv, g_out = sums
        squares = sum(jnp.sum(g * g) for g in sums)
        sums = lax.psum(jnp.stack([loss_local, squares])[None], ("dp", "mp"))
    sums = sums[0]
    loss = sums[0]
    grad_norm = jnp.sqrt(sums[1])
    factor = CLIP_AT / jnp.maximum(grad_norm, CLIP_AT)

    tw, tm, tv = adam_update(in_table, table_first, table_second, g_thin[:, :width].T, factor)
    cw, cm, cv = adam_update(
        channel_rows, channel_first, channel_second, g_thin[:, THIN_CHAN : THIN_CHAN + nch].T, factor
    )
    hw, hm_, hv = adam_update(mel_head, head_first, head_second, g_thin[:, THIN_HEAD : THIN_HEAD + mel], factor)
    qw, qm, qv = adam_update(attn_qkv, qkv_first, qkv_second, g_qkv, factor)
    ow, om, ov = adam_update(attn_out, merge_first, merge_second, g_out.T, factor)
    uw, um, uv = adam_update(ffn_up, upward_first, upward_second, g_up, factor)
    dw, dm, dv = adam_update(ffn_down, downward_first, downward_second, g_down.T, factor)
    return (
        loss, grad_norm,
        tw, tm, tv, cw, cm, cv, qw, qm, qv, ow, om, ov, uw, um, uv, dw, dm, dv, hw, hm_, hv,
    )


def solution(mesh):
    wide = P(None, ("dp", "mp"))
    tall = P(("dp", "mp"), None)
    down = P("dp", "mp")
    flat = P("mp", "dp")
    weights = (wide, wide, down, flat, down, flat, tall)
    pair = P(None, "dp")
    data = (P(None, "dp", None, None), P(None, "dp", None, None), pair, pair, pair)
    data = data + (P(None, "dp", None), pair)
    return jax.shard_map(
        shards,
        mesh=mesh,
        in_specs=data + weights * 3,
        out_specs=(P(), P()) + tuple(w for w in weights for _ in range(3)),
        check_vma=False,
    )
```

```python
import functools
from typing import Any, NamedTuple

import jax
import jax.numpy as jnp
from jax import lax
from jax.experimental import pallas as pl
from jax.experimental.pallas import tpu as pltpu
from jax.sharding import PartitionSpec as P

HEADS = 16
HEAD_DIM = 64
PHONES = 128
KERNEL = 31
HALF = 15
PAD = 16
TSTEPS = 1000
STEP = 10

SIGMA = 1e-05
BETA_ONE = 0.9
BETA_TWO = 0.999
EPSILON = 1e-08
DECAY = 0.01
RATE = 0.15
CLIP_AT = 0.1
NORM_EPS = 1e-05
SCALE = HEAD_DIM**-0.5
bf = jnp.bfloat16
f32 = jnp.float32


def gelu(v):
    return jax.nn.gelu(v, approximate=True)


def gelu_back(v, dv):
    return jax.vjp(gelu, v)[1](dv)[0]


def dot(left, right):
    return jnp.dot(left, right, preferred_element_type=f32)


def tdot(left, right):
    return lax.dot_general(
        left, right, (((0,), (0,)), ((), ())), preferred_element_type=f32
    )


def rdot(left, right):
    return lax.dot_general(
        left, right, (((1,), (1,)), ((), ())), preferred_element_type=f32
    )


def norm_parts(v):
    centered = v - jnp.mean(v, axis=-1, keepdims=True)
    spread = jnp.mean(centered * centered, axis=-1, keepdims=True)
    r = lax.rsqrt(spread + NORM_EPS)
    return centered * r, r


def norm_back(da, xhat, r, gain):
    dgain = jnp.sum(da * xhat, axis=0)
    dbias = jnp.sum(da, axis=0)
    dx = da * gain
    dv = r * (
        dx
        - jnp.mean(dx, axis=-1, keepdims=True)
        - xhat * jnp.mean(dx * xhat, axis=-1, keepdims=True)
    )
    return dv, dgain, dbias


def adam_update(weight, first, second, grad, factor):
    clipped = grad * factor
    first_new = BETA_ONE * first + (1.0 - BETA_ONE) * clipped
    second_new = BETA_TWO * second + (1.0 - BETA_TWO) * clipped * clipped
    first_hat = first_new / (1.0 - BETA_ONE**STEP)
    second_hat = second_new / (1.0 - BETA_TWO**STEP)
    weight_new = weight - RATE * (first_hat / (jnp.sqrt(second_hat) + EPSILON) + DECAY * weight)
    return (weight_new, first_new, second_new)


MESH = pl.DeviceIdType.MESH
AXES = ("z", "x", "y", "c")


class Wires:
    def __init__(self, ndp, nmp):
        self.sizes = {"z": ndp // 2, "x": 2, "y": nmp // 2, "c": 2}
        dp = lax.axis_index("dp")
        mp = lax.axis_index("mp")
        self.at = {"z": dp // 2, "x": dp % 2, "y": mp // 2, "c": mp % 2}

    def peer(self, axis, k):
        at = dict(self.at)
        at[axis] = lax.rem(at[axis] + k, self.sizes[axis])
        return (at["z"] * 2 + at["x"], at["y"] * 2 + at["c"])

    def owner_mp(self, ky, kc):
        ny = self.sizes["y"]
        return lax.rem(self.at["y"] + ny - ky, ny) * 2 + lax.rem(self.at["c"] + 2 - kc, 2)

    def near(self, k):
        nmp = self.sizes["y"] * self.sizes["c"]
        return (lax.axis_index("dp"), lax.rem(lax.axis_index("mp") + k, nmp))

    def far(self, k):
        ndp = self.sizes["z"] * self.sizes["x"]
        return (lax.rem(lax.axis_index("dp") + k, ndp), lax.axis_index("mp"))

    def align(self, again):
        fars = [self.far(k) for k in range(1, self.sizes["z"] * self.sizes["x"])]
        self.greet([self.near(k) for k in range(1, self.sizes["y"] * self.sizes["c"])] + fars)
        for p in fars:
            pl.semaphore_signal(again, inc=1, device_id=p, device_id_type=MESH)
        pl.semaphore_wait(again, len(fars))

    def greet(self, peers):
        barrier = pltpu.get_barrier_semaphore()
        for p in peers:
            pl.semaphore_signal(barrier, inc=1, device_id=p, device_id_type=MESH)
        pl.semaphore_wait(barrier, len(peers))


def slot_number(sizes, k):
    return ((k["z"] * sizes["x"] + k["x"]) * sizes["y"] + k["y"]) * sizes["c"] + k["c"]


def spread(sizes, order):
    slots = [(dict.fromkeys(AXES, 0), -1)]
    for stage, axis in enumerate(order):
        slots += [
            ({**k, axis: n}, stage) for n in range(1, sizes[axis]) for k, _ in list(slots)
        ]
    return slots


class Gather:
    def __init__(self, wires, order, own, slot, send, recv):
        self.wires, self.order, self.own, self.slot = wires, order, own, slot
        self.send, self.recv = send, recv
        self.slots = spread(wires.sizes, order)
        self.by_number = {slot_number(wires.sizes, k): i for i, (k, _) in enumerate(self.slots)}
        self.started = []

    def forward(self, source, k, stage):
        for later in range(stage + 1, len(self.order)):
            axis = self.order[later]
            for n in range(1, self.wires.sizes[axis]):
                there = {**k, axis: n}
                number = slot_number(self.wires.sizes, there)
                copy = pltpu.make_async_remote_copy(
                    source, self.slot(there, k), self.send.at[number], self.recv.at[number],
                    device_id=self.wires.peer(axis, n), device_id_type=MESH,
                )
                copy.start()
                self.started.append((copy, number))

    def begin(self):
        k, stage = self.slots[0]
        self.forward(self.own, k, stage)

    def arrive(self, number):
        k, stage = self.slots[self.by_number[number]]
        here = self.slot(k, k)
        pltpu.make_async_remote_copy(
            here, here, self.send.at[number], self.recv.at[number],
            device_id=self.wires.peer("c", 1), device_id_type=MESH,
        ).wait_recv()
        self.forward(here, k, stage)

    def finish(self):
        for copy, _ in self.started:
            copy.wait_send()


FIRST = ("z", "x", "y", "c")
OTHER = ("z", "y", "x", "c")


def total(ref):
    rows = 8

    def body(i, part):
        x = ref[pl.ds(i * rows, rows)]
        return part + x * x

    part = lax.fori_loop(0, ref.shape[0] // rows, body, jnp.zeros((rows, ref.shape[1]), f32))
    return jnp.sum(part)


BLOCK = 256
TILE = 64
FAR = 1e12


def distances(dist, base, other_base, size):
    rows = dist.shape[1]

    def body(i, _):
        here = pl.ds(pl.multiple_of(i * TILE, TILE), TILE)
        down = lax.broadcasted_iota(jnp.int32, (TILE, rows), 0) + i * TILE
        key = jnp.where(down < rows, base + down, other_base + down - rows)
        query = base + lax.broadcasted_iota(jnp.int32, (TILE, rows), 1)
        dist[here] = jnp.where(key < size, jnp.abs(key - query).astype(f32), FAR)
        return 0

    lax.fori_loop(0, dist.shape[0] // TILE, body, 0)


def key_blocks(packed, other, m, col):
    rows = packed.shape[1]
    twin = m + 1 - 2 * (m % 2)
    for part, (ref, index) in enumerate(((packed, m), (other, twin))):
        for start in range(0, rows, BLOCK):
            k = ref[index, start : start + BLOCK, col + HEAD_DIM : col + 2 * HEAD_DIM]
            v = ref[index, start : start + BLOCK, col + 2 * HEAD_DIM : col + 3 * HEAD_DIM]
            yield part, start, part * rows + start, k, v


def attend(packed, other, dist, slopes, mixed, mixed_t, lse, score, m):
    heads = packed.shape[2] // (3 * HEAD_DIM)
    for j in range(heads):
        col = j * 3 * HEAD_DIM
        q = packed[m, :, col : col + HEAD_DIM] * bf(SCALE)
        slope = slopes[m * heads + j]
        top = None
        for _, _, at, k, _ in key_blocks(packed, other, m, col):
            s = rdot(k, q) - slope * dist[at : at + BLOCK]
            score[at : at + BLOCK] = s
            peak = jnp.max(s, axis=0, keepdims=True)
            top = peak if top is None else jnp.maximum(top, peak)
        total_e = jnp.zeros_like(top)
        acc = None
        for _, _, at, _, v in key_blocks(packed, other, m, col):
            e = jnp.exp(score[at : at + BLOCK] - top)
            total_e = total_e + jnp.sum(e, axis=0, keepdims=True)
            part = tdot(v, e.astype(bf))
            acc = part if acc is None else acc + part
        out = acc / total_e
        row = (m * heads + j) * HEAD_DIM
        mixed_t[pl.ds(pl.multiple_of(row, HEAD_DIM), HEAD_DIM)] = out
        mixed[m, :, j * HEAD_DIM : (j + 1) * HEAD_DIM] = out.T.astype(bf)
        lse[m * heads + j] = top + jnp.log(total_e)
        yield


def attend_back(packed, other, dist, slopes, mixed_t, lse, dmixed, down, dother, m):
    heads = packed.shape[2] // (3 * HEAD_DIM)
    for j in range(heads):
        col = j * 3 * HEAD_DIM
        q = packed[m, :, col : col + HEAD_DIM] * bf(SCALE)
        slope = slopes[m * heads + j]
        row = (m * heads + j) * HEAD_DIM
        mt = mixed_t[pl.ds(pl.multiple_of(row, HEAD_DIM), HEAD_DIM)]
        dm = dmixed[m, :, j * HEAD_DIM : (j + 1) * HEAD_DIM]
        delta = jnp.sum(dm.astype(f32).T * mt, axis=0, keepdims=True)
        level = lse[m * heads + j]
        dq = None
        for part, start, at, k, v in key_blocks(packed, other, m, col):
            p = jnp.exp(rdot(k, q) - slope * dist[at : at + BLOCK] - level)
            dv = dot(p.astype(bf), dm)
            t = (p * (rdot(v, dm) - delta)).astype(bf)
            dk = dot(t, q)
            more = tdot(k, t)
            dq = more if dq is None else dq + more
            here = slice(start, start + BLOCK)
            ref = dother if part else down.at[m]
            ref[here, col + HEAD_DIM : col + 2 * HEAD_DIM] = dk.astype(ref.dtype)
            ref[here, col + 2 * HEAD_DIM : col + 3 * HEAD_DIM] = dv.astype(ref.dtype)
        down[m, :, col : col + HEAD_DIM] = (dq * SCALE).T.astype(down.dtype)
        yield


def windows(x, count):
    for j in range(8):
        moved = x if j == 0 else pltpu.roll(x, x.shape[0] - j, 0)
        for far in range(0, count + 1, 8):
            if 1 <= far + j <= count:
                yield far + j, moved[far : far + TILE]


def convolve(hm, chan, conv, column):
    lanes = slice(column, column + 128)

    def body(r, _):
        start = pl.multiple_of(r * TILE, TILE)
        x = hm[pl.ds(start, TILE + 2 * PAD), lanes]
        acc = jnp.broadcast_to(chan[KERNEL + 7, lanes][None], (TILE, 128))
        for offset, moved in windows(x, KERNEL):
            acc = acc + chan[offset - 1, lanes][None] * moved
        conv[pl.ds(start, TILE), lanes] = acc
        return 0

    lax.fori_loop(0, conv.shape[0] // TILE, body, 0)


def convolve_back(dconv, hm, chan, back, gtaps, column):
    lanes = slice(column, column + 128)

    def body(r, _):
        start = pl.multiple_of(r * TILE, TILE)
        x = dconv[pl.ds(start, TILE + 2 * PAD), lanes]
        acc = jnp.zeros((TILE, 128), f32)
        for offset, moved in windows(x, KERNEL):
            acc = acc + chan[KERNEL - offset, lanes][None] * moved
        back[pl.ds(start, TILE), lanes] = acc
        here = x[PAD : PAD + TILE]
        y = hm[pl.ds(start, TILE + 2 * PAD), lanes]
        for offset, moved in windows(y, KERNEL):
            part = here * moved
            part = sum(part[i : i + 8] for i in range(8, TILE, 8)) + part[:8]
            rows_at = slice((offset - 1) * 8, offset * 8)
            gtaps[rows_at, lanes] = gtaps[rows_at, lanes] + part
        return 0

    lax.fori_loop(0, back.shape[0] // TILE, body, 0)


VMEM = pl.BlockSpec(memory_space=pltpu.VMEM)
SMEM = pl.BlockSpec(memory_space=pltpu.SMEM)


class Reduce:
    def __init__(self, wires, order, source, landing, out, send, recv):
        self.wires, self.order, self.source, self.landing = wires, order, source, landing
        self.out, self.send, self.recv = out, send, recv
        self.where = {}
        self.started = []
        sizes = {a: wires.sizes[a] if a in order else 1 for a in AXES}
        slots = [k for k, _ in spread(sizes, order[::-1])]
        self.stages = []
        for axis in order:
            self.stages.append([k for k in slots if k[axis]])
            slots = [k for k in slots if not k[axis]]
        self.by_number = {
            self.number(k): (stage, k) for stage, ks in enumerate(self.stages) for k in ks
        }
        self.summed = set()

    def number(self, k):
        return slot_number(self.wires.sizes, k)

    def now(self, k):
        n = self.number(k)
        return self.landing(self.where[n]) if n in self.where else self.source(k)

    def leave(self, stage, k):
        axis = self.order[stage]
        n = self.wires.sizes[axis]
        number = self.number(k)
        source = self.now(k)
        pltpu.make_async_remote_copy(
            source, self.landing(k), self.send.at[number], self.recv.at[number],
            device_id=self.wires.peer(axis, (n - k[axis]) % n), device_id_type=MESH,
        ).start()
        self.started.append((k, number))

    def keep(self):
        add_rows(self.out, self.source(dict.fromkeys(AXES, 0)), None)

    def depart(self, number):
        self.leave(0, self.by_number[number][1])

    def terms(self, stage, kept):
        return {
            self.number({**kept, axis: n})
            for axis in self.order[: stage + 1]
            for n in range(1, self.wires.sizes[axis])
        }

    def arrive(self, number):
        stage, k = self.by_number[number]
        self.summed.add(number)
        here = self.landing(k)
        axis = self.order[stage]
        pltpu.make_async_remote_copy(
            here, here, self.send.at[number], self.recv.at[number],
            device_id=self.wires.peer(axis, 1), device_id_type=MESH,
        ).wait_recv()
        kept = {**k, axis: 0}
        if not any(kept.values()):
            add_rows(self.out, self.out, here)
            return
        add_rows(here, self.now(kept), here)
        self.where[self.number(kept)] = k
        last = k[axis] == self.wires.sizes[axis] - 1
        if last and stage + 1 < len(self.order) and kept[self.order[stage + 1]]:
            assert self.terms(stage, kept) <= self.summed
            self.leave(stage + 1, kept)

    def finish(self):
        for k, number in self.started:
            here = self.landing(k)
            pltpu.make_async_remote_copy(
                here, here, self.send.at[number], self.recv.at[number],
                device_id=self.wires.peer("c", 1), device_id_type=MESH,
            ).wait_send()


class Crossing:
    def __init__(self, *parts):
        self.parts = parts

    def make(self):
        (src, *s), (dst, *d), send, recv, i, wires = self.parts
        return pltpu.make_async_remote_copy(
            src.at[s[0]] if s else src, dst.at[d[0]] if d else dst, send.at[i], recv.at[i],
            device_id=wires.peer("c", 1), device_id_type=MESH,
        )

    def wait_send(self):
        self.make().wait_send()

    def wait_recv(self):
        self.make().wait_recv()


def add_rows(out, left, right):
    step = 16

    def body(i, _):
        here = pl.ds(pl.multiple_of(i * step, step), step)
        value = left[here].astype(f32)
        if right is not None:
            value = value + right[here].astype(f32)
        out[here] = value.astype(out.dtype)
        return 0

    lax.fori_loop(0, out.shape[0] // step, body, 0)


def gelu_slope(v):
    cube = 0.044715 * v * v * v
    t = jnp.tanh(0.7978845608028654 * (v + cube))
    inner = 0.7978845608028654 * (1.0 + 3.0 * 0.044715 * v * v)
    return 0.5 * (1.0 + t) + 0.5 * v * (1.0 - t * t) * inner


THIN_CHAN = 384
THIN_HEAD = 512
THIN = 640


class BackIn(NamedTuple):
    places: Any
    slopes: Any
    loss: Any
    g_up: Any
    g_down: Any
    dattn: Any
    mixed: Any
    extra: Any
    g_head: Any
    chan: Any
    packed: Any
    other: Any
    mixed_t: Any
    lse: Any
    dmixed: Any
    w_qkv: Any
    first: Any
    conv: Any
    dsecond: Any
    hm: Any
    features: Any


class BackRefs(NamedTuple):
    places: Any
    slopes: Any
    loss: Any
    g_up: Any
    g_down: Any
    dattn: Any
    mixed: Any
    extra: Any
    g_head: Any
    chan: Any
    packed: Any
    other: Any
    mixed_t: Any
    lse: Any
    dmixed: Any
    w_qkv: Any
    first: Any
    conv: Any
    dsecond: Any
    hm: Any
    features: Any
    o_thin: Any
    o_up: Any
    o_down: Any
    o_qkv: Any
    o_out: Any
    sums: Any
    g_qkv: Any
    g_out: Any
    thin: Any
    l_up0: Any
    l_up1: Any
    l_down0: Any
    l_down1: Any
    l_qkv0: Any
    l_qkv1: Any
    l_out0: Any
    l_out1: Any
    l_thin: Any
    down: Any
    dother: Any
    l_other: Any
    a1: Any
    l_a1: Any
    l_dattn: Any
    l_mixed: Any
    l_dpack: Any
    halo: Any
    edge: Any
    parts: Any
    w_buf: Any
    rows_buf: Any
    send: Any
    recv: Any
    c_send: Any
    c_recv: Any
    local: Any
    near_send: Any
    near_recv: Any
    far_send: Any
    far_recv: Any
    again: Any


COLS = 256


def by_tiles(count, size, body):
    def step(i, _):
        body(pl.ds(pl.multiple_of(i * size, size), size))
        return 0

    lax.fori_loop(0, count // size, step, 0)


def fold(x):
    return jnp.sum(x, axis=0, keepdims=True)


def norm_turn(da, xhat, scale, gain):
    dx = da * gain
    return scale * (
        dx
        - jnp.mean(dx, axis=-1, keepdims=True)
        - xhat * jnp.mean(dx * xhat, axis=-1, keepdims=True)
    )


FORE_TURNS = (
    (
        1, 8, 4, 2, 9, 16, 5, 3, 24, 17, 25, 12, 10, 6, 20, 13, 11, 28, 18, 7, 21, 26, 29, 19, 14, 27, 22,
        15, 30, 23, 31, 33, 65, 36, 34, 68, 66, 40, 48,
    ),
    (56,),
    (),
    (72,),
    (37, 35),
    (69, 67),
    (41,),
    (49,),
    (38,),
    (97, 70),
    (129,),
    (80, 42, 44, 57),
    (73, 88, 50, 52),
    (),
    (39, 71),
    (98,),
    (100, 81, 43, 45),
    (),
    (89, 51, 53),
    (130,),
    (132,),
    (104, 58),
    (
        60, 74, 76, 82, 84, 59, 61, 75, 77, 83, 46, 85, 92, 90, 47, 93, 91, 54, 55, 78, 86, 79, 87, 62, 94,
        63, 95, 99, 101, 112, 131, 120, 133, 105, 134, 108, 136, 102, 144, 106, 152,
    ),
    (),
    (),
    (),
    (113,),
    (121, 135, 109, 137, 103, 145, 107, 116, 153, 114),
    (),
    (124,),
    (122, 161, 193),
    (140,),
    (117, 115, 110),
    (),
    (148, 125, 138, 168, 123),
    (141,),
    (156, 176, 146, 111),
    (184, 164),
    (149, 154, 139, 169),
    (196,),
    (162, 157, 177, 147),
    (142, 200, 185, 194, 165),
    (155, 172, 208),
    (118, 143, 126, 150, 119, 127, 151, 158, 159, 197, 163, 180, 216, 201, 195, 173, 209, 170, 188),
    (178,),
    (186,),
    (204, 181, 166, 217, 171, 189),
    (198, 202, 179),
    (212, 174, 187),
    (
        220, 205, 210, 167, 199, 182, 203, 206, 213, 218, 175, 221, 211, 183, 207, 219, 214, 190, 215, 222,
        191, 223,
    ),
)
BACK_TURNS = (
    (34, 100, 42, 108, 50, 116, 58, 124, 38, 102, 46, 110),
    (54, 118),
    (62, 126, 162, 228, 2, 68),
    (170, 236, 10, 76),
    (178, 244, 18, 84),
    (186, 252, 26, 92, 166, 230, 6, 70),
    (14, 78),
    (22, 86),
    (30, 94),
    (130, 196),
    (174, 238, 138, 204, 182, 246, 146, 212),
    (190, 254, 154, 220),
    (290, 356, 298, 364, 306, 372, 134, 198),
    (314, 380, 66, 4, 294, 358, 74, 12, 302, 366),
    (310, 374, 318, 382, 82, 20),
    (90, 28),
    (72, 142, 206, 8, 150, 214),
    (158, 222, 258, 324, 266, 332),
    (274, 340, 80),
    (194, 132, 282, 348),
    (262, 326, 270, 334, 278, 342, 16, 286, 350),
    (88, 202, 140),
    (418, 484, 426, 492, 434, 500, 442, 508, 422, 486, 430, 494, 438, 502, 446, 510, 24, 210, 148),
    (218, 156, 322, 260),
    (330, 268, 338, 276, 346, 284, 200),
    (),
    (386, 452, 136, 394, 460),
    (402, 468),
    (410, 476, 208),
    (390, 454),
    (398, 462, 144, 406, 470),
    (414, 478, 216),
    (388, 450, 152),
    (328, 264, 396, 458),
    (336, 404, 466, 272, 344),
    (
        545, 553, 561, 569, 549, 557, 565, 573, 547, 555, 563, 571, 551, 559, 567, 575, 280, 412, 474, 392,
        456, 513, 521, 529, 537, 517, 525, 533, 541, 515, 523, 531, 539, 519, 527, 535, 543, 400, 514, 522,
        530, 464, 538, 518, 408, 526, 534, 516, 542, 472, 524, 532, 540, 520, 528, 536,
    ),
)


class ForeIn(NamedTuple):
    places: Any
    slopes: Any
    thin_own: Any
    near_own: Any
    mid_own: Any
    down_own: Any
    features: Any


class ForeOut(NamedTuple):
    thin: Any
    near: Any
    mid: Any
    down: Any
    hm: Any
    conv: Any
    first: Any
    packed: Any
    other: Any
    mixed: Any
    mixed_t: Any
    lse: Any
    chan: Any
    second: Any
    a2: Any
    active: Any
    slope: Any


class ForeRefs(NamedTuple):
    places: Any
    slopes: Any
    thin_own: Any
    near_own: Any
    mid_own: Any
    down_own: Any
    features: Any
    o_thin: Any
    o_near: Any
    mid: Any
    down: Any
    o_hm: Any
    o_conv: Any
    o_first: Any
    o_packed: Any
    o_other: Any
    o_mixed: Any
    o_mixed_t: Any
    o_lse: Any
    o_chan: Any
    o_second: Any
    o_a2: Any
    o_active: Any
    o_slope: Any
    thin: Any
    near: Any
    hm: Any
    conv: Any
    first: Any
    packed: Any
    other: Any
    mixed: Any
    mixed_t: Any
    lse: Any
    chan: Any
    second: Any
    a2: Any
    active: Any
    slope: Any
    a1: Any
    dist: Any
    score: Any
    w: Any
    send: Any
    recv: Any
    local: Any
    c_send: Any
    c_recv: Any
    again: Any


def fore_kernel(ndp, nmp, *refs):
    r = ForeRefs(*refs)
    wires = Wires(ndp, nmp)
    wires.align(r.again)
    sizes = wires.sizes
    thin_rows = r.thin_own.shape[0]
    rows, model = r.first.shape
    size = r.places[2]

    def thin_slot(k, sent):
        block = (k["z"] * sizes["x"] + k["x"]) * nmp + wires.owner_mp(sent["y"], sent["c"])
        return r.thin.at[pl.ds(pl.multiple_of(block * thin_rows, thin_rows), thin_rows)]

    flows = [Gather(wires, FIRST, r.thin_own, thin_slot, r.send.at[0], r.recv.at[0])]

    def wide_flow(own, out, half, order):
        height = own.shape[0] // 2

        def slot(k, sent):
            start = (k["z"] * sizes["x"] + k["x"]) * 2 * height + half * height
            return out.at[k["y"] * sizes["c"] + k["c"], pl.ds(start, height)]

        n = len(flows)
        part = own.at[pl.ds(half * height, height)]
        flows.append(Gather(wires, order, part, slot, r.send.at[n], r.recv.at[n]))
        return flows[-1]

    near = [wide_flow(r.near_own, r.near, h, o) for h, o in enumerate((FIRST, OTHER))]
    mid = [wide_flow(r.mid_own, r.mid, h, o) for h, o in enumerate((FIRST, OTHER))]
    down = [wide_flow(r.down_own, r.down, h, o) for h, o in enumerate((FIRST, OTHER))]
    zero = dict.fromkeys(AXES, 0)
    kept = [
        pltpu.make_async_copy(f.own, f.slot(zero, zero), r.local.at[i])
        for i, f in enumerate(flows)
    ]
    for copy in kept:
        copy.start()
    for f in flows[:1] + near:
        f.begin()
    turns = iter(FORE_TURNS)
    slots = ndp * nmp
    saves = []

    def save(src, dst):
        copy = pltpu.make_async_copy(src, dst, r.local.at[len(flows) + nmp + len(saves)])
        copy.start()
        saves.append(copy)

    def turn():
        for code in next(turns):
            flows[code // slots].arrive(code % slots)

    turn()
    for f in mid:
        f.begin()
    for copy in kept:
        copy.wait()

    for i in range(0, model, 128):
        cols = r.thin[i : i + 128, THIN_CHAN:THIN_HEAD].astype(f32)
        r.chan[:, i : i + 128] = cols.T
    save(r.chan, r.o_chan)
    save(r.thin, r.o_thin)
    distances(r.dist, r.places[0], r.places[1], size)
    turn()

    for column in range(0, model, 128):
        cols = slice(column, column + 128)
        h = rdot(r.features[...], r.thin[cols, :THIN_CHAN])
        h = h + r.chan[KERNEL + 6, cols][None]
        place = r.places[0] - PAD + lax.broadcasted_iota(jnp.int32, (h.shape[0], 1), 0)
        r.first[:, cols] = h[PAD : PAD + rows]
        r.hm[:, cols] = jnp.where((place >= 0) & (place < size), h, 0.0)
        turn()
    for c in range(0, model, 128):
        convolve(r.hm, r.chan, r.conv, c)
        turn()

    def norm(i, _):
        here = pl.ds(pl.multiple_of(i * TILE, TILE), TILE)
        v = r.conv[here]
        inner = 0.7978845608028654 * v * (1.0 + 0.044715 * v * v)
        first = r.first[here] + v * (0.5 + 0.5 * jnp.tanh(inner))
        r.first[here] = first
        xhat, _ = norm_parts(first)
        r.a1[here] = (xhat * r.chan[KERNEL][None] + r.chan[KERNEL + 1][None]).astype(bf)

        return 0

    save(r.hm, r.o_hm)
    save(r.conv, r.o_conv)
    for i in range(0, rows // TILE, 2):
        lax.fori_loop(i, i + 2, norm, 0)
        turn()
    save(r.first, r.o_first)
    turn()
    crossings = []
    width = r.packed.shape[2]
    for m in range(nmp):
        def expand(cols):
            r.packed[m, :, cols] = dot(r.a1[...], r.near[m, :, cols]).astype(bf)

        by_tiles(width, COLS, expand)
        copy = pltpu.make_async_remote_copy(
            r.packed.at[m], r.other.at[m], r.c_send.at[m], r.c_recv.at[m],
            device_id=wires.peer("c", 1), device_id_type=MESH,
        )
        copy.start()
        crossings.append(copy)
        turn()
    for f in down:
        f.begin()
    save(r.near, r.o_near)
    save(r.packed, r.o_packed)
    for m in range(nmp):
        crossings[m + 1 - 2 * (m % 2)].wait_recv()
        for _ in attend(
            r.packed, r.other, r.dist, r.slopes, r.mixed, r.mixed_t, r.lse,
            r.score, m,
        ):
            turn()
    turn()
    for src, dst in (
        (r.other, r.o_other), (r.mixed, r.o_mixed), (r.mixed_t, r.o_mixed_t), (r.lse, r.o_lse)
    ):
        save(src, dst)
    loads = [
        pltpu.make_async_copy(r.mid.at[m], r.w.at[m], r.local.at[len(flows) + m])
        for m in range(nmp)
    ]
    for copy in loads:
        copy.start()
    c_out = r.mixed.shape[2]
    hid = r.active.shape[2]
    w_out = [r.w.at[m, :, pl.ds(0, c_out)] for m in range(nmp)]
    w_up = [r.w.at[m, :, pl.ds(c_out, hid)] for m in range(nmp)]
    for copy in loads:
        copy.wait()

    def project(cols):
        acc = r.first[:, cols]
        for m in range(nmp):
            acc = acc + rdot(r.mixed[m], w_out[m][cols, :])
        r.second[:, cols] = acc

    by_tiles(model, COLS, project)

    def second_norm(here):
        xhat, _ = norm_parts(r.second[here])
        gain, bias = r.chan[KERNEL + 2][None], r.chan[KERNEL + 3][None]
        r.a2[here] = (xhat * gain + bias).astype(bf)

    by_tiles(rows, TILE, second_norm)
    save(r.second, r.o_second)
    save(r.a2, r.o_a2)
    turn()
    for m in range(nmp):

        def gelu_pair(v, cols):
            square = v * v
            t = jnp.tanh(0.7978845608028654 * v * (1.0 + 0.044715 * square))
            half = 0.5 + 0.5 * t
            r.active[m, :, cols] = (v * half).astype(bf)
            inner = 0.3989422804014327 * (1.0 + 0.134145 * square)
            r.slope[m, :, cols] = (half + v * (1.0 - t * t) * inner).astype(bf)

        def expand(i, _):
            cols = [pl.ds(pl.multiple_of((2 * i + n) * COLS, COLS), COLS) for n in range(2)]
            values = [dot(r.a2[...], w_up[m][:, c]) for c in cols]
            for v, c in zip(values, cols):
                gelu_pair(v, c)
            return 0

        lax.fori_loop(0, hid // COLS // 2, expand, 0)
        save(r.active.at[m], r.o_active.at[m])
        save(r.slope.at[m], r.o_slope.at[m])
        turn()
    turn()
    assert next(turns, None) is None
    for copy in saves:
        copy.wait()
    for f in flows:
        f.finish()
    for copy in crossings:
        copy.wait_send()


def fore_all(ndp, nmp, given):
    model = given.near_own.shape[0] * ndp
    width = given.near_own.shape[1]
    hid = given.down_own.shape[1]
    wide = HEADS * HEAD_DIM
    rows = given.features.shape[0] - 2 * PAD
    struct = jax.ShapeDtypeStruct
    dma = pltpu.SemaphoreType.DMA
    anywhere = pl.BlockSpec(memory_space=pl.ANY)
    outs = [
        struct((model, THIN), bf),
        struct((nmp, model, width), bf),
        struct((nmp, model, given.mid_own.shape[1]), bf),
        struct((nmp, model, hid), bf),
        struct((rows + 2 * PAD, model), f32),
        struct((rows, model), f32),
        struct((rows, model), f32),
        struct((nmp, rows, width), bf),
        struct((nmp, rows, width), bf),
        struct((nmp, rows, wide // nmp), bf),
        struct((wide, rows), f32),
        struct((HEADS, 1, rows), f32),
        struct((128, model), f32),
        struct((rows, model), f32),
        struct((rows, model), bf),
        struct((nmp, rows, hid), bf),
        struct((nmp, rows, hid), bf),
    ]
    outs = pl.pallas_call(
        functools.partial(fore_kernel, ndp, nmp),
        name="fore",
        out_shape=outs,
        in_specs=[SMEM] * 2 + [anywhere] * 4 + [VMEM],
        out_specs=[anywhere] * len(outs),
        scratch_shapes=[pltpu.VMEM(o.shape, o.dtype) for o in outs[:2] + outs[4:]]
        + [
            pltpu.VMEM((rows, model), bf),
            pltpu.VMEM((2 * rows, rows), f32),
            pltpu.VMEM((2 * rows, rows), f32),
            pltpu.VMEM((nmp, model, given.mid_own.shape[1]), bf),
            dma((7, ndp * nmp)),
            dma((7, ndp * nmp)),
            dma((7 + nmp + 13 + 2 * nmp,)),
            dma((nmp,)),
            dma((nmp,)),
            pltpu.SemaphoreType.REGULAR,
        ],
        compiler_params=pltpu.CompilerParams(
            collective_id=0, has_side_effects=True, vmem_limit_bytes=62 << 20
        ),
    )(*given)
    return ForeOut(*outs)


class MiddleIn(NamedTuple):
    places: Any
    second: Any
    a2: Any
    active: Any
    slope: Any
    chan: Any
    thin: Any
    target: Any
    mid: Any
    down: Any


class MiddleOut(NamedTuple):
    g_up: Any
    g_down: Any
    dsecond: Any
    dattn: Any
    dmixed: Any
    extra: Any
    g_head: Any
    loss: Any


class MiddleRefs(NamedTuple):
    places: Any
    second: Any
    a2: Any
    active: Any
    slope: Any
    chan: Any
    thin: Any
    target: Any
    mid: Any
    down: Any
    g_up: Any
    g_down: Any
    dsecond: Any
    dattn: Any
    dmixed: Any
    extra: Any
    g_head: Any
    loss: Any
    ffn: Any
    l_a2: Any
    dffn: Any
    l_dffn: Any
    l_active: Any
    l_dhid: Any
    dhid: Any
    a3: Any
    stage: Any
    w: Any
    w_down: Any
    c_send: Any
    c_recv: Any
    local: Any


def middle_kernel(ndp, nmp, *refs):
    r = MiddleRefs(*refs)
    wires = Wires(ndp, nmp)
    partner = wires.peer("c", 1)
    wires.greet([partner])
    rows, model = r.second.shape
    ny = nmp // 2
    theirs = list(range(1, nmp, 2))
    mine = list(range(0, nmp, 2))
    hid = r.active.shape[2]
    c_out = r.mid.shape[2] - hid
    w_out = [r.w.at[m, :, pl.ds(0, c_out)] for m in range(nmp)]
    w_up = [r.w.at[m, :, pl.ds(c_out, hid)] for m in range(nmp)]
    loads = [
        [
            pltpu.make_async_copy(src.at[m], dst.at[m], r.local.at[i * nmp + m])
            for m in range(nmp)
        ]
        for i, (src, dst) in enumerate(((r.down, r.w_down), (r.mid, r.w)))
    ]
    for group in loads:
        for m in theirs + mine:
            group[m].start()
    w_down = [r.w_down.at[m] for m in range(nmp)]
    crossings = []

    def cross(src, dst):
        i = len(crossings)
        copy = pltpu.make_async_remote_copy(
            src, dst, r.c_send.at[i], r.c_recv.at[i],
            device_id=partner, device_id_type=MESH,
        )
        copy.start()
        crossings.append(copy)
        return copy

    def row(i):
        return r.chan[KERNEL + i][None]

    got_a2 = cross(r.a2, r.l_a2)
    got_active = [cross(r.active.at[m], r.l_active.at[m // 2]) for m in theirs]
    for m in theirs + mine:
        loads[0][m].wait()

        def shrink(cols):
            part = rdot(r.active[m], w_down[m][cols, :])
            r.ffn[:, cols] = part if m == theirs[0] else r.ffn[:, cols] + part

        by_tiles(model, COLS, shrink)

    def third_norm(here):
        xhat, _ = norm_parts(r.second[here] + r.ffn[here])
        r.a3[here] = (xhat * row(4) + row(5)).astype(bf)

    by_tiles(rows, TILE, third_norm)
    mel = r.places[6]
    lanes = lax.broadcasted_iota(jnp.int32, (16, 128), 1)
    digits = jnp.zeros((16, 128), f32)
    for d in range(ndp):
        start = d * (model // ndp)
        digits = digits + r.thin[start : start + 16, THIN_HEAD:].astype(f32)
    first_digit = mel + 2 * r.places[5]
    scale = jnp.where(lanes == first_digit, 32.0, jnp.where(lanes == first_digit + 1, 1.0, 0.0))
    count = jnp.sum(digits[0:1] * scale[0:1], axis=1, keepdims=True)
    place = r.places[0] + lax.broadcasted_iota(jnp.int32, (rows, 1), 0)
    weights = jnp.where((place >= r.places[3]) & (place < r.places[4]), 1.0, 0.0) / count
    head_lanes = lax.broadcasted_iota(jnp.int32, (model, 128), 1)
    head = jnp.where(head_lanes < mel, r.thin[:, THIN_HEAD:].astype(f32), 0.0).astype(bf)
    error = dot(r.a3[...], head) - r.target[...]
    weighted = weights * error
    lanes = lanes[:8]
    r.loss[...] = jnp.where(lanes == 0, jnp.sum(weighted * error), 0.0)
    dpred = (2.0 * weighted).astype(bf)
    r.g_head[...] = tdot(r.a3[...], dpred).astype(bf)
    r.dsecond[...] = rdot(dpred, head)

    zero = jnp.zeros((1, model), f32)

    def third_back(i, acc):
        here = pl.ds(pl.multiple_of(i * TILE, TILE), TILE)
        xhat, scale = norm_parts(r.second[here] + r.ffn[here])
        da = r.dsecond[here]
        dv = norm_turn(da, xhat, scale, row(4))
        r.ffn[here] = dv
        r.dffn[here] = dv.astype(bf)
        return acc[0] + fold(da * xhat), acc[1] + fold(da)

    dgain, dbias = lax.fori_loop(0, rows // TILE, third_back, (zero, zero))
    r.extra[...] = jnp.zeros_like(r.extra)
    r.extra[2:3] = dgain
    r.extra[3:4] = dbias
    got_dffn = cross(r.dffn, r.l_dffn)
    got_dhid = []
    stored = []

    def store(out, y, left, right, left_other, right_other):
        slot = len(stored) % 2
        if len(stored) >= 2:
            stored[-2].wait()

        def body(cols):
            part = tdot(left[:, cols], right[...]) + tdot(left_other[:, cols], right_other[...])
            r.stage[slot, cols] = part.astype(bf)

        by_tiles(model, COLS, body)
        copy = pltpu.make_async_copy(r.stage.at[slot], out.at[y], r.local.at[2 * nmp + len(stored)])
        copy.start()
        stored.append(copy)

    got_a2.wait_recv()
    for m in theirs + mine:
        loads[1][m].wait()

        def contract(cols):
            dact = dot(r.dffn[...], w_down[m][:, cols])
            r.dhid[m, :, cols] = (dact * r.slope[m, :, cols].astype(f32)).astype(bf)

        by_tiles(hid, COLS, contract)
        if m in theirs:
            got_dhid.append(cross(r.dhid.at[m], r.l_dhid.at[m // 2]))

        def gather_da2(cols):
            part = rdot(r.dhid[m], w_up[m][cols, :])
            r.dsecond[:, cols] = part if m == theirs[0] else r.dsecond[:, cols] + part

        by_tiles(model, COLS, gather_da2)
    got_dffn.wait_recv()
    for y in range(ny):
        got_active[y].wait_recv()
        store(r.g_down, y, r.dffn, r.active.at[2 * y], r.l_dffn, r.l_active.at[y])
    for y in range(ny):
        got_dhid[y].wait_recv()
        store(r.g_up, y, r.a2, r.dhid.at[2 * y], r.l_a2, r.l_dhid.at[y])

    def second_back(i, acc):
        here = pl.ds(pl.multiple_of(i * TILE, TILE), TILE)
        xhat, scale = norm_parts(r.second[here])
        da = r.dsecond[here]
        dsecond = r.ffn[here] + norm_turn(da, xhat, scale, row(2))
        r.dsecond[here] = dsecond
        r.dattn[here] = dsecond.astype(bf)
        return acc[0] + fold(da * xhat), acc[1] + fold(da)

    dgain, dbias = lax.fori_loop(0, rows // TILE, second_back, (zero, zero))
    r.extra[0:1] = dgain
    r.extra[1:2] = dbias
    for m in range(nmp):
        r.dmixed[m] = dot(r.dattn[...], w_out[m][...]).astype(bf)
    for copy in stored[-2:]:
        copy.wait()
    for copy in crossings:
        copy.wait_send()


def middle_all(ndp, nmp, given):
    rows, model = given.second.shape
    ny = nmp // 2
    hid = given.active.shape[2]
    c_out = given.mid.shape[2] - hid
    dma = pltpu.SemaphoreType.DMA
    anywhere = pl.BlockSpec(memory_space=pl.ANY)
    struct = jax.ShapeDtypeStruct
    outs = [
        struct((ny, model, hid), bf),
        struct((ny, model, hid), bf),
        struct((rows, model), f32),
        struct((rows, model), bf),
        struct((nmp, rows, c_out), bf),
        struct((8, model), f32),
        struct((model, 128), bf),
        struct((8, 128), f32),
    ]
    flat, tall = pltpu.VMEM((rows, model), f32), pltpu.VMEM((rows, model), bf)
    scratch = [
        flat,
        tall,
        tall,
        tall,
        pltpu.VMEM((ny, rows, hid), bf),
        pltpu.VMEM((ny, rows, hid), bf),
        pltpu.VMEM((nmp, rows, hid), bf),
        tall,
        pltpu.VMEM((2, model, hid), bf),
        pltpu.VMEM(given.mid.shape, bf),
        pltpu.VMEM(given.down.shape, bf),
        dma((8,)),
        dma((8,)),
        dma((2 * nmp + 2 * ny,)),
    ]
    outs = pl.pallas_call(
        functools.partial(middle_kernel, ndp, nmp),
        name="middle",
        out_shape=outs,
        in_specs=[SMEM] + [VMEM] * 7 + [anywhere] * 2,
        out_specs=[anywhere] * 2 + [VMEM] * 6,
        scratch_shapes=scratch,
        compiler_params=pltpu.CompilerParams(
            collective_id=2, has_side_effects=True, vmem_limit_bytes=62 << 20
        ),
    )(*given)
    return MiddleOut(*outs)


def back_kernel(ndp, nmp, *refs):
    r = BackRefs(*refs)
    wires = Wires(ndp, nmp)
    sizes = wires.sizes
    rows, model = r.dattn.shape
    ny = sizes["y"]
    seq = wires.at["c"]
    nears = [wires.near(k) for k in range(1, nmp)]
    fars = [wires.far(k) for k in range(1, ndp)]
    wires.align(r.again)
    pending = []
    size = r.places[2]

    count = iter(range(16))

    def cross(src, dst):
        i = next(count)
        copy = Crossing(src, dst, r.c_send, r.c_recv, i, wires)
        copy.make().start()
        pending.append(copy)
        return copy

    def sent(copy):
        copy.wait_send()
        pending[:] = [c for c in pending if c is not copy]

    locals_used = []

    def fetch(src, dst):
        copy = pltpu.make_async_copy(src, dst, r.local.at[len(locals_used)])
        copy.start()
        locals_used.append(copy)
        return copy

    flows = []

    def wide_flow(term, out, box, half, order):
        height = term.shape[1] // ndp // 2
        n = len(flows)

        def source(k):
            start = (k["z"] * sizes["x"] + k["x"]) * 2 * height + half * height
            return term.at[k["y"], pl.ds(start, height)]

        def landing(k):
            return box.at[slot_number(sizes, k) // sizes["c"] - 1]

        here = out.at[pl.ds(half * height, height)]
        flows.append(
            Reduce(wires, order, source, landing, here, r.send.at[n], r.recv.at[n])
        )
        return flows[-1]

    def both(term, out, *boxes):
        orders = (("y", "x", "z"), ("x", "y", "z"))
        return [wide_flow(term, out, boxes[h], h, order) for h, order in enumerate(orders)]

    def thin_source(k):
        height = r.o_thin.shape[0]
        block = (k["z"] * sizes["x"] + k["x"]) * nmp + wires.owner_mp(k["y"], k["c"])
        return r.thin.at[pl.ds(pl.multiple_of(block * height, height), height)]

    down_flows = both(r.g_down, r.o_down, r.l_down0, r.l_down1)
    up_flows = both(r.g_up, r.o_up, r.l_up0, r.l_up1)
    out_flows = both(r.g_out, r.o_out, r.l_out0, r.l_out1)
    qkv_flows = both(r.g_qkv, r.o_qkv, r.l_qkv0, r.l_qkv1)
    n = len(flows)
    thin_flow = Reduce(
        wires, ("c", "y", "x", "z"), thin_source,
        lambda k: r.l_thin.at[slot_number(sizes, k) - 1],
        r.o_thin, r.send.at[n], r.recv.at[n],
    )
    flows.append(thin_flow)
    turns = iter(BACK_TURNS)
    slots = ndp * nmp

    def turn():
        for code in next(turns):
            flow = flows[code // (2 * slots)]
            if code // slots % 2:
                flow.depart(code % slots)
            else:
                flow.arrive(code % slots)

    mine = [m for m in range(nmp) if m % 2 == 0]
    theirs = [m for m in range(nmp) if m % 2]
    for f in down_flows + up_flows:
        f.keep()
    turn()
    got_dattn = cross((r.dattn,), (r.l_dattn,))
    got_mixed = [cross((r.mixed, m), (r.l_mixed, m // 2)) for m in theirs]

    got_other = {}
    loads = {m: fetch(r.w_qkv.at[m], r.w_buf.at[m]) for m in range(2)}

    def attention(packed, other, mixed_t, dmixed, dist):
        copies = [
            fetch(src, ref)
            for src, ref in (
                (r.packed, packed), (r.other, other), (r.mixed_t, mixed_t), (r.dmixed, dmixed)
            )
        ]
        distances(dist, r.places[0], r.places[1], size)
        turn()
        got_dattn.wait_recv()
        for copy in got_mixed:
            copy.wait_recv()
        for y in range(ny):
            g = tdot(r.dattn[...], r.mixed[2 * y])
            r.g_out[y] = (g + tdot(r.l_dattn[...], r.l_mixed[y])).astype(bf)
        for f in out_flows:
            f.keep()
        for copy in copies:
            copy.wait()
        leaving = []
        for m in theirs + mine:
            slot = len(leaving) % 2
            if len(leaving) >= 2:
                sent(leaving[-2])
            for _ in attend_back(
                packed, other, dist, r.slopes, mixed_t, r.lse, dmixed,
                r.down, r.dother.at[slot], m,
            ):
                turn()
            twin = m + 1 - 2 * (m % 2)
            leaving.append(cross((r.dother, slot), (r.l_other, twin)))
            got_other[twin] = leaving[-1]

    chunks, _, width = r.packed.shape
    pl.run_scoped(
        attention,
        pltpu.VMEM(r.packed.shape, bf),
        pltpu.VMEM(r.other.shape, bf),
        pltpu.VMEM(r.mixed_t.shape, f32),
        pltpu.VMEM(r.dmixed.shape, bf),
        pltpu.VMEM((2 * rows, rows), f32),
    )

    lane = lax.broadcasted_iota(jnp.int32, (TILE, width), 1)
    is_query = lax.rem(lane, 3 * HEAD_DIM) < HEAD_DIM

    def front(first, conv, back, hm, features, dconv, gtaps):
        copies = [
            fetch(src, ref)
            for src, ref in (
                (r.first, first), (r.conv, conv), (r.dsecond, back), (r.hm, hm),
                (r.features.at[pl.ds(PAD, rows)], features),
            )
        ]
        copies[0].wait()
        gain = r.chan[KERNEL][None]
        bias = r.chan[KERNEL + 1][None]

        def act(i, _):
            here = pl.ds(pl.multiple_of(i * TILE, TILE), TILE)
            xhat, _ = norm_parts(first[here])
            r.a1[here] = (xhat * gain + bias).astype(bf)
            return 0

        lax.fori_loop(0, rows // TILE, act, 0)
        got_a1 = cross((r.a1,), (r.l_a1,))
        turn()

        def combine(m):
            got_other[m].wait_recv()

            def body(i, _):
                here = pl.ds(pl.multiple_of(i * TILE, TILE), TILE)
                own = r.down[m, here].astype(f32)
                more = own + r.l_other[m, here].astype(f32)
                r.down[m, here] = jnp.where(is_query, own, more).astype(bf)
                return 0

            lax.fori_loop(0, rows // TILE, body, 0)

        got_pack = []
        for m in theirs:
            combine(m)
            got_pack.append(cross((r.down, m), (r.l_dpack, m // 2)))
        for m in mine:
            combine(m)
        turn()
        got_a1.wait_recv()
        for y in range(ny):
            got_pack[y].wait_recv()
            g = tdot(r.a1[...], r.down[2 * y])
            r.g_qkv[y] = (g + tdot(r.l_a1[...], r.l_dpack[y])).astype(bf)
            turn()
        for f in qkv_flows:
            f.keep()
        inner = pl.ds(PAD, rows)
        for m in range(chunks):
            loads[m].wait()
            part = rdot(r.down[m], r.w_buf[m % 2])
            dconv[inner] = part if m == 0 else dconv[inner] + part
            if m + 2 < chunks:
                loads[m + 2] = fetch(r.w_qkv.at[m + 2], r.w_buf.at[m % 2])
            turn()
        for copy in copies[1:]:
            copy.wait()
        r.rows_buf[...] = jnp.zeros_like(r.rows_buf)
        r.rows_buf[KERNEL + 2 : KERNEL + 6] = r.extra[0:4]

        def norm(i, sums_in):
            here = pl.ds(pl.multiple_of(i * TILE, TILE), TILE)
            xhat, scale = norm_parts(first[here])
            shifted = pl.ds(pl.multiple_of(i * TILE + PAD, PAD), TILE)
            da = dconv[shifted]
            dx = da * gain
            dv = scale * (
                dx
                - jnp.mean(dx, axis=-1, keepdims=True)
                - xhat * jnp.mean(dx * xhat, axis=-1, keepdims=True)
            )
            dfirst = back[here] + dv
            first[here] = dfirst
            dc = dfirst * gelu_slope(conv[here])
            dconv[shifted] = dc
            return tuple(a + fold(b) for a, b in zip(sums_in, (da * xhat, da, dc)))

        zero = jnp.zeros((1, model), f32)
        dgain, dbias, dcsum = lax.fori_loop(0, rows // TILE, norm, (zero, zero, zero))
        r.rows_buf[KERNEL : KERNEL + 1] = dgain
        r.rows_buf[KERNEL + 1 : KERNEL + 2] = dbias
        r.rows_buf[KERNEL + 7 : KERNEL + 8] = dcsum
        r.edge[0] = dconv[PAD : 2 * PAD]
        r.edge[1] = dconv[rows : rows + PAD]
        got_edge = cross((r.edge,), (r.halo,))
        turn()
        got_edge.wait_recv()
        dconv[0:PAD] = jnp.where(seq == 0, 0.0, r.halo[1])
        dconv[rows + PAD :] = jnp.where(seq == 0, r.halo[0], 0.0)
        gtaps[...] = jnp.zeros_like(gtaps)
        for c in range(0, model, 128):
            convolve_back(dconv, hm, r.chan, back, gtaps, c)
            turn()

        def finish(i, acc):
            here = pl.ds(pl.multiple_of(i * TILE, TILE), TILE)
            place = r.places[0] + i * TILE + lax.broadcasted_iota(jnp.int32, (TILE, 1), 0)
            dstart = first[here] + jnp.where(place < size, back[here], 0.0)
            r.a1[here] = dstart.astype(bf)
            return acc + fold(dstart)

        sent(got_a1)
        r.rows_buf[KERNEL + 6 : KERNEL + 7] = lax.fori_loop(0, rows // TILE, finish, zero)
        for k in range(KERNEL):
            r.rows_buf[k : k + 1] = fold(gtaps[8 * k : 8 * k + 8])
        r.thin[:, :THIN_CHAN] = tdot(r.a1[...], features[...]).astype(bf)
        for i in range(0, model, 128):
            r.thin[i : i + 128, THIN_CHAN:THIN_HEAD] = r.rows_buf[:, i : i + 128].T.astype(bf)
        r.thin[:, THIN_HEAD:] = r.g_head[...]

    pl.run_scoped(
        front,
        pltpu.VMEM((rows, model), f32),
        pltpu.VMEM((rows, model), f32),
        pltpu.VMEM((rows, model), f32),
        pltpu.VMEM((rows + 2 * PAD, model), f32),
        pltpu.VMEM((rows, r.features.shape[1]), bf),
        pltpu.VMEM((rows + 2 * PAD, model), f32),
        pltpu.VMEM((8 * KERNEL, model), f32),
    )
    thin_flow.keep()
    turn()
    assert next(turns, None) is None
    for f in flows:
        f.finish()
    for copy in pending:
        copy.wait_send()

    squares = None
    for out in (r.o_thin, r.o_up, r.o_down, r.o_qkv, r.o_out):
        part = total(out)
        squares = part if squares is None else squares + part
    lanes = lax.broadcasted_iota(jnp.int32, (8, 128), 1)
    block = jnp.where(lanes == 1, squares, r.loss[...])
    parts = r.parts
    for peers, sends, recvs, lower in (
        (nears, r.near_send, r.near_recv, 0),
        (fars, r.far_send, r.far_recv, nmp),
    ):
        parts[lower] = block
        copies = []
        for i, p in enumerate(peers):
            copy = pltpu.make_async_remote_copy(
                parts.at[lower], parts.at[lower + 1 + i], sends.at[i], recvs.at[i],
                device_id=p, device_id_type=MESH,
            )
            copy.start()
            copies.append(copy)
        for copy in copies:
            copy.wait()
        for i in range(len(peers)):
            block = block + parts[lower + 1 + i]
    r.sums[...] = block


def back_all(ndp, nmp, given):
    rows, model = given.dattn.shape
    ny = nmp // 2
    width = given.packed.shape[2]
    c_out = given.mixed.shape[2]
    c_up = given.g_up.shape[2]
    height = model // ndp
    pairs = (ndp * ny - 1, height // 2)
    dma = pltpu.SemaphoreType.DMA
    wide = (c_up, given.g_down.shape[2], width, c_out)
    outs = [jax.ShapeDtypeStruct((height // nmp, THIN), f32)]
    outs += [jax.ShapeDtypeStruct((height, n), f32) for n in wide]
    outs += [jax.ShapeDtypeStruct((8, 128), f32)]
    scratch = [
        pltpu.VMEM((ny, model, width), bf),
        pltpu.VMEM((ny, model, c_out), bf),
        pltpu.VMEM((model, THIN), bf),
    ]
    for n in wide:
        scratch += [pltpu.VMEM((*pairs, n), bf)] * 2
    scratch += [
        pltpu.VMEM((ndp * nmp - 1, height // nmp, THIN), bf),
        pltpu.VMEM((nmp, rows, width), bf),
        pltpu.VMEM((2, rows, width), bf),
        pltpu.VMEM((nmp, rows, width), bf),
        pltpu.VMEM((rows, model), bf),
        pltpu.VMEM((rows, model), bf),
        pltpu.VMEM((rows, model), bf),
        pltpu.VMEM((ny, rows, c_out), bf),
        pltpu.VMEM((ny, rows, width), bf),
        pltpu.VMEM((2, PAD, model), f32),
        pltpu.VMEM((2, PAD, model), f32),
        pltpu.VMEM((nmp + ndp, 8, 128), f32),
        pltpu.VMEM((2, model, width), bf),
        pltpu.VMEM((128, model), f32),
        dma((9, ndp * nmp)),
        dma((9, ndp * nmp)),
        dma((16,)),
        dma((16,)),
        dma((16,)),
        dma((nmp - 1,)),
        dma((nmp - 1,)),
        dma((ndp - 1,)),
        dma((ndp - 1,)),
        pltpu.SemaphoreType.REGULAR,
    ]
    anywhere = pl.BlockSpec(memory_space=pl.ANY)
    specs = [SMEM] * 2 + [VMEM] * 8 + [anywhere] * 3 + [VMEM] * 1 + [anywhere] * 7
    return pl.pallas_call(
        functools.partial(back_kernel, ndp, nmp),
        name="back",
        out_shape=outs,
        in_specs=specs,
        out_specs=[VMEM] * len(outs),
        scratch_shapes=scratch,
        compiler_params=pltpu.CompilerParams(
            collective_id=1, has_side_effects=True, vmem_limit_bytes=62 << 20
        ),
    )(*given)


def step_kernel(sums, g_thin, g_qkv, g_out, g_up, g_down, *refs):
    weights, firsts, seconds = refs[:7], refs[7:14], refs[14:21]
    loss, grad_norm = refs[21:23]
    outs = refs[23:]
    norm = jnp.sqrt(sums[0:1, 1:2])
    loss[...] = sums[0:1, 0:1]
    grad_norm[...] = norm
    factor = CLIP_AT / jnp.maximum(norm, CLIP_AT)

    def update(i, here, grad):
        new = adam_update(weights[i][here], firsts[i][here], seconds[i][here], grad, factor)
        for n in range(3):
            outs[3 * i + n][here] = new[n]

    inputs, channels = weights[0].shape[1], weights[1].shape[1]
    mel = weights[6].shape[1]
    every = slice(None)
    update(0, every, g_thin[:, :THIN_CHAN][:, :inputs])
    update(1, every, g_thin[:, THIN_CHAN:THIN_HEAD][:, :channels])
    update(6, every, g_thin[:, THIN_HEAD:][:, :mel])
    for i, grad in ((2, g_qkv), (4, g_up)):
        by_tiles(grad.shape[0], 16, lambda here, i=i, grad=grad: update(i, here, grad[here]))
    for i, grad in ((3, g_out), (5, g_down)):
        by_tiles(grad.shape[1], 128, lambda here, i=i, grad=grad: update(i, here, grad[:, here].T))


def step_all(sums, grads, state):
    state = [x.T if i % 7 < 2 else x for i, x in enumerate(state)]
    one = jax.ShapeDtypeStruct((1, 1), f32)
    outs = [jax.ShapeDtypeStruct(state[i].shape, f32) for i in range(7) for _ in range(3)]
    loss, norm, *new = pl.pallas_call(
        step_kernel,
        name="step",
        out_shape=[one, one] + outs,
        in_specs=[VMEM] * 27,
        out_specs=[VMEM] * 23,
        compiler_params=pltpu.CompilerParams(vmem_limit_bytes=62 << 20),
    )(sums, *grads, *state)
    return (loss[0, 0], norm[0, 0], *[x.T for x in new[:6]], *new[6:])


def shards(
    clean_mel,
    noise_mel,
    lengths,
    span_start,
    span_end,
    phone_ids,
    flow_steps,
    in_table,
    channel_rows,
    attn_qkv,
    attn_out,
    ffn_up,
    ffn_down,
    mel_head,
    table_first,
    channel_first,
    qkv_first,
    merge_first,
    upward_first,
    downward_first,
    head_first,
    table_second,
    channel_second,
    qkv_second,
    merge_second,
    upward_second,
    downward_second,
    head_second,
):
    micro, units, length, mel = clean_mel.shape
    nmp = lax.axis_size("mp")
    seqs = nmp // micro
    rows = length // seqs
    mp = lax.axis_index("mp")
    batch = mp // seqs
    seq = mp % seqs
    base = seq * rows
    width = in_table.shape[0]
    nch = channel_rows.shape[0]

    c_qkv = attn_qkv.shape[1]
    c_out = attn_out.shape[0]
    c_up = ffn_up.shape[1]

    ndp = lax.axis_size("dp")
    spans = jnp.sum(span_end - span_start, axis=1)
    digits = jnp.stack([spans // 32, spans % 32], axis=1).reshape(1, -1)
    digits = jnp.broadcast_to(digits, (mel_head.shape[0], 2 * micro))

    def columns(x, size):
        return jnp.pad(x.astype(bf), ((0, 0), (0, size - x.shape[1])))

    thin = jnp.concatenate(
        [
            columns(in_table.T, THIN_CHAN),
            columns(channel_rows.T, THIN_HEAD - THIN_CHAN),
            columns(jnp.concatenate([mel_head, digits.astype(f32)], axis=1), THIN - THIN_HEAD),
        ],
        axis=1,
    )
    mid = jnp.concatenate([attn_out.T, ffn_up], axis=1).astype(bf)
    own = (ndp, nmp, seqs) == (8, 4, 2)
    def mine(x):
        return lax.dynamic_index_in_dim(x, batch, 0, keepdims=False)[0]

    def widen(x):
        x = jnp.pad(mine(x), [(PAD, PAD)] + [(0, 0)] * (x.ndim - 3))
        return lax.dynamic_slice_in_dim(x, base, rows + 2 * PAD, 0)

    size = mine(lengths)
    first_frame = mine(span_start)
    last_frame = mine(span_end)
    place = base - PAD + jnp.arange(rows + 2 * PAD)
    valid_ext = ((place >= 0) & (place < size)).astype(f32)[:, None]
    masked_ext = ((place >= first_frame) & (place < last_frame)).astype(f32)[:, None]
    inside = slice(PAD, PAD + rows)
    valid = valid_ext[inside]
    masked = masked_ext[inside]
    tau = mine(flow_steps).astype(f32) / TSTEPS
    clean = widen(clean_mel).astype(f32)
    noise = widen(noise_mel).astype(f32)
    noisy = (1.0 - (1.0 - SIGMA) * tau) * noise + tau * clean
    context = clean * (valid_ext * (1.0 - masked_ext))
    target = (clean - (1.0 - SIGMA) * noise)[inside]
    onehot = (widen(phone_ids)[:, None] == jnp.arange(PHONES)).astype(bf)
    features_ext = jnp.concatenate([noisy.astype(bf), context.astype(bf), onehot], axis=-1)
    features = features_ext[inside]

    wires = Wires(ndp, nmp)
    owners = [wires.owner_mp(m // 2, m % 2) if own else m for m in range(nmp)]
    owners = jnp.stack(owners) if own else jnp.arange(nmp)
    heads = (owners[:, None] * (HEADS // nmp) + jnp.arange(HEADS // nmp)).reshape(-1)
    slopes = jnp.exp2(-8.0 * (heads + 1).astype(f32) / HEADS)
    if own:
        numbers = [base, (1 - seq) * rows, size, first_frame, last_frame, batch, mel]
        places = jnp.stack([jnp.asarray(n, jnp.int32) for n in numbers])
        features_wide = columns(features_ext, THIN_CHAN)
        fore = fore_all(
            ndp,
            nmp,
            ForeIn(
                places=places,
                slopes=slopes,
                thin_own=thin,
                near_own=attn_qkv.astype(bf),
                mid_own=mid,
                down_own=ffn_down.T.astype(bf),
                features=features_wide,
            ),
        )
        thin = fore.thin
    else:
        thin = lax.all_gather(thin, ("dp", "mp"), axis=0, tiled=True)
        w_qkv = lax.all_gather(attn_qkv.astype(bf), ("mp", "dp"), axis=0, tiled=True)
        w_qkv = w_qkv.reshape(nmp, -1, c_qkv)
        rest = jnp.concatenate([mid, ffn_down.T.astype(bf)], axis=1)
        rest = lax.all_gather(rest, ("mp", "dp"), axis=0, tiled=True)
        rest = rest.reshape(nmp, -1, rest.shape[1])
        owners = jnp.arange(nmp)
    model = thin.shape[0]
    if own:
        middle = middle_all(
            ndp,
            nmp,
            MiddleIn(
                places=places,
                second=fore.second,
                a2=fore.a2,
                active=fore.active,
                slope=fore.slope,
                chan=fore.chan,
                thin=fore.thin,
                target=jnp.pad(target, ((0, 0), (0, 128 - mel))),
                mid=fore.mid,
                down=fore.down,
            ),
        )
        given = BackIn(
            places=places,
            slopes=slopes,
            loss=middle.loss,
            g_up=middle.g_up,
            g_down=middle.g_down,
            dattn=middle.dattn,
            mixed=fore.mixed,
            extra=middle.extra,
            g_head=middle.g_head,
            chan=fore.chan,
            packed=fore.packed,
            other=fore.other,
            mixed_t=fore.mixed_t,
            lse=fore.lse,
            dmixed=middle.dmixed,
            w_qkv=fore.near,
            first=fore.first,
            conv=fore.conv,
            dsecond=middle.dsecond,
            hm=fore.hm,
            features=features_wide,
        )
        g_thin, g_up, g_down, g_qkv, g_out, sums = back_all(ndp, nmp, given)
        state = (
            in_table, channel_rows, attn_qkv, attn_out, ffn_up, ffn_down, mel_head,
            table_first, channel_first, qkv_first, merge_first, upward_first, downward_first,
            head_first, table_second, channel_second, qkv_second, merge_second, upward_second,
            downward_second, head_second,
        )
        return step_all(sums, (g_thin, g_qkv, g_out, g_up, g_down), state)
    else:
        digits = thin[:, THIN_HEAD + mel : THIN_HEAD + mel + 2 * micro]
        digits = jnp.sum(digits.reshape(ndp, -1, 2 * micro)[:, 0].astype(f32), axis=0)
        count = lax.dynamic_slice_in_dim(digits, 2 * batch, 2, 0)
        count = count[0] * 32.0 + count[1]
        w_out = rest[:, :, :c_out]
        w_up = rest[:, :, c_out : c_out + c_up]
        w_down = rest[:, :, c_out + c_up :]
        w_in = thin[:, :width]
        channel = thin[:, THIN_CHAN : THIN_CHAN + nch].T.astype(f32)
        w_head = thin[:, THIN_HEAD : THIN_HEAD + mel]
        taps = channel[:KERNEL]
        vecs = channel[KERNEL:]

        start_ext = rdot(features_ext, w_in) + vecs[6]
        hm = start_ext * valid_ext
        conv = jnp.zeros((rows, model), f32) + vecs[7]
        for k in range(KERNEL):
            conv = conv + taps[k] * hm[k + 1 : k + 1 + rows]
        first = start_ext[inside] + gelu(conv)
        x_one, r_one = norm_parts(first)
        act_one = (x_one * vecs[0] + vecs[1]).astype(bf)

        groups = [[g * seqs + s for s in range(seqs)] for g in range(micro)]

        def shift(x, i):
            pairs = [(g[(s + i) % seqs], g[s]) for g in groups for s in range(seqs)]
            return lax.ppermute(x, "mp", pairs)

        def unshift(x, i):
            pairs = [(g[s], g[(s + i) % seqs]) for g in groups for s in range(seqs)]
            return lax.ppermute(x, "mp", pairs)

        packed = jnp.einsum("rd,mdc->rmc", act_one, w_qkv, preferred_element_type=f32).astype(bf)
        packed = packed.reshape(rows, HEADS, 3, HEAD_DIM)
        query, key, value = packed[:, :, 0], packed[:, :, 1], packed[:, :, 2]
        both = jnp.stack([key, value])
        both = jnp.concatenate([both] + [shift(both, i) for i in range(1, seqs)], axis=1)
        keys, values = both[0], both[1]
        blocks = (seq + jnp.arange(seqs)) % seqs
        key_place = (blocks[:, None] * rows + jnp.arange(rows)).reshape(-1)
        query_place = base + jnp.arange(rows)
        distance = jnp.abs(query_place[:, None] - key_place[None, :]).astype(f32)
        raw = jnp.einsum("qhd,khd->hqk", query, keys, preferred_element_type=f32)
        score = raw * SCALE - slopes[:, None, None] * distance
        score = jnp.where((key_place < size)[None, None, :], score, -1000000000.0)
        top = jnp.max(score, axis=-1, keepdims=True)
        prob = jnp.exp(score - top)
        prob = prob / jnp.sum(prob, axis=-1, keepdims=True)
        prob_low = prob.astype(bf)
        mixed = jnp.einsum("hqk,khd->qhd", prob_low, values, preferred_element_type=f32)
        mixed = mixed.astype(bf).reshape(rows, nmp, c_out)
        mixed = [mixed[:, m] for m in range(nmp)]
        attn = jnp.zeros((rows, model), f32)
        for m in range(nmp):
            attn = attn + rdot(mixed[m], w_out[m])
        second = first + attn

        x_two, r_two = norm_parts(second)
        act_two = (x_two * vecs[2] + vecs[3]).astype(bf)
        ffn = jnp.zeros((rows, model), f32)
        hidden = []
        active = []
        for m in range(nmp):
            hidden.append(dot(act_two, w_up[m]))
            active.append(gelu(hidden[m]).astype(bf))
            ffn = ffn + rdot(active[m], w_down[m])
        third = second + ffn

        x_three, r_three = norm_parts(third)
        act_three = (x_three * vecs[4] + vecs[5]).astype(bf)
        error = dot(act_three, w_head) - target
        weight_rows = masked / count
        loss_local = jnp.sum(weight_rows * error * error)
        dpred = (2.0 * weight_rows * error).astype(bf)
        g_head = tdot(act_three, dpred)
        dthird, dg3, db3 = norm_back(rdot(dpred, w_head), x_three, r_three, vecs[4])

        dffn = dthird.astype(bf)
        da2 = jnp.zeros((rows, model), f32)
        dhids = []
        for m in range(nmp):
            dhid = gelu_back(hidden[m], dot(dffn, w_down[m])).astype(bf)
            dhids.append(dhid)
            da2 = da2 + rdot(dhid, w_up[m])
        dnorm, dg2, db2 = norm_back(da2, x_two, r_two, vecs[2])
        dsecond = dthird + dnorm

        dattn = dsecond.astype(bf)
        g_out = [tdot(dattn, mixed[m]).astype(bf) for m in range(nmp)]
        dmixed = [dot(dattn, w_out[m]).astype(bf) for m in range(nmp)]
        dmixed = jnp.stack(dmixed, axis=1).reshape(rows, HEADS, HEAD_DIM)
        dvalues = jnp.einsum("hqk,qhd->khd", prob_low, dmixed, preferred_element_type=f32)
        dprob = jnp.einsum("qhd,khd->hqk", dmixed, values, preferred_element_type=f32)
        dscore = prob * (dprob - jnp.sum(prob * dprob, axis=-1, keepdims=True))
        draw = (dscore * SCALE).astype(bf)
        dquery = jnp.einsum("hqk,khd->qhd", draw, keys, preferred_element_type=f32)
        dkeys = jnp.einsum("hqk,qhd->khd", draw, query, preferred_element_type=f32)
        dboth = jnp.stack([dkeys, dvalues])
        parts = [dboth[:, i * rows : (i + 1) * rows] for i in range(seqs)]
        dboth = parts[0]
        for i in range(1, seqs):
            dboth = dboth + unshift(parts[i].astype(bf), i).astype(f32)
        dpacked = jnp.stack([dquery, dboth[0], dboth[1]], axis=2).astype(bf)
        dpacked = dpacked.reshape(rows, nmp, c_qkv)
        dpacked = [dpacked[:, m] for m in range(nmp)]
        g_qkv = [tdot(act_one, dpacked[m]).astype(bf) for m in range(nmp)]
        da1 = jnp.zeros((rows, model), f32)
        for m in range(nmp):
            da1 = da1 + rdot(dpacked[m], w_qkv[m])

        dnorm, dg1, db1 = norm_back(da1, x_one, r_one, vecs[0])
        dfirst = dsecond + dnorm
        dconv = gelu_back(conv, dfirst)
        right = lax.ppermute(
            dconv[:PAD], "mp", [(g[s + 1], g[s]) for g in groups for s in range(seqs - 1)]
        )
        left = lax.ppermute(
            dconv[rows - PAD :], "mp", [(g[s], g[s + 1]) for g in groups for s in range(seqs - 1)]
        )
        dconv_ext = jnp.concatenate([left, dconv, right], axis=0)
        back = jnp.zeros((rows, model), f32)
        g_taps = []
        for k in range(KERNEL):
            back = back + taps[k] * dconv_ext[2 * PAD - 1 - k : 2 * PAD - 1 - k + rows]
            g_taps.append(jnp.sum(dconv * hm[k + 1 : k + 1 + rows], axis=0))
        dstart = dfirst + valid * back
        g_in = tdot(dstart.astype(bf), features)
        g_rows = g_taps + [dg1, db1, dg2, db2, dg3, db3, jnp.sum(dstart, axis=0), jnp.sum(dconv, axis=0)]
        g_chan = jnp.stack(g_rows, axis=1)

        g_thin = jnp.concatenate(
            [
                columns(g_in, THIN_CHAN),
                columns(g_chan, THIN_HEAD - THIN_CHAN),
                columns(g_head, THIN - THIN_HEAD),
            ],
            axis=1,
        )
        g_up = [tdot(act_two, dhids[m]).astype(bf) for m in range(nmp)]
        g_down = [tdot(dffn, active[m]).astype(bf) for m in range(nmp)]
        terms = [g_thin, jnp.stack(g_up), jnp.stack(g_down), jnp.stack(g_qkv), jnp.stack(g_out)]
        g_thin = lax.psum_scatter(g_thin, ("dp", "mp"), scatter_dimension=0, tiled=True)
        sums = [g_thin.astype(f32)] + [
            lax.psum_scatter(
                t.reshape(-1, t.shape[2]), ("mp", "dp"), scatter_dimension=0, tiled=True
            ).astype(f32)
            for t in terms[1:]
        ]
        g_thin, g_up, g_down, g_qkv, g_out = sums
        squares = sum(jnp.sum(g * g) for g in sums)
        sums = lax.psum(jnp.stack([loss_local, squares])[None], ("dp", "mp"))
    sums = sums[0]
    loss = sums[0]
    grad_norm = jnp.sqrt(sums[1])
    factor = CLIP_AT / jnp.maximum(grad_norm, CLIP_AT)

    tw, tm, tv = adam_update(in_table, table_first, table_second, g_thin[:, :width].T, factor)
    cw, cm, cv = adam_update(
        channel_rows, channel_first, channel_second, g_thin[:, THIN_CHAN : THIN_CHAN + nch].T, factor
    )
    hw, hm_, hv = adam_update(mel_head, head_first, head_second, g_thin[:, THIN_HEAD : THIN_HEAD + mel], factor)
    qw, qm, qv = adam_update(attn_qkv, qkv_first, qkv_second, g_qkv, factor)
    ow, om, ov = adam_update(attn_out, merge_first, merge_second, g_out.T, factor)
    uw, um, uv = adam_update(ffn_up, upward_first, upward_second, g_up, factor)
    dw, dm, dv = adam_update(ffn_down, downward_first, downward_second, g_down.T, factor)
    return (
        loss, grad_norm,
        tw, tm, tv, cw, cm, cv, qw, qm, qv, ow, om, ov, uw, um, uv, dw, dm, dv, hw, hm_, hv,
    )


def solution(mesh):
    wide = P(None, ("dp", "mp"))
    tall = P(("dp", "mp"), None)
    down = P("dp", "mp")
    flat = P("mp", "dp")
    weights = (wide, wide, down, flat, down, flat, tall)
    pair = P(None, "dp")
    data = (P(None, "dp", None, None), P(None, "dp", None, None), pair, pair, pair)
    data = data + (P(None, "dp", None), pair)
    return jax.shard_map(
        shards,
        mesh=mesh,
        in_specs=data + weights * 3,
        out_specs=(P(), P()) + tuple(w for w in weights for _ in range(3)),
        check_vma=False,
    )
```

```python
import functools
from typing import Any, NamedTuple

import jax
import jax.numpy as jnp
from jax import lax
from jax.experimental import pallas as pl
from jax.experimental.pallas import tpu as pltpu
from jax.sharding import PartitionSpec as P

HEADS = 16
HEAD_DIM = 64
PHONES = 128
KERNEL = 31
HALF = 15
PAD = 16
TSTEPS = 1000
STEP = 10

SIGMA = 1e-05
BETA_ONE = 0.9
BETA_TWO = 0.999
EPSILON = 1e-08
DECAY = 0.01
RATE = 0.15
CLIP_AT = 0.1
NORM_EPS = 1e-05
SCALE = HEAD_DIM**-0.5
bf = jnp.bfloat16
f32 = jnp.float32


def gelu(v):
    return jax.nn.gelu(v, approximate=True)


def gelu_back(v, dv):
    return jax.vjp(gelu, v)[1](dv)[0]


def dot(left, right):
    return jnp.dot(left, right, preferred_element_type=f32)


def tdot(left, right):
    return lax.dot_general(
        left, right, (((0,), (0,)), ((), ())), preferred_element_type=f32
    )


def rdot(left, right):
    return lax.dot_general(
        left, right, (((1,), (1,)), ((), ())), preferred_element_type=f32
    )


def norm_parts(v):
    centered = v - jnp.mean(v, axis=-1, keepdims=True)
    spread = jnp.mean(centered * centered, axis=-1, keepdims=True)
    r = lax.rsqrt(spread + NORM_EPS)
    return centered * r, r


def norm_back(da, xhat, r, gain):
    dgain = jnp.sum(da * xhat, axis=0)
    dbias = jnp.sum(da, axis=0)
    dx = da * gain
    dv = r * (
        dx
        - jnp.mean(dx, axis=-1, keepdims=True)
        - xhat * jnp.mean(dx * xhat, axis=-1, keepdims=True)
    )
    return dv, dgain, dbias


def adam_update(weight, first, second, grad, factor):
    clipped = grad * factor
    first_new = BETA_ONE * first + (1.0 - BETA_ONE) * clipped
    second_new = BETA_TWO * second + (1.0 - BETA_TWO) * clipped * clipped
    first_hat = first_new / (1.0 - BETA_ONE**STEP)
    second_hat = second_new / (1.0 - BETA_TWO**STEP)
    weight_new = weight - RATE * (first_hat / (jnp.sqrt(second_hat) + EPSILON) + DECAY * weight)
    return (weight_new, first_new, second_new)


MESH = pl.DeviceIdType.MESH
AXES = ("z", "x", "y", "c")


class Wires:
    def __init__(self, ndp, nmp):
        self.sizes = {"z": ndp // 2, "x": 2, "y": nmp // 2, "c": 2}
        dp = lax.axis_index("dp")
        mp = lax.axis_index("mp")
        self.at = {"z": dp // 2, "x": dp % 2, "y": mp // 2, "c": mp % 2}

    def peer(self, axis, k):
        at = dict(self.at)
        at[axis] = lax.rem(at[axis] + k, self.sizes[axis])
        return (at["z"] * 2 + at["x"], at["y"] * 2 + at["c"])

    def owner_mp(self, ky, kc):
        ny = self.sizes["y"]
        return lax.rem(self.at["y"] + ny - ky, ny) * 2 + lax.rem(self.at["c"] + 2 - kc, 2)

    def near(self, k):
        nmp = self.sizes["y"] * self.sizes["c"]
        return (lax.axis_index("dp"), lax.rem(lax.axis_index("mp") + k, nmp))

    def far(self, k):
        ndp = self.sizes["z"] * self.sizes["x"]
        return (lax.rem(lax.axis_index("dp") + k, ndp), lax.axis_index("mp"))

    def align(self, again):
        fars = [self.far(k) for k in range(1, self.sizes["z"] * self.sizes["x"])]
        self.greet([self.near(k) for k in range(1, self.sizes["y"] * self.sizes["c"])] + fars)
        for p in fars:
            pl.semaphore_signal(again, inc=1, device_id=p, device_id_type=MESH)
        pl.semaphore_wait(again, len(fars))

    def greet(self, peers):
        barrier = pltpu.get_barrier_semaphore()
        for p in peers:
            pl.semaphore_signal(barrier, inc=1, device_id=p, device_id_type=MESH)
        pl.semaphore_wait(barrier, len(peers))


def slot_number(sizes, k):
    return ((k["z"] * sizes["x"] + k["x"]) * sizes["y"] + k["y"]) * sizes["c"] + k["c"]


def spread(sizes, order):
    slots = [(dict.fromkeys(AXES, 0), -1)]
    for stage, axis in enumerate(order):
        slots += [
            ({**k, axis: n}, stage) for n in range(1, sizes[axis]) for k, _ in list(slots)
        ]
    return slots


class Gather:
    def __init__(self, wires, order, own, slot, send, recv):
        self.wires, self.order, self.own, self.slot = wires, order, own, slot
        self.send, self.recv = send, recv
        self.slots = spread(wires.sizes, order)
        self.by_number = {slot_number(wires.sizes, k): i for i, (k, _) in enumerate(self.slots)}
        self.started = []

    def forward(self, source, k, stage):
        for later in range(stage + 1, len(self.order)):
            axis = self.order[later]
            for n in range(1, self.wires.sizes[axis]):
                there = {**k, axis: n}
                number = slot_number(self.wires.sizes, there)
                copy = pltpu.make_async_remote_copy(
                    source, self.slot(there, k), self.send.at[number], self.recv.at[number],
                    device_id=self.wires.peer(axis, n), device_id_type=MESH,
                )
                copy.start()
                self.started.append((copy, number))

    def begin(self):
        k, stage = self.slots[0]
        self.forward(self.own, k, stage)

    def arrive(self, number):
        k, stage = self.slots[self.by_number[number]]
        here = self.slot(k, k)
        pltpu.make_async_remote_copy(
            here, here, self.send.at[number], self.recv.at[number],
            device_id=self.wires.peer("c", 1), device_id_type=MESH,
        ).wait_recv()
        self.forward(here, k, stage)

    def finish(self):
        for copy, _ in self.started:
            copy.wait_send()


FIRST = ("z", "x", "y", "c")
OTHER = ("z", "y", "x", "c")


def total(ref):
    rows = 8

    def body(i, part):
        x = ref[pl.ds(i * rows, rows)]
        return part + x * x

    part = lax.fori_loop(0, ref.shape[0] // rows, body, jnp.zeros((rows, ref.shape[1]), f32))
    return jnp.sum(part)


BLOCK = 256
TILE = 64
FAR = 1e12


def distances(dist, base, other_base, size):
    rows = dist.shape[1]

    def body(i, _):
        here = pl.ds(pl.multiple_of(i * TILE, TILE), TILE)
        down = lax.broadcasted_iota(jnp.int32, (TILE, rows), 0) + i * TILE
        key = jnp.where(down < rows, base + down, other_base + down - rows)
        query = base + lax.broadcasted_iota(jnp.int32, (TILE, rows), 1)
        dist[here] = jnp.where(key < size, jnp.abs(key - query).astype(f32), FAR)
        return 0

    lax.fori_loop(0, dist.shape[0] // TILE, body, 0)


def key_blocks(packed, other, m, col):
    rows = packed.shape[1]
    twin = m + 1 - 2 * (m % 2)
    for part, (ref, index) in enumerate(((packed, m), (other, twin))):
        for start in range(0, rows, BLOCK):
            k = ref[index, start : start + BLOCK, col + HEAD_DIM : col + 2 * HEAD_DIM]
            v = ref[index, start : start + BLOCK, col + 2 * HEAD_DIM : col + 3 * HEAD_DIM]
            yield part, start, part * rows + start, k, v


def attend(packed, other, dist, slopes, mixed, mixed_t, lse, score, m):
    heads = packed.shape[2] // (3 * HEAD_DIM)
    for j in range(heads):
        col = j * 3 * HEAD_DIM
        q = packed[m, :, col : col + HEAD_DIM] * bf(SCALE)
        slope = slopes[m * heads + j]
        top = None
        for _, _, at, k, _ in key_blocks(packed, other, m, col):
            s = rdot(k, q) - slope * dist[at : at + BLOCK]
            score[at : at + BLOCK] = s
            peak = jnp.max(s, axis=0, keepdims=True)
            top = peak if top is None else jnp.maximum(top, peak)
        total_e = jnp.zeros_like(top)
        acc = None
        for _, _, at, _, v in key_blocks(packed, other, m, col):
            e = jnp.exp(score[at : at + BLOCK] - top)
            total_e = total_e + jnp.sum(e, axis=0, keepdims=True)
            part = tdot(v, e.astype(bf))
            acc = part if acc is None else acc + part
        out = acc / total_e
        row = (m * heads + j) * HEAD_DIM
        mixed_t[pl.ds(pl.multiple_of(row, HEAD_DIM), HEAD_DIM)] = out
        mixed[m, :, j * HEAD_DIM : (j + 1) * HEAD_DIM] = out.T.astype(bf)
        lse[m * heads + j] = top + jnp.log(total_e)
        yield


def attend_back(packed, other, dist, slopes, mixed_t, lse, dmixed, down, dother, m):
    heads = packed.shape[2] // (3 * HEAD_DIM)
    for j in range(heads):
        col = j * 3 * HEAD_DIM
        q = packed[m, :, col : col + HEAD_DIM] * bf(SCALE)
        slope = slopes[m * heads + j]
        row = (m * heads + j) * HEAD_DIM
        mt = mixed_t[pl.ds(pl.multiple_of(row, HEAD_DIM), HEAD_DIM)]
        dm = dmixed[m, :, j * HEAD_DIM : (j + 1) * HEAD_DIM]
        delta = jnp.sum(dm.astype(f32).T * mt, axis=0, keepdims=True)
        level = lse[m * heads + j]
        dq = None
        for part, start, at, k, v in key_blocks(packed, other, m, col):
            p = jnp.exp(rdot(k, q) - slope * dist[at : at + BLOCK] - level)
            dv = dot(p.astype(bf), dm)
            t = (p * (rdot(v, dm) - delta)).astype(bf)
            dk = dot(t, q)
            more = tdot(k, t)
            dq = more if dq is None else dq + more
            here = slice(start, start + BLOCK)
            ref = dother if part else down.at[m]
            ref[here, col + HEAD_DIM : col + 2 * HEAD_DIM] = dk.astype(ref.dtype)
            ref[here, col + 2 * HEAD_DIM : col + 3 * HEAD_DIM] = dv.astype(ref.dtype)
        down[m, :, col : col + HEAD_DIM] = (dq * SCALE).T.astype(down.dtype)
        yield


def windows(x, count):
    for j in range(8):
        moved = x if j == 0 else pltpu.roll(x, x.shape[0] - j, 0)
        for far in range(0, count + 1, 8):
            if 1 <= far + j <= count:
                yield far + j, moved[far : far + TILE]


def convolve(hm, chan, conv, column):
    lanes = slice(column, column + 128)

    def body(r, _):
        start = pl.multiple_of(r * TILE, TILE)
        x = hm[pl.ds(start, TILE + 2 * PAD), lanes]
        acc = jnp.broadcast_to(chan[KERNEL + 7, lanes][None], (TILE, 128))
        for offset, moved in windows(x, KERNEL):
            acc = acc + chan[offset - 1, lanes][None] * moved
        conv[pl.ds(start, TILE), lanes] = acc
        return 0

    lax.fori_loop(0, conv.shape[0] // TILE, body, 0)


def convolve_back(dconv, hm, chan, back, gtaps, column):
    lanes = slice(column, column + 128)

    def body(r, _):
        start = pl.multiple_of(r * TILE, TILE)
        x = dconv[pl.ds(start, TILE + 2 * PAD), lanes]
        acc = jnp.zeros((TILE, 128), f32)
        for offset, moved in windows(x, KERNEL):
            acc = acc + chan[KERNEL - offset, lanes][None] * moved
        back[pl.ds(start, TILE), lanes] = acc
        here = x[PAD : PAD + TILE]
        y = hm[pl.ds(start, TILE + 2 * PAD), lanes]
        for offset, moved in windows(y, KERNEL):
            part = here * moved
            part = sum(part[i : i + 8] for i in range(8, TILE, 8)) + part[:8]
            rows_at = slice((offset - 1) * 8, offset * 8)
            gtaps[rows_at, lanes] = gtaps[rows_at, lanes] + part
        return 0

    lax.fori_loop(0, back.shape[0] // TILE, body, 0)


VMEM = pl.BlockSpec(memory_space=pltpu.VMEM)
SMEM = pl.BlockSpec(memory_space=pltpu.SMEM)


class Reduce:
    def __init__(self, wires, order, source, landing, out, send, recv):
        self.wires, self.order, self.source, self.landing = wires, order, source, landing
        self.out, self.send, self.recv = out, send, recv
        self.where = {}
        self.started = []
        sizes = {a: wires.sizes[a] if a in order else 1 for a in AXES}
        slots = [k for k, _ in spread(sizes, order[::-1])]
        self.stages = []
        for axis in order:
            self.stages.append([k for k in slots if k[axis]])
            slots = [k for k in slots if not k[axis]]
        self.by_number = {
            self.number(k): (stage, k) for stage, ks in enumerate(self.stages) for k in ks
        }
        self.summed = set()

    def number(self, k):
        return slot_number(self.wires.sizes, k)

    def now(self, k):
        n = self.number(k)
        return self.landing(self.where[n]) if n in self.where else self.source(k)

    def leave(self, stage, k):
        axis = self.order[stage]
        n = self.wires.sizes[axis]
        number = self.number(k)
        source = self.now(k)
        pltpu.make_async_remote_copy(
            source, self.landing(k), self.send.at[number], self.recv.at[number],
            device_id=self.wires.peer(axis, (n - k[axis]) % n), device_id_type=MESH,
        ).start()
        self.started.append((k, number))

    def keep(self):
        add_rows(self.out, self.source(dict.fromkeys(AXES, 0)), None)

    def depart(self, number):
        self.leave(0, self.by_number[number][1])

    def terms(self, stage, kept):
        return {
            self.number({**kept, axis: n})
            for axis in self.order[: stage + 1]
            for n in range(1, self.wires.sizes[axis])
        }

    def arrive(self, number):
        stage, k = self.by_number[number]
        self.summed.add(number)
        here = self.landing(k)
        axis = self.order[stage]
        pltpu.make_async_remote_copy(
            here, here, self.send.at[number], self.recv.at[number],
            device_id=self.wires.peer(axis, 1), device_id_type=MESH,
        ).wait_recv()
        kept = {**k, axis: 0}
        if not any(kept.values()):
            add_rows(self.out, self.out, here)
            return
        add_rows(here, self.now(kept), here)
        self.where[self.number(kept)] = k
        last = k[axis] == self.wires.sizes[axis] - 1
        if last and stage + 1 < len(self.order) and kept[self.order[stage + 1]]:
            assert self.terms(stage, kept) <= self.summed
            self.leave(stage + 1, kept)

    def finish(self):
        for k, number in self.started:
            here = self.landing(k)
            pltpu.make_async_remote_copy(
                here, here, self.send.at[number], self.recv.at[number],
                device_id=self.wires.peer("c", 1), device_id_type=MESH,
            ).wait_send()


class Crossing:
    def __init__(self, *parts):
        self.parts = parts

    def make(self):
        (src, *s), (dst, *d), send, recv, i, wires = self.parts
        return pltpu.make_async_remote_copy(
            src.at[s[0]] if s else src, dst.at[d[0]] if d else dst, send.at[i], recv.at[i],
            device_id=wires.peer("c", 1), device_id_type=MESH,
        )

    def wait_send(self):
        self.make().wait_send()

    def wait_recv(self):
        self.make().wait_recv()


def add_rows(out, left, right):
    step = 16

    def body(i, _):
        here = pl.ds(pl.multiple_of(i * step, step), step)
        value = left[here].astype(f32)
        if right is not None:
            value = value + right[here].astype(f32)
        out[here] = value.astype(out.dtype)
        return 0

    lax.fori_loop(0, out.shape[0] // step, body, 0)


def gelu_slope(v):
    cube = 0.044715 * v * v * v
    t = jnp.tanh(0.7978845608028654 * (v + cube))
    inner = 0.7978845608028654 * (1.0 + 3.0 * 0.044715 * v * v)
    return 0.5 * (1.0 + t) + 0.5 * v * (1.0 - t * t) * inner


THIN_CHAN = 384
THIN_HEAD = 512
THIN = 640


class BackIn(NamedTuple):
    places: Any
    slopes: Any
    loss: Any
    g_up: Any
    g_down: Any
    dattn: Any
    mixed: Any
    extra: Any
    g_head: Any
    chan: Any
    packed: Any
    other: Any
    mixed_t: Any
    lse: Any
    dmixed: Any
    w_qkv: Any
    first: Any
    conv: Any
    dsecond: Any
    hm: Any
    features: Any


class BackRefs(NamedTuple):
    places: Any
    slopes: Any
    loss: Any
    g_up: Any
    g_down: Any
    dattn: Any
    mixed: Any
    extra: Any
    g_head: Any
    chan: Any
    packed: Any
    other: Any
    mixed_t: Any
    lse: Any
    dmixed: Any
    w_qkv: Any
    first: Any
    conv: Any
    dsecond: Any
    hm: Any
    features: Any
    o_thin: Any
    o_up: Any
    o_down: Any
    o_qkv: Any
    o_out: Any
    sums: Any
    g_qkv: Any
    g_out: Any
    thin: Any
    l_up0: Any
    l_up1: Any
    l_down0: Any
    l_down1: Any
    l_qkv0: Any
    l_qkv1: Any
    l_out0: Any
    l_out1: Any
    l_thin: Any
    down: Any
    dother: Any
    l_other: Any
    a1: Any
    l_a1: Any
    l_dattn: Any
    l_mixed: Any
    l_dpack: Any
    halo: Any
    edge: Any
    parts: Any
    w_buf: Any
    rows_buf: Any
    send: Any
    recv: Any
    c_send: Any
    c_recv: Any
    local: Any
    near_send: Any
    near_recv: Any
    far_send: Any
    far_recv: Any
    again: Any


COLS = 256


def by_tiles(count, size, body):
    def step(i, _):
        body(pl.ds(pl.multiple_of(i * size, size), size))
        return 0

    lax.fori_loop(0, count // size, step, 0)


def fold(x):
    return jnp.sum(x, axis=0, keepdims=True)


def norm_turn(da, xhat, scale, gain):
    dx = da * gain
    return scale * (
        dx
        - jnp.mean(dx, axis=-1, keepdims=True)
        - xhat * jnp.mean(dx * xhat, axis=-1, keepdims=True)
    )


FORE_TURNS = (
    (
        1, 8, 4, 2, 9, 16, 5, 3, 24, 17, 25, 12, 10, 6, 20, 13, 11, 28, 18, 7, 21, 26, 29, 19, 14, 27, 22,
        15, 30, 23, 31, 33, 65, 36, 34, 68, 66, 40, 48,
    ),
    (56, 72, 37, 35, 69, 67, 41, 49, 38),
    (97, 70, 129),
    (),
    (80, 42, 44),
    (),
    (88, 50),
    (52, 57, 73),
    (39,),
    (71,),
    (98,),
    (100, 81, 43, 45),
    (89, 51),
    (53, 130),
    (132, 104),
    (58, 99, 60),
    (101, 74),
    (76, 112),
    (131, 82, 84, 120, 133, 105),
    (46, 59, 92, 61),
    (75, 90),
    (77, 113),
    (
        54, 83, 85, 47, 93, 91, 55, 78, 79, 62, 63, 86, 87, 94, 95, 134, 121, 136, 108, 102, 144, 106, 152,
        116, 114, 124,
    ),
    (122,),
    (),
    (135, 137),
    (109, 103, 145, 107, 153, 117, 115, 125),
    (138, 140, 123),
    (110, 148),
    (),
    (161, 146, 156, 193),
    (139, 141, 164),
    (154, 111, 149, 168),
    (196, 118),
    (147, 157, 176, 142, 184, 165),
    (126, 155),
    (169, 150),
    (162, 197, 119),
    (177, 143, 185, 194, 158, 200),
    (127, 166, 172, 208, 151),
    (216, 163),
    (170, 180, 195, 159),
    (201, 178, 188, 167, 173),
    (),
    (209, 186, 198, 217, 171, 181, 202, 204, 179, 189),
    (174, 212, 210, 220),
    (187, 199, 203, 205, 218, 206, 182),
    (175, 213, 211, 221, 190, 214),
    (219, 207, 183, 222),
    (191, 215, 223),
)
BACK_TURNS = (
    (34, 100, 42, 108, 50, 116, 58, 124, 38, 102),
    (46, 110),
    (54, 118, 62, 126),
    (162, 228, 2, 68),
    (170, 236, 10, 76),
    (178, 244, 18, 186, 252, 84, 26, 92),
    (166, 230, 6, 70),
    (14, 78),
    (22, 86),
    (30, 94),
    (130, 174, 238, 196, 138, 204),
    (182, 246, 146, 212),
    (190, 254, 154, 220),
    (290, 356, 298, 364, 306, 372, 314, 380, 134, 294, 198, 66, 4),
    (358, 302, 366, 74, 12, 310, 374),
    (318, 382, 82, 20),
    (90, 28),
    (142, 206, 72, 150, 214),
    (),
    (8, 158, 222, 258, 324, 266, 332, 274, 340, 282, 348),
    (262,),
    (80, 132, 194, 326, 270, 334, 278, 342, 286, 350),
    (418, 484, 426, 492, 434, 500, 442, 508, 422, 486, 430, 494, 16, 202, 140, 438, 502),
    (88, 210, 446, 510, 148),
    (),
    (24, 218, 156, 322, 260, 330, 268),
    (338, 276, 346, 284, 386, 452, 200),
    (394, 460, 136),
    (402, 468),
    (410, 476),
    (390, 454, 208),
    (398, 462),
    (406, 470, 144, 414, 478),
    (),
    (216, 388, 450),
    (
        545, 553, 561, 569, 549, 557, 565, 573, 547, 555, 563, 571, 551, 559, 567, 575, 152, 328, 396, 264,
        458, 336, 404, 466, 272, 344, 412, 280, 474, 513, 521, 529, 537, 517, 525, 533, 541, 515, 523, 531,
        539, 519, 527, 535, 543, 392, 456, 514, 522, 530, 538, 518, 400, 526, 534, 516, 542, 524, 532, 540,
        464, 408, 472, 520, 528, 536,
    ),
)


class ForeIn(NamedTuple):
    places: Any
    slopes: Any
    thin_own: Any
    near_own: Any
    mid_own: Any
    down_own: Any
    features: Any


class ForeOut(NamedTuple):
    thin: Any
    near: Any
    mid: Any
    down: Any
    hm: Any
    conv: Any
    first: Any
    packed: Any
    other: Any
    mixed: Any
    mixed_t: Any
    lse: Any
    chan: Any
    second: Any
    a2: Any
    active: Any
    slope: Any


class ForeRefs(NamedTuple):
    places: Any
    slopes: Any
    thin_own: Any
    near_own: Any
    mid_own: Any
    down_own: Any
    features: Any
    o_thin: Any
    o_near: Any
    mid: Any
    down: Any
    o_hm: Any
    o_conv: Any
    o_first: Any
    o_packed: Any
    o_other: Any
    o_mixed: Any
    o_mixed_t: Any
    o_lse: Any
    o_chan: Any
    o_second: Any
    o_a2: Any
    o_active: Any
    o_slope: Any
    thin: Any
    near: Any
    hm: Any
    conv: Any
    first: Any
    packed: Any
    other: Any
    mixed: Any
    mixed_t: Any
    lse: Any
    chan: Any
    second: Any
    a2: Any
    active: Any
    slope: Any
    a1: Any
    dist: Any
    score: Any
    w: Any
    send: Any
    recv: Any
    local: Any
    c_send: Any
    c_recv: Any
    again: Any


def fore_kernel(ndp, nmp, *refs):
    r = ForeRefs(*refs)
    wires = Wires(ndp, nmp)
    wires.align(r.again)
    sizes = wires.sizes
    thin_rows = r.thin_own.shape[0]
    rows, model = r.first.shape
    size = r.places[2]

    def thin_slot(k, sent):
        block = (k["z"] * sizes["x"] + k["x"]) * nmp + wires.owner_mp(sent["y"], sent["c"])
        return r.thin.at[pl.ds(pl.multiple_of(block * thin_rows, thin_rows), thin_rows)]

    flows = [Gather(wires, FIRST, r.thin_own, thin_slot, r.send.at[0], r.recv.at[0])]

    def wide_flow(own, out, half, order):
        height = own.shape[0] // 2

        def slot(k, sent):
            start = (k["z"] * sizes["x"] + k["x"]) * 2 * height + half * height
            return out.at[k["y"] * sizes["c"] + k["c"], pl.ds(start, height)]

        n = len(flows)
        part = own.at[pl.ds(half * height, height)]
        flows.append(Gather(wires, order, part, slot, r.send.at[n], r.recv.at[n]))
        return flows[-1]

    near = [wide_flow(r.near_own, r.near, h, o) for h, o in enumerate((FIRST, OTHER))]
    mid = [wide_flow(r.mid_own, r.mid, h, o) for h, o in enumerate((FIRST, OTHER))]
    down = [wide_flow(r.down_own, r.down, h, o) for h, o in enumerate((FIRST, OTHER))]
    zero = dict.fromkeys(AXES, 0)
    kept = [
        pltpu.make_async_copy(f.own, f.slot(zero, zero), r.local.at[i])
        for i, f in enumerate(flows)
    ]
    for copy in kept:
        copy.start()
    for f in flows[:1] + near:
        f.begin()
    turns = iter(FORE_TURNS)
    slots = ndp * nmp
    saves = []

    def save(src, dst):
        copy = pltpu.make_async_copy(src, dst, r.local.at[len(flows) + nmp + len(saves)])
        copy.start()
        saves.append(copy)

    def turn():
        for code in next(turns):
            flows[code // slots].arrive(code % slots)

    turn()
    for f in mid:
        f.begin()
    for copy in kept:
        copy.wait()

    for i in range(0, model, 128):
        cols = r.thin[i : i + 128, THIN_CHAN:THIN_HEAD].astype(f32)
        r.chan[:, i : i + 128] = cols.T
    save(r.chan, r.o_chan)
    save(r.thin, r.o_thin)
    distances(r.dist, r.places[0], r.places[1], size)
    turn()

    for column in range(0, model, 128):
        cols = slice(column, column + 128)
        h = rdot(r.features[...], r.thin[cols, :THIN_CHAN])
        h = h + r.chan[KERNEL + 6, cols][None]
        place = r.places[0] - PAD + lax.broadcasted_iota(jnp.int32, (h.shape[0], 1), 0)
        r.first[:, cols] = h[PAD : PAD + rows]
        r.hm[:, cols] = jnp.where((place >= 0) & (place < size), h, 0.0)
        turn()
    for c in range(0, model, 128):
        convolve(r.hm, r.chan, r.conv, c)
        turn()

    def norm(i, _):
        here = pl.ds(pl.multiple_of(i * TILE, TILE), TILE)
        v = r.conv[here]
        inner = 0.7978845608028654 * v * (1.0 + 0.044715 * v * v)
        first = r.first[here] + v * (0.5 + 0.5 * jnp.tanh(inner))
        r.first[here] = first
        xhat, _ = norm_parts(first)
        r.a1[here] = (xhat * r.chan[KERNEL][None] + r.chan[KERNEL + 1][None]).astype(bf)

        return 0

    save(r.hm, r.o_hm)
    save(r.conv, r.o_conv)
    for i in range(0, rows // TILE, 2):
        lax.fori_loop(i, i + 2, norm, 0)
        turn()
    save(r.first, r.o_first)
    turn()
    crossings = []
    width = r.packed.shape[2]
    for m in range(nmp):
        def expand(cols):
            r.packed[m, :, cols] = dot(r.a1[...], r.near[m, :, cols]).astype(bf)

        by_tiles(width, COLS, expand)
        copy = pltpu.make_async_remote_copy(
            r.packed.at[m], r.other.at[m], r.c_send.at[m], r.c_recv.at[m],
            device_id=wires.peer("c", 1), device_id_type=MESH,
        )
        copy.start()
        crossings.append(copy)
        turn()
    for f in down:
        f.begin()
    save(r.near, r.o_near)
    save(r.packed, r.o_packed)
    for m in range(nmp):
        crossings[m + 1 - 2 * (m % 2)].wait_recv()
        for _ in attend(
            r.packed, r.other, r.dist, r.slopes, r.mixed, r.mixed_t, r.lse,
            r.score, m,
        ):
            turn()
    turn()
    for src, dst in (
        (r.other, r.o_other), (r.mixed, r.o_mixed), (r.mixed_t, r.o_mixed_t), (r.lse, r.o_lse)
    ):
        save(src, dst)
    loads = [
        pltpu.make_async_copy(r.mid.at[m], r.w.at[m], r.local.at[len(flows) + m])
        for m in range(nmp)
    ]
    for copy in loads:
        copy.start()
    c_out = r.mixed.shape[2]
    hid = r.active.shape[2]
    w_out = [r.w.at[m, :, pl.ds(0, c_out)] for m in range(nmp)]
    w_up = [r.w.at[m, :, pl.ds(c_out, hid)] for m in range(nmp)]
    for copy in loads:
        copy.wait()

    def project(cols):
        acc = r.first[:, cols]
        for m in range(nmp):
            acc = acc + rdot(r.mixed[m], w_out[m][cols, :])
        r.second[:, cols] = acc

    by_tiles(model, COLS, project)

    def second_norm(here):
        xhat, _ = norm_parts(r.second[here])
        gain, bias = r.chan[KERNEL + 2][None], r.chan[KERNEL + 3][None]
        r.a2[here] = (xhat * gain + bias).astype(bf)

    by_tiles(rows, TILE, second_norm)
    save(r.second, r.o_second)
    save(r.a2, r.o_a2)
    turn()
    for m in range(nmp):

        def gelu_pair(v, cols):
            square = v * v
            t = jnp.tanh(0.7978845608028654 * v * (1.0 + 0.044715 * square))
            half = 0.5 + 0.5 * t
            r.active[m, :, cols] = (v * half).astype(bf)
            inner = 0.3989422804014327 * (1.0 + 0.134145 * square)
            r.slope[m, :, cols] = (half + v * (1.0 - t * t) * inner).astype(bf)

        def expand(i, _):
            cols = [pl.ds(pl.multiple_of((2 * i + n) * COLS, COLS), COLS) for n in range(2)]
            values = [dot(r.a2[...], w_up[m][:, c]) for c in cols]
            for v, c in zip(values, cols):
                gelu_pair(v, c)
            return 0

        lax.fori_loop(0, hid // COLS // 2, expand, 0)
        save(r.active.at[m], r.o_active.at[m])
        save(r.slope.at[m], r.o_slope.at[m])
        turn()
    turn()
    assert next(turns, None) is None
    for copy in saves:
        copy.wait()
    for f in flows:
        f.finish()
    for copy in crossings:
        copy.wait_send()


def fore_all(ndp, nmp, given):
    model = given.near_own.shape[0] * ndp
    width = given.near_own.shape[1]
    hid = given.down_own.shape[1]
    wide = HEADS * HEAD_DIM
    rows = given.features.shape[0] - 2 * PAD
    struct = jax.ShapeDtypeStruct
    dma = pltpu.SemaphoreType.DMA
    anywhere = pl.BlockSpec(memory_space=pl.ANY)
    outs = [
        struct((model, THIN), bf),
        struct((nmp, model, width), bf),
        struct((nmp, model, given.mid_own.shape[1]), bf),
        struct((nmp, model, hid), bf),
        struct((rows + 2 * PAD, model), f32),
        struct((rows, model), f32),
        struct((rows, model), f32),
        struct((nmp, rows, width), bf),
        struct((nmp, rows, width), bf),
        struct((nmp, rows, wide // nmp), bf),
        struct((wide, rows), f32),
        struct((HEADS, 1, rows), f32),
        struct((128, model), f32),
        struct((rows, model), f32),
        struct((rows, model), bf),
        struct((nmp, rows, hid), bf),
        struct((nmp, rows, hid), bf),
    ]
    outs = pl.pallas_call(
        functools.partial(fore_kernel, ndp, nmp),
        name="fore",
        out_shape=outs,
        in_specs=[SMEM] * 2 + [anywhere] * 4 + [VMEM],
        out_specs=[anywhere] * len(outs),
        scratch_shapes=[pltpu.VMEM(o.shape, o.dtype) for o in outs[:2] + outs[4:]]
        + [
            pltpu.VMEM((rows, model), bf),
            pltpu.VMEM((2 * rows, rows), f32),
            pltpu.VMEM((2 * rows, rows), f32),
            pltpu.VMEM((nmp, model, given.mid_own.shape[1]), bf),
            dma((7, ndp * nmp)),
            dma((7, ndp * nmp)),
            dma((7 + nmp + 13 + 2 * nmp,)),
            dma((nmp,)),
            dma((nmp,)),
            pltpu.SemaphoreType.REGULAR,
        ],
        compiler_params=pltpu.CompilerParams(
            collective_id=0, has_side_effects=True, vmem_limit_bytes=62 << 20
        ),
    )(*given)
    return ForeOut(*outs)


class MiddleIn(NamedTuple):
    places: Any
    second: Any
    a2: Any
    active: Any
    slope: Any
    chan: Any
    thin: Any
    target: Any
    mid: Any
    down: Any


class MiddleOut(NamedTuple):
    g_up: Any
    g_down: Any
    dsecond: Any
    dattn: Any
    dmixed: Any
    extra: Any
    g_head: Any
    loss: Any


class MiddleRefs(NamedTuple):
    places: Any
    second: Any
    a2: Any
    active: Any
    slope: Any
    chan: Any
    thin: Any
    target: Any
    mid: Any
    down: Any
    g_up: Any
    g_down: Any
    dsecond: Any
    dattn: Any
    dmixed: Any
    extra: Any
    g_head: Any
    loss: Any
    ffn: Any
    l_a2: Any
    dffn: Any
    l_dffn: Any
    l_active: Any
    l_dhid: Any
    dhid: Any
    a3: Any
    stage: Any
    w: Any
    w_down: Any
    c_send: Any
    c_recv: Any
    local: Any


def middle_kernel(ndp, nmp, *refs):
    r = MiddleRefs(*refs)
    wires = Wires(ndp, nmp)
    partner = wires.peer("c", 1)
    wires.greet([partner])
    rows, model = r.second.shape
    ny = nmp // 2
    theirs = list(range(1, nmp, 2))
    mine = list(range(0, nmp, 2))
    hid = r.active.shape[2]
    c_out = r.mid.shape[2] - hid
    w_out = [r.w.at[m, :, pl.ds(0, c_out)] for m in range(nmp)]
    w_up = [r.w.at[m, :, pl.ds(c_out, hid)] for m in range(nmp)]
    loads = [
        [
            pltpu.make_async_copy(src.at[m], dst.at[m], r.local.at[i * nmp + m])
            for m in range(nmp)
        ]
        for i, (src, dst) in enumerate(((r.down, r.w_down), (r.mid, r.w)))
    ]
    for group in loads:
        for m in theirs + mine:
            group[m].start()
    w_down = [r.w_down.at[m] for m in range(nmp)]
    crossings = []

    def cross(src, dst):
        i = len(crossings)
        copy = pltpu.make_async_remote_copy(
            src, dst, r.c_send.at[i], r.c_recv.at[i],
            device_id=partner, device_id_type=MESH,
        )
        copy.start()
        crossings.append(copy)
        return copy

    def row(i):
        return r.chan[KERNEL + i][None]

    got_a2 = cross(r.a2, r.l_a2)
    got_active = [cross(r.active.at[m], r.l_active.at[m // 2]) for m in theirs]
    for m in theirs + mine:
        loads[0][m].wait()

        def shrink(cols):
            part = rdot(r.active[m], w_down[m][cols, :])
            r.ffn[:, cols] = part if m == theirs[0] else r.ffn[:, cols] + part

        by_tiles(model, 4 * COLS, shrink)

    def third_norm(here):
        xhat, _ = norm_parts(r.second[here] + r.ffn[here])
        r.a3[here] = (xhat * row(4) + row(5)).astype(bf)

    by_tiles(rows, TILE, third_norm)
    mel = r.places[6]
    lanes = lax.broadcasted_iota(jnp.int32, (16, 128), 1)
    digits = jnp.zeros((16, 128), f32)
    for d in range(ndp):
        start = d * (model // ndp)
        digits = digits + r.thin[start : start + 16, THIN_HEAD:].astype(f32)
    first_digit = mel + 2 * r.places[5]
    scale = jnp.where(lanes == first_digit, 32.0, jnp.where(lanes == first_digit + 1, 1.0, 0.0))
    count = jnp.sum(digits[0:1] * scale[0:1], axis=1, keepdims=True)
    place = r.places[0] + lax.broadcasted_iota(jnp.int32, (rows, 1), 0)
    weights = jnp.where((place >= r.places[3]) & (place < r.places[4]), 1.0, 0.0) / count
    head_lanes = lax.broadcasted_iota(jnp.int32, (model, 128), 1)
    head = jnp.where(head_lanes < mel, r.thin[:, THIN_HEAD:].astype(f32), 0.0).astype(bf)
    error = dot(r.a3[...], head) - r.target[...]
    weighted = weights * error
    lanes = lanes[:8]
    r.loss[...] = jnp.where(lanes == 0, jnp.sum(weighted * error), 0.0)
    dpred = (2.0 * weighted).astype(bf)
    r.g_head[...] = tdot(r.a3[...], dpred).astype(bf)
    r.dsecond[...] = rdot(dpred, head)

    zero = jnp.zeros((1, model), f32)

    def third_back(i, acc):
        here = pl.ds(pl.multiple_of(i * TILE, TILE), TILE)
        xhat, scale = norm_parts(r.second[here] + r.ffn[here])
        da = r.dsecond[here]
        dv = norm_turn(da, xhat, scale, row(4))
        r.ffn[here] = dv
        r.dffn[here] = dv.astype(bf)
        return acc[0] + fold(da * xhat), acc[1] + fold(da)

    dgain, dbias = lax.fori_loop(0, rows // TILE, third_back, (zero, zero))
    r.extra[...] = jnp.zeros_like(r.extra)
    r.extra[2:3] = dgain
    r.extra[3:4] = dbias
    got_dffn = cross(r.dffn, r.l_dffn)
    got_dhid = []
    stored = []

    def store(out, y, left, right, left_other, right_other):
        slot = len(stored) % 2
        if len(stored) >= 2:
            stored[-2].wait()

        def body(cols):
            part = tdot(left[:, cols], right[...]) + tdot(left_other[:, cols], right_other[...])
            r.stage[slot, cols] = part.astype(bf)

        by_tiles(model, 4 * COLS, body)
        copy = pltpu.make_async_copy(r.stage.at[slot], out.at[y], r.local.at[2 * nmp + len(stored)])
        copy.start()
        stored.append(copy)

    got_a2.wait_recv()
    for m in theirs + mine:
        loads[1][m].wait()

        def contract(cols):
            dact = dot(r.dffn[...], w_down[m][:, cols])
            r.dhid[m, :, cols] = (dact * r.slope[m, :, cols].astype(f32)).astype(bf)

        by_tiles(hid, 4 * COLS, contract)
        if m in theirs:
            got_dhid.append(cross(r.dhid.at[m], r.l_dhid.at[m // 2]))

        def gather_da2(cols):
            part = rdot(r.dhid[m], w_up[m][cols, :])
            r.dsecond[:, cols] = part if m == theirs[0] else r.dsecond[:, cols] + part

        by_tiles(model, 4 * COLS, gather_da2)
    got_dffn.wait_recv()
    for y in range(ny):
        got_active[y].wait_recv()
        store(r.g_down, y, r.dffn, r.active.at[2 * y], r.l_dffn, r.l_active.at[y])
    for y in range(ny):
        got_dhid[y].wait_recv()
        store(r.g_up, y, r.a2, r.dhid.at[2 * y], r.l_a2, r.l_dhid.at[y])

    def second_back(i, acc):
        here = pl.ds(pl.multiple_of(i * TILE, TILE), TILE)
        xhat, scale = norm_parts(r.second[here])
        da = r.dsecond[here]
        dsecond = r.ffn[here] + norm_turn(da, xhat, scale, row(2))
        r.dsecond[here] = dsecond
        r.dattn[here] = dsecond.astype(bf)
        return acc[0] + fold(da * xhat), acc[1] + fold(da)

    dgain, dbias = lax.fori_loop(0, rows // TILE, second_back, (zero, zero))
    r.extra[0:1] = dgain
    r.extra[1:2] = dbias
    for m in range(nmp):
        r.dmixed[m] = dot(r.dattn[...], w_out[m][...]).astype(bf)
    for copy in stored[-2:]:
        copy.wait()
    for copy in crossings:
        copy.wait_send()


def middle_all(ndp, nmp, given):
    rows, model = given.second.shape
    ny = nmp // 2
    hid = given.active.shape[2]
    c_out = given.mid.shape[2] - hid
    dma = pltpu.SemaphoreType.DMA
    anywhere = pl.BlockSpec(memory_space=pl.ANY)
    struct = jax.ShapeDtypeStruct
    outs = [
        struct((ny, model, hid), bf),
        struct((ny, model, hid), bf),
        struct((rows, model), f32),
        struct((rows, model), bf),
        struct((nmp, rows, c_out), bf),
        struct((8, model), f32),
        struct((model, 128), bf),
        struct((8, 128), f32),
    ]
    flat, tall = pltpu.VMEM((rows, model), f32), pltpu.VMEM((rows, model), bf)
    scratch = [
        flat,
        tall,
        tall,
        tall,
        pltpu.VMEM((ny, rows, hid), bf),
        pltpu.VMEM((ny, rows, hid), bf),
        pltpu.VMEM((nmp, rows, hid), bf),
        tall,
        pltpu.VMEM((2, model, hid), bf),
        pltpu.VMEM(given.mid.shape, bf),
        pltpu.VMEM(given.down.shape, bf),
        dma((8,)),
        dma((8,)),
        dma((2 * nmp + 2 * ny,)),
    ]
    outs = pl.pallas_call(
        functools.partial(middle_kernel, ndp, nmp),
        name="middle",
        out_shape=outs,
        in_specs=[SMEM] + [VMEM] * 7 + [anywhere] * 2,
        out_specs=[anywhere] * 2 + [VMEM] * 6,
        scratch_shapes=scratch,
        compiler_params=pltpu.CompilerParams(
            collective_id=2, has_side_effects=True, vmem_limit_bytes=62 << 20
        ),
    )(*given)
    return MiddleOut(*outs)


def back_kernel(ndp, nmp, *refs):
    r = BackRefs(*refs)
    wires = Wires(ndp, nmp)
    sizes = wires.sizes
    rows, model = r.dattn.shape
    ny = sizes["y"]
    seq = wires.at["c"]
    nears = [wires.near(k) for k in range(1, nmp)]
    fars = [wires.far(k) for k in range(1, ndp)]
    wires.align(r.again)
    pending = []
    size = r.places[2]

    count = iter(range(16))

    def cross(src, dst):
        i = next(count)
        copy = Crossing(src, dst, r.c_send, r.c_recv, i, wires)
        copy.make().start()
        pending.append(copy)
        return copy

    def sent(copy):
        copy.wait_send()
        pending[:] = [c for c in pending if c is not copy]

    locals_used = []

    def fetch(src, dst):
        copy = pltpu.make_async_copy(src, dst, r.local.at[len(locals_used)])
        copy.start()
        locals_used.append(copy)
        return copy

    flows = []

    def wide_flow(term, out, box, half, order):
        height = term.shape[1] // ndp // 2
        n = len(flows)

        def source(k):
            start = (k["z"] * sizes["x"] + k["x"]) * 2 * height + half * height
            return term.at[k["y"], pl.ds(start, height)]

        def landing(k):
            return box.at[slot_number(sizes, k) // sizes["c"] - 1]

        here = out.at[pl.ds(half * height, height)]
        flows.append(
            Reduce(wires, order, source, landing, here, r.send.at[n], r.recv.at[n])
        )
        return flows[-1]

    def both(term, out, *boxes):
        orders = (("y", "x", "z"), ("x", "y", "z"))
        return [wide_flow(term, out, boxes[h], h, order) for h, order in enumerate(orders)]

    def thin_source(k):
        height = r.o_thin.shape[0]
        block = (k["z"] * sizes["x"] + k["x"]) * nmp + wires.owner_mp(k["y"], k["c"])
        return r.thin.at[pl.ds(pl.multiple_of(block * height, height), height)]

    down_flows = both(r.g_down, r.o_down, r.l_down0, r.l_down1)
    up_flows = both(r.g_up, r.o_up, r.l_up0, r.l_up1)
    out_flows = both(r.g_out, r.o_out, r.l_out0, r.l_out1)
    qkv_flows = both(r.g_qkv, r.o_qkv, r.l_qkv0, r.l_qkv1)
    n = len(flows)
    thin_flow = Reduce(
        wires, ("c", "y", "x", "z"), thin_source,
        lambda k: r.l_thin.at[slot_number(sizes, k) - 1],
        r.o_thin, r.send.at[n], r.recv.at[n],
    )
    flows.append(thin_flow)
    turns = iter(BACK_TURNS)
    slots = ndp * nmp

    def turn():
        for code in next(turns):
            flow = flows[code // (2 * slots)]
            if code // slots % 2:
                flow.depart(code % slots)
            else:
                flow.arrive(code % slots)

    mine = [m for m in range(nmp) if m % 2 == 0]
    theirs = [m for m in range(nmp) if m % 2]
    for f in down_flows + up_flows:
        f.keep()
    turn()
    got_dattn = cross((r.dattn,), (r.l_dattn,))
    got_mixed = [cross((r.mixed, m), (r.l_mixed, m // 2)) for m in theirs]

    got_other = {}
    loads = {m: fetch(r.w_qkv.at[m], r.w_buf.at[m]) for m in range(2)}

    def attention(packed, other, mixed_t, dmixed, dist):
        copies = [
            fetch(src, ref)
            for src, ref in (
                (r.packed, packed), (r.other, other), (r.mixed_t, mixed_t), (r.dmixed, dmixed)
            )
        ]
        distances(dist, r.places[0], r.places[1], size)
        turn()
        got_dattn.wait_recv()
        for copy in got_mixed:
            copy.wait_recv()
        for y in range(ny):
            g = tdot(r.dattn[...], r.mixed[2 * y])
            r.g_out[y] = (g + tdot(r.l_dattn[...], r.l_mixed[y])).astype(bf)
        for f in out_flows:
            f.keep()
        for copy in copies:
            copy.wait()
        leaving = []
        for m in theirs + mine:
            slot = len(leaving) % 2
            if len(leaving) >= 2:
                sent(leaving[-2])
            for _ in attend_back(
                packed, other, dist, r.slopes, mixed_t, r.lse, dmixed,
                r.down, r.dother.at[slot], m,
            ):
                turn()
            twin = m + 1 - 2 * (m % 2)
            leaving.append(cross((r.dother, slot), (r.l_other, twin)))
            got_other[twin] = leaving[-1]

    chunks, _, width = r.packed.shape
    pl.run_scoped(
        attention,
        pltpu.VMEM(r.packed.shape, bf),
        pltpu.VMEM(r.other.shape, bf),
        pltpu.VMEM(r.mixed_t.shape, f32),
        pltpu.VMEM(r.dmixed.shape, bf),
        pltpu.VMEM((2 * rows, rows), f32),
    )

    lane = lax.broadcasted_iota(jnp.int32, (TILE, width), 1)
    is_query = lax.rem(lane, 3 * HEAD_DIM) < HEAD_DIM

    def front(first, conv, back, hm, features, dconv, gtaps):
        copies = [
            fetch(src, ref)
            for src, ref in (
                (r.first, first), (r.conv, conv), (r.dsecond, back), (r.hm, hm),
                (r.features.at[pl.ds(PAD, rows)], features),
            )
        ]
        copies[0].wait()
        gain = r.chan[KERNEL][None]
        bias = r.chan[KERNEL + 1][None]

        def act(i, _):
            here = pl.ds(pl.multiple_of(i * TILE, TILE), TILE)
            xhat, _ = norm_parts(first[here])
            r.a1[here] = (xhat * gain + bias).astype(bf)
            return 0

        lax.fori_loop(0, rows // TILE, act, 0)
        got_a1 = cross((r.a1,), (r.l_a1,))
        turn()

        def combine(m):
            got_other[m].wait_recv()

            def body(i, _):
                here = pl.ds(pl.multiple_of(i * TILE, TILE), TILE)
                own = r.down[m, here].astype(f32)
                more = own + r.l_other[m, here].astype(f32)
                r.down[m, here] = jnp.where(is_query, own, more).astype(bf)
                return 0

            lax.fori_loop(0, rows // TILE, body, 0)

        got_pack = []
        for m in theirs:
            combine(m)
            got_pack.append(cross((r.down, m), (r.l_dpack, m // 2)))
        for m in mine:
            combine(m)
        turn()
        got_a1.wait_recv()
        for y in range(ny):
            got_pack[y].wait_recv()
            g = tdot(r.a1[...], r.down[2 * y])
            r.g_qkv[y] = (g + tdot(r.l_a1[...], r.l_dpack[y])).astype(bf)
            turn()
        for f in qkv_flows:
            f.keep()
        inner = pl.ds(PAD, rows)
        for m in range(chunks):
            loads[m].wait()
            part = rdot(r.down[m], r.w_buf[m % 2])
            dconv[inner] = part if m == 0 else dconv[inner] + part
            if m + 2 < chunks:
                loads[m + 2] = fetch(r.w_qkv.at[m + 2], r.w_buf.at[m % 2])
            turn()
        for copy in copies[1:]:
            copy.wait()
        r.rows_buf[...] = jnp.zeros_like(r.rows_buf)
        r.rows_buf[KERNEL + 2 : KERNEL + 6] = r.extra[0:4]

        def norm(i, sums_in):
            here = pl.ds(pl.multiple_of(i * TILE, TILE), TILE)
            xhat, scale = norm_parts(first[here])
            shifted = pl.ds(pl.multiple_of(i * TILE + PAD, PAD), TILE)
            da = dconv[shifted]
            dx = da * gain
            dv = scale * (
                dx
                - jnp.mean(dx, axis=-1, keepdims=True)
                - xhat * jnp.mean(dx * xhat, axis=-1, keepdims=True)
            )
            dfirst = back[here] + dv
            first[here] = dfirst
            dc = dfirst * gelu_slope(conv[here])
            dconv[shifted] = dc
            return tuple(a + fold(b) for a, b in zip(sums_in, (da * xhat, da, dc)))

        zero = jnp.zeros((1, model), f32)
        dgain, dbias, dcsum = lax.fori_loop(0, rows // TILE, norm, (zero, zero, zero))
        r.rows_buf[KERNEL : KERNEL + 1] = dgain
        r.rows_buf[KERNEL + 1 : KERNEL + 2] = dbias
        r.rows_buf[KERNEL + 7 : KERNEL + 8] = dcsum
        r.edge[0] = dconv[PAD : 2 * PAD]
        r.edge[1] = dconv[rows : rows + PAD]
        got_edge = cross((r.edge,), (r.halo,))
        turn()
        got_edge.wait_recv()
        dconv[0:PAD] = jnp.where(seq == 0, 0.0, r.halo[1])
        dconv[rows + PAD :] = jnp.where(seq == 0, r.halo[0], 0.0)
        gtaps[...] = jnp.zeros_like(gtaps)
        for c in range(0, model, 128):
            convolve_back(dconv, hm, r.chan, back, gtaps, c)
            turn()

        def finish(i, acc):
            here = pl.ds(pl.multiple_of(i * TILE, TILE), TILE)
            place = r.places[0] + i * TILE + lax.broadcasted_iota(jnp.int32, (TILE, 1), 0)
            dstart = first[here] + jnp.where(place < size, back[here], 0.0)
            r.a1[here] = dstart.astype(bf)
            return acc + fold(dstart)

        sent(got_a1)
        r.rows_buf[KERNEL + 6 : KERNEL + 7] = lax.fori_loop(0, rows // TILE, finish, zero)
        for k in range(KERNEL):
            r.rows_buf[k : k + 1] = fold(gtaps[8 * k : 8 * k + 8])
        r.thin[:, :THIN_CHAN] = tdot(r.a1[...], features[...]).astype(bf)
        for i in range(0, model, 128):
            r.thin[i : i + 128, THIN_CHAN:THIN_HEAD] = r.rows_buf[:, i : i + 128].T.astype(bf)
        r.thin[:, THIN_HEAD:] = r.g_head[...]

    pl.run_scoped(
        front,
        pltpu.VMEM((rows, model), f32),
        pltpu.VMEM((rows, model), f32),
        pltpu.VMEM((rows, model), f32),
        pltpu.VMEM((rows + 2 * PAD, model), f32),
        pltpu.VMEM((rows, r.features.shape[1]), bf),
        pltpu.VMEM((rows + 2 * PAD, model), f32),
        pltpu.VMEM((8 * KERNEL, model), f32),
    )
    thin_flow.keep()
    turn()
    assert next(turns, None) is None
    for f in flows:
        f.finish()
    for copy in pending:
        copy.wait_send()

    squares = None
    for out in (r.o_thin, r.o_up, r.o_down, r.o_qkv, r.o_out):
        part = total(out)
        squares = part if squares is None else squares + part
    lanes = lax.broadcasted_iota(jnp.int32, (8, 128), 1)
    block = jnp.where(lanes == 1, squares, r.loss[...])
    parts = r.parts
    for peers, sends, recvs, lower in (
        (nears, r.near_send, r.near_recv, 0),
        (fars, r.far_send, r.far_recv, nmp),
    ):
        parts[lower] = block
        copies = []
        for i, p in enumerate(peers):
            copy = pltpu.make_async_remote_copy(
                parts.at[lower], parts.at[lower + 1 + i], sends.at[i], recvs.at[i],
                device_id=p, device_id_type=MESH,
            )
            copy.start()
            copies.append(copy)
        for copy in copies:
            copy.wait()
        for i in range(len(peers)):
            block = block + parts[lower + 1 + i]
    r.sums[...] = block


def back_all(ndp, nmp, given):
    rows, model = given.dattn.shape
    ny = nmp // 2
    width = given.packed.shape[2]
    c_out = given.mixed.shape[2]
    c_up = given.g_up.shape[2]
    height = model // ndp
    pairs = (ndp * ny - 1, height // 2)
    dma = pltpu.SemaphoreType.DMA
    wide = (c_up, given.g_down.shape[2], width, c_out)
    outs = [jax.ShapeDtypeStruct((height // nmp, THIN), f32)]
    outs += [jax.ShapeDtypeStruct((height, n), f32) for n in wide]
    outs += [jax.ShapeDtypeStruct((8, 128), f32)]
    scratch = [
        pltpu.VMEM((ny, model, width), bf),
        pltpu.VMEM((ny, model, c_out), bf),
        pltpu.VMEM((model, THIN), bf),
    ]
    for n in wide:
        scratch += [pltpu.VMEM((*pairs, n), bf)] * 2
    scratch += [
        pltpu.VMEM((ndp * nmp - 1, height // nmp, THIN), bf),
        pltpu.VMEM((nmp, rows, width), bf),
        pltpu.VMEM((2, rows, width), bf),
        pltpu.VMEM((nmp, rows, width), bf),
        pltpu.VMEM((rows, model), bf),
        pltpu.VMEM((rows, model), bf),
        pltpu.VMEM((rows, model), bf),
        pltpu.VMEM((ny, rows, c_out), bf),
        pltpu.VMEM((ny, rows, width), bf),
        pltpu.VMEM((2, PAD, model), f32),
        pltpu.VMEM((2, PAD, model), f32),
        pltpu.VMEM((nmp + ndp, 8, 128), f32),
        pltpu.VMEM((2, model, width), bf),
        pltpu.VMEM((128, model), f32),
        dma((9, ndp * nmp)),
        dma((9, ndp * nmp)),
        dma((16,)),
        dma((16,)),
        dma((16,)),
        dma((nmp - 1,)),
        dma((nmp - 1,)),
        dma((ndp - 1,)),
        dma((ndp - 1,)),
        pltpu.SemaphoreType.REGULAR,
    ]
    anywhere = pl.BlockSpec(memory_space=pl.ANY)
    specs = [SMEM] * 2 + [VMEM] * 8 + [anywhere] * 3 + [VMEM] * 1 + [anywhere] * 7
    return pl.pallas_call(
        functools.partial(back_kernel, ndp, nmp),
        name="back",
        out_shape=outs,
        in_specs=specs,
        out_specs=[VMEM] * len(outs),
        scratch_shapes=scratch,
        compiler_params=pltpu.CompilerParams(
            collective_id=1, has_side_effects=True, vmem_limit_bytes=62 << 20
        ),
    )(*given)


def step_kernel(sums, g_thin, g_qkv, g_out, g_up, g_down, *refs):
    weights, firsts, seconds = refs[:7], refs[7:14], refs[14:21]
    loss, grad_norm = refs[21:23]
    outs = refs[23:]
    norm = jnp.sqrt(sums[0:1, 1:2])
    loss[...] = sums[0:1, 0:1]
    grad_norm[...] = norm
    factor = CLIP_AT / jnp.maximum(norm, CLIP_AT)

    def update(i, here, grad):
        new = adam_update(weights[i][here], firsts[i][here], seconds[i][here], grad, factor)
        for n in range(3):
            outs[3 * i + n][here] = new[n]

    inputs, channels = weights[0].shape[1], weights[1].shape[1]
    mel = weights[6].shape[1]
    every = slice(None)
    update(0, every, g_thin[:, :THIN_CHAN][:, :inputs])
    update(1, every, g_thin[:, THIN_CHAN:THIN_HEAD][:, :channels])
    update(6, every, g_thin[:, THIN_HEAD:][:, :mel])
    for i, grad in ((2, g_qkv), (4, g_up)):
        by_tiles(grad.shape[0], 16, lambda here, i=i, grad=grad: update(i, here, grad[here]))
    for i, grad in ((3, g_out), (5, g_down)):
        by_tiles(grad.shape[1], 128, lambda here, i=i, grad=grad: update(i, here, grad[:, here].T))


def step_all(sums, grads, state):
    state = [x.T if i % 7 < 2 else x for i, x in enumerate(state)]
    one = jax.ShapeDtypeStruct((1, 1), f32)
    outs = [jax.ShapeDtypeStruct(state[i].shape, f32) for i in range(7) for _ in range(3)]
    loss, norm, *new = pl.pallas_call(
        step_kernel,
        name="step",
        out_shape=[one, one] + outs,
        in_specs=[VMEM] * 27,
        out_specs=[VMEM] * 23,
        compiler_params=pltpu.CompilerParams(vmem_limit_bytes=62 << 20),
    )(sums, *grads, *state)
    return (loss[0, 0], norm[0, 0], *[x.T for x in new[:6]], *new[6:])


def shards(
    clean_mel,
    noise_mel,
    lengths,
    span_start,
    span_end,
    phone_ids,
    flow_steps,
    in_table,
    channel_rows,
    attn_qkv,
    attn_out,
    ffn_up,
    ffn_down,
    mel_head,
    table_first,
    channel_first,
    qkv_first,
    merge_first,
    upward_first,
    downward_first,
    head_first,
    table_second,
    channel_second,
    qkv_second,
    merge_second,
    upward_second,
    downward_second,
    head_second,
):
    micro, units, length, mel = clean_mel.shape
    nmp = lax.axis_size("mp")
    seqs = nmp // micro
    rows = length // seqs
    mp = lax.axis_index("mp")
    batch = mp // seqs
    seq = mp % seqs
    base = seq * rows
    width = in_table.shape[0]
    nch = channel_rows.shape[0]

    c_qkv = attn_qkv.shape[1]
    c_out = attn_out.shape[0]
    c_up = ffn_up.shape[1]

    ndp = lax.axis_size("dp")
    spans = jnp.sum(span_end - span_start, axis=1)
    digits = jnp.stack([spans // 32, spans % 32], axis=1).reshape(1, -1)
    digits = jnp.broadcast_to(digits, (mel_head.shape[0], 2 * micro))

    def columns(x, size):
        return jnp.pad(x.astype(bf), ((0, 0), (0, size - x.shape[1])))

    thin = jnp.concatenate(
        [
            columns(in_table.T, THIN_CHAN),
            columns(channel_rows.T, THIN_HEAD - THIN_CHAN),
            columns(jnp.concatenate([mel_head, digits.astype(f32)], axis=1), THIN - THIN_HEAD),
        ],
        axis=1,
    )
    mid = jnp.concatenate([attn_out.T, ffn_up], axis=1).astype(bf)
    own = (ndp, nmp, seqs) == (8, 4, 2)
    def mine(x):
        return lax.dynamic_index_in_dim(x, batch, 0, keepdims=False)[0]

    def widen(x):
        x = jnp.pad(mine(x), [(PAD, PAD)] + [(0, 0)] * (x.ndim - 3))
        return lax.dynamic_slice_in_dim(x, base, rows + 2 * PAD, 0)

    size = mine(lengths)
    first_frame = mine(span_start)
    last_frame = mine(span_end)
    place = base - PAD + jnp.arange(rows + 2 * PAD)
    valid_ext = ((place >= 0) & (place < size)).astype(f32)[:, None]
    masked_ext = ((place >= first_frame) & (place < last_frame)).astype(f32)[:, None]
    inside = slice(PAD, PAD + rows)
    valid = valid_ext[inside]
    masked = masked_ext[inside]
    tau = mine(flow_steps).astype(f32) / TSTEPS
    clean = widen(clean_mel).astype(f32)
    noise = widen(noise_mel).astype(f32)
    noisy = (1.0 - (1.0 - SIGMA) * tau) * noise + tau * clean
    context = clean * (valid_ext * (1.0 - masked_ext))
    target = (clean - (1.0 - SIGMA) * noise)[inside]
    onehot = (widen(phone_ids)[:, None] == jnp.arange(PHONES)).astype(bf)
    features_ext = jnp.concatenate([noisy.astype(bf), context.astype(bf), onehot], axis=-1)
    features = features_ext[inside]

    wires = Wires(ndp, nmp)
    owners = [wires.owner_mp(m // 2, m % 2) if own else m for m in range(nmp)]
    owners = jnp.stack(owners) if own else jnp.arange(nmp)
    heads = (owners[:, None] * (HEADS // nmp) + jnp.arange(HEADS // nmp)).reshape(-1)
    slopes = jnp.exp2(-8.0 * (heads + 1).astype(f32) / HEADS)
    if own:
        numbers = [base, (1 - seq) * rows, size, first_frame, last_frame, batch, mel]
        places = jnp.stack([jnp.asarray(n, jnp.int32) for n in numbers])
        features_wide = columns(features_ext, THIN_CHAN)
        fore = fore_all(
            ndp,
            nmp,
            ForeIn(
                places=places,
                slopes=slopes,
                thin_own=thin,
                near_own=attn_qkv.astype(bf),
                mid_own=mid,
                down_own=ffn_down.T.astype(bf),
                features=features_wide,
            ),
        )
        thin = fore.thin
    else:
        thin = lax.all_gather(thin, ("dp", "mp"), axis=0, tiled=True)
        w_qkv = lax.all_gather(attn_qkv.astype(bf), ("mp", "dp"), axis=0, tiled=True)
        w_qkv = w_qkv.reshape(nmp, -1, c_qkv)
        rest = jnp.concatenate([mid, ffn_down.T.astype(bf)], axis=1)
        rest = lax.all_gather(rest, ("mp", "dp"), axis=0, tiled=True)
        rest = rest.reshape(nmp, -1, rest.shape[1])
        owners = jnp.arange(nmp)
    model = thin.shape[0]
    if own:
        middle = middle_all(
            ndp,
            nmp,
            MiddleIn(
                places=places,
                second=fore.second,
                a2=fore.a2,
                active=fore.active,
                slope=fore.slope,
                chan=fore.chan,
                thin=fore.thin,
                target=jnp.pad(target, ((0, 0), (0, 128 - mel))),
                mid=fore.mid,
                down=fore.down,
            ),
        )
        given = BackIn(
            places=places,
            slopes=slopes,
            loss=middle.loss,
            g_up=middle.g_up,
            g_down=middle.g_down,
            dattn=middle.dattn,
            mixed=fore.mixed,
            extra=middle.extra,
            g_head=middle.g_head,
            chan=fore.chan,
            packed=fore.packed,
            other=fore.other,
            mixed_t=fore.mixed_t,
            lse=fore.lse,
            dmixed=middle.dmixed,
            w_qkv=fore.near,
            first=fore.first,
            conv=fore.conv,
            dsecond=middle.dsecond,
            hm=fore.hm,
            features=features_wide,
        )
        g_thin, g_up, g_down, g_qkv, g_out, sums = back_all(ndp, nmp, given)
        state = (
            in_table, channel_rows, attn_qkv, attn_out, ffn_up, ffn_down, mel_head,
            table_first, channel_first, qkv_first, merge_first, upward_first, downward_first,
            head_first, table_second, channel_second, qkv_second, merge_second, upward_second,
            downward_second, head_second,
        )
        return step_all(sums, (g_thin, g_qkv, g_out, g_up, g_down), state)
    else:
        digits = thin[:, THIN_HEAD + mel : THIN_HEAD + mel + 2 * micro]
        digits = jnp.sum(digits.reshape(ndp, -1, 2 * micro)[:, 0].astype(f32), axis=0)
        count = lax.dynamic_slice_in_dim(digits, 2 * batch, 2, 0)
        count = count[0] * 32.0 + count[1]
        w_out = rest[:, :, :c_out]
        w_up = rest[:, :, c_out : c_out + c_up]
        w_down = rest[:, :, c_out + c_up :]
        w_in = thin[:, :width]
        channel = thin[:, THIN_CHAN : THIN_CHAN + nch].T.astype(f32)
        w_head = thin[:, THIN_HEAD : THIN_HEAD + mel]
        taps = channel[:KERNEL]
        vecs = channel[KERNEL:]

        start_ext = rdot(features_ext, w_in) + vecs[6]
        hm = start_ext * valid_ext
        conv = jnp.zeros((rows, model), f32) + vecs[7]
        for k in range(KERNEL):
            conv = conv + taps[k] * hm[k + 1 : k + 1 + rows]
        first = start_ext[inside] + gelu(conv)
        x_one, r_one = norm_parts(first)
        act_one = (x_one * vecs[0] + vecs[1]).astype(bf)

        groups = [[g * seqs + s for s in range(seqs)] for g in range(micro)]

        def shift(x, i):
            pairs = [(g[(s + i) % seqs], g[s]) for g in groups for s in range(seqs)]
            return lax.ppermute(x, "mp", pairs)

        def unshift(x, i):
            pairs = [(g[s], g[(s + i) % seqs]) for g in groups for s in range(seqs)]
            return lax.ppermute(x, "mp", pairs)

        packed = jnp.einsum("rd,mdc->rmc", act_one, w_qkv, preferred_element_type=f32).astype(bf)
        packed = packed.reshape(rows, HEADS, 3, HEAD_DIM)
        query, key, value = packed[:, :, 0], packed[:, :, 1], packed[:, :, 2]
        both = jnp.stack([key, value])
        both = jnp.concatenate([both] + [shift(both, i) for i in range(1, seqs)], axis=1)
        keys, values = both[0], both[1]
        blocks = (seq + jnp.arange(seqs)) % seqs
        key_place = (blocks[:, None] * rows + jnp.arange(rows)).reshape(-1)
        query_place = base + jnp.arange(rows)
        distance = jnp.abs(query_place[:, None] - key_place[None, :]).astype(f32)
        raw = jnp.einsum("qhd,khd->hqk", query, keys, preferred_element_type=f32)
        score = raw * SCALE - slopes[:, None, None] * distance
        score = jnp.where((key_place < size)[None, None, :], score, -1000000000.0)
        top = jnp.max(score, axis=-1, keepdims=True)
        prob = jnp.exp(score - top)
        prob = prob / jnp.sum(prob, axis=-1, keepdims=True)
        prob_low = prob.astype(bf)
        mixed = jnp.einsum("hqk,khd->qhd", prob_low, values, preferred_element_type=f32)
        mixed = mixed.astype(bf).reshape(rows, nmp, c_out)
        mixed = [mixed[:, m] for m in range(nmp)]
        attn = jnp.zeros((rows, model), f32)
        for m in range(nmp):
            attn = attn + rdot(mixed[m], w_out[m])
        second = first + attn

        x_two, r_two = norm_parts(second)
        act_two = (x_two * vecs[2] + vecs[3]).astype(bf)
        ffn = jnp.zeros((rows, model), f32)
        hidden = []
        active = []
        for m in range(nmp):
            hidden.append(dot(act_two, w_up[m]))
            active.append(gelu(hidden[m]).astype(bf))
            ffn = ffn + rdot(active[m], w_down[m])
        third = second + ffn

        x_three, r_three = norm_parts(third)
        act_three = (x_three * vecs[4] + vecs[5]).astype(bf)
        error = dot(act_three, w_head) - target
        weight_rows = masked / count
        loss_local = jnp.sum(weight_rows * error * error)
        dpred = (2.0 * weight_rows * error).astype(bf)
        g_head = tdot(act_three, dpred)
        dthird, dg3, db3 = norm_back(rdot(dpred, w_head), x_three, r_three, vecs[4])

        dffn = dthird.astype(bf)
        da2 = jnp.zeros((rows, model), f32)
        dhids = []
        for m in range(nmp):
            dhid = gelu_back(hidden[m], dot(dffn, w_down[m])).astype(bf)
            dhids.append(dhid)
            da2 = da2 + rdot(dhid, w_up[m])
        dnorm, dg2, db2 = norm_back(da2, x_two, r_two, vecs[2])
        dsecond = dthird + dnorm

        dattn = dsecond.astype(bf)
        g_out = [tdot(dattn, mixed[m]).astype(bf) for m in range(nmp)]
        dmixed = [dot(dattn, w_out[m]).astype(bf) for m in range(nmp)]
        dmixed = jnp.stack(dmixed, axis=1).reshape(rows, HEADS, HEAD_DIM)
        dvalues = jnp.einsum("hqk,qhd->khd", prob_low, dmixed, preferred_element_type=f32)
        dprob = jnp.einsum("qhd,khd->hqk", dmixed, values, preferred_element_type=f32)
        dscore = prob * (dprob - jnp.sum(prob * dprob, axis=-1, keepdims=True))
        draw = (dscore * SCALE).astype(bf)
        dquery = jnp.einsum("hqk,khd->qhd", draw, keys, preferred_element_type=f32)
        dkeys = jnp.einsum("hqk,qhd->khd", draw, query, preferred_element_type=f32)
        dboth = jnp.stack([dkeys, dvalues])
        parts = [dboth[:, i * rows : (i + 1) * rows] for i in range(seqs)]
        dboth = parts[0]
        for i in range(1, seqs):
            dboth = dboth + unshift(parts[i].astype(bf), i).astype(f32)
        dpacked = jnp.stack([dquery, dboth[0], dboth[1]], axis=2).astype(bf)
        dpacked = dpacked.reshape(rows, nmp, c_qkv)
        dpacked = [dpacked[:, m] for m in range(nmp)]
        g_qkv = [tdot(act_one, dpacked[m]).astype(bf) for m in range(nmp)]
        da1 = jnp.zeros((rows, model), f32)
        for m in range(nmp):
            da1 = da1 + rdot(dpacked[m], w_qkv[m])

        dnorm, dg1, db1 = norm_back(da1, x_one, r_one, vecs[0])
        dfirst = dsecond + dnorm
        dconv = gelu_back(conv, dfirst)
        right = lax.ppermute(
            dconv[:PAD], "mp", [(g[s + 1], g[s]) for g in groups for s in range(seqs - 1)]
        )
        left = lax.ppermute(
            dconv[rows - PAD :], "mp", [(g[s], g[s + 1]) for g in groups for s in range(seqs - 1)]
        )
        dconv_ext = jnp.concatenate([left, dconv, right], axis=0)
        back = jnp.zeros((rows, model), f32)
        g_taps = []
        for k in range(KERNEL):
            back = back + taps[k] * dconv_ext[2 * PAD - 1 - k : 2 * PAD - 1 - k + rows]
            g_taps.append(jnp.sum(dconv * hm[k + 1 : k + 1 + rows], axis=0))
        dstart = dfirst + valid * back
        g_in = tdot(dstart.astype(bf), features)
        g_rows = g_taps + [dg1, db1, dg2, db2, dg3, db3, jnp.sum(dstart, axis=0), jnp.sum(dconv, axis=0)]
        g_chan = jnp.stack(g_rows, axis=1)

        g_thin = jnp.concatenate(
            [
                columns(g_in, THIN_CHAN),
                columns(g_chan, THIN_HEAD - THIN_CHAN),
                columns(g_head, THIN - THIN_HEAD),
            ],
            axis=1,
        )
        g_up = [tdot(act_two, dhids[m]).astype(bf) for m in range(nmp)]
        g_down = [tdot(dffn, active[m]).astype(bf) for m in range(nmp)]
        terms = [g_thin, jnp.stack(g_up), jnp.stack(g_down), jnp.stack(g_qkv), jnp.stack(g_out)]
        g_thin = lax.psum_scatter(g_thin, ("dp", "mp"), scatter_dimension=0, tiled=True)
        sums = [g_thin.astype(f32)] + [
            lax.psum_scatter(
                t.reshape(-1, t.shape[2]), ("mp", "dp"), scatter_dimension=0, tiled=True
            ).astype(f32)
            for t in terms[1:]
        ]
        g_thin, g_up, g_down, g_qkv, g_out = sums
        squares = sum(jnp.sum(g * g) for g in sums)
        sums = lax.psum(jnp.stack([loss_local, squares])[None], ("dp", "mp"))
    sums = sums[0]
    loss = sums[0]
    grad_norm = jnp.sqrt(sums[1])
    factor = CLIP_AT / jnp.maximum(grad_norm, CLIP_AT)

    tw, tm, tv = adam_update(in_table, table_first, table_second, g_thin[:, :width].T, factor)
    cw, cm, cv = adam_update(
        channel_rows, channel_first, channel_second, g_thin[:, THIN_CHAN : THIN_CHAN + nch].T, factor
    )
    hw, hm_, hv = adam_update(mel_head, head_first, head_second, g_thin[:, THIN_HEAD : THIN_HEAD + mel], factor)
    qw, qm, qv = adam_update(attn_qkv, qkv_first, qkv_second, g_qkv, factor)
    ow, om, ov = adam_update(attn_out, merge_first, merge_second, g_out.T, factor)
    uw, um, uv = adam_update(ffn_up, upward_first, upward_second, g_up, factor)
    dw, dm, dv = adam_update(ffn_down, downward_first, downward_second, g_down.T, factor)
    return (
        loss, grad_norm,
        tw, tm, tv, cw, cm, cv, qw, qm, qv, ow, om, ov, uw, um, uv, dw, dm, dv, hw, hm_, hv,
    )


def solution(mesh):
    wide = P(None, ("dp", "mp"))
    tall = P(("dp", "mp"), None)
    down = P("dp", "mp")
    flat = P("mp", "dp")
    weights = (wide, wide, down, flat, down, flat, tall)
    pair = P(None, "dp")
    data = (P(None, "dp", None, None), P(None, "dp", None, None), pair, pair, pair)
    data = data + (P(None, "dp", None), pair)
    return jax.shard_map(
        shards,
        mesh=mesh,
        in_specs=data + weights * 3,
        out_specs=(P(), P()) + tuple(w for w in weights for _ in range(3)),
        check_vma=False,
    )
```

```python
import functools
from typing import Any, NamedTuple

import jax
import jax.numpy as jnp
from jax import lax
from jax.experimental import pallas as pl
from jax.experimental.pallas import tpu as pltpu
from jax.sharding import PartitionSpec as P

HEADS = 16
HEAD_DIM = 64
PHONES = 128
KERNEL = 31
HALF = 15
PAD = 16
TSTEPS = 1000
STEP = 10

SIGMA = 1e-05
BETA_ONE = 0.9
BETA_TWO = 0.999
EPSILON = 1e-08
DECAY = 0.01
RATE = 0.15
CLIP_AT = 0.1
NORM_EPS = 1e-05
SCALE = HEAD_DIM**-0.5
bf = jnp.bfloat16
f32 = jnp.float32


def gelu(v):
    return jax.nn.gelu(v, approximate=True)


def gelu_back(v, dv):
    return jax.vjp(gelu, v)[1](dv)[0]


def dot(left, right):
    return jnp.dot(left, right, preferred_element_type=f32)


def tdot(left, right):
    return lax.dot_general(
        left, right, (((0,), (0,)), ((), ())), preferred_element_type=f32
    )


def rdot(left, right):
    return lax.dot_general(
        left, right, (((1,), (1,)), ((), ())), preferred_element_type=f32
    )


def norm_parts(v):
    centered = v - jnp.mean(v, axis=-1, keepdims=True)
    spread = jnp.mean(centered * centered, axis=-1, keepdims=True)
    r = lax.rsqrt(spread + NORM_EPS)
    return centered * r, r


def norm_back(da, xhat, r, gain):
    dgain = jnp.sum(da * xhat, axis=0)
    dbias = jnp.sum(da, axis=0)
    dx = da * gain
    dv = r * (
        dx
        - jnp.mean(dx, axis=-1, keepdims=True)
        - xhat * jnp.mean(dx * xhat, axis=-1, keepdims=True)
    )
    return dv, dgain, dbias


def adam_update(weight, first, second, grad, factor):
    clipped = grad * factor
    first_new = BETA_ONE * first + (1.0 - BETA_ONE) * clipped
    second_new = BETA_TWO * second + (1.0 - BETA_TWO) * clipped * clipped
    first_hat = first_new / (1.0 - BETA_ONE**STEP)
    second_hat = second_new / (1.0 - BETA_TWO**STEP)
    weight_new = weight - RATE * (first_hat / (jnp.sqrt(second_hat) + EPSILON) + DECAY * weight)
    return (weight_new, first_new, second_new)


MESH = pl.DeviceIdType.MESH
AXES = ("z", "x", "y", "c")


class Wires:
    def __init__(self, ndp, nmp):
        self.sizes = {"z": ndp // 2, "x": 2, "y": nmp // 2, "c": 2}
        dp = lax.axis_index("dp")
        mp = lax.axis_index("mp")
        self.at = {"z": dp // 2, "x": dp % 2, "y": mp // 2, "c": mp % 2}

    def peer(self, axis, k):
        at = dict(self.at)
        at[axis] = lax.rem(at[axis] + k, self.sizes[axis])
        return (at["z"] * 2 + at["x"], at["y"] * 2 + at["c"])

    def owner_mp(self, ky, kc):
        ny = self.sizes["y"]
        return lax.rem(self.at["y"] + ny - ky, ny) * 2 + lax.rem(self.at["c"] + 2 - kc, 2)

    def near(self, k):
        nmp = self.sizes["y"] * self.sizes["c"]
        return (lax.axis_index("dp"), lax.rem(lax.axis_index("mp") + k, nmp))

    def far(self, k):
        ndp = self.sizes["z"] * self.sizes["x"]
        return (lax.rem(lax.axis_index("dp") + k, ndp), lax.axis_index("mp"))

    def align(self, again):
        fars = [self.far(k) for k in range(1, self.sizes["z"] * self.sizes["x"])]
        self.greet([self.near(k) for k in range(1, self.sizes["y"] * self.sizes["c"])] + fars)
        for p in fars:
            pl.semaphore_signal(again, inc=1, device_id=p, device_id_type=MESH)
        pl.semaphore_wait(again, len(fars))

    def greet(self, peers):
        barrier = pltpu.get_barrier_semaphore()
        for p in peers:
            pl.semaphore_signal(barrier, inc=1, device_id=p, device_id_type=MESH)
        pl.semaphore_wait(barrier, len(peers))


def slot_number(sizes, k):
    return ((k["z"] * sizes["x"] + k["x"]) * sizes["y"] + k["y"]) * sizes["c"] + k["c"]


def spread(sizes, order):
    slots = [(dict.fromkeys(AXES, 0), -1)]
    for stage, axis in enumerate(order):
        slots += [
            ({**k, axis: n}, stage) for n in range(1, sizes[axis]) for k, _ in list(slots)
        ]
    return slots


class Gather:
    def __init__(self, wires, order, own, slot, send, recv):
        self.wires, self.order, self.own, self.slot = wires, order, own, slot
        self.send, self.recv = send, recv
        self.slots = spread(wires.sizes, order)
        self.by_number = {slot_number(wires.sizes, k): i for i, (k, _) in enumerate(self.slots)}
        self.started = []

    def forward(self, source, k, stage):
        for later in range(stage + 1, len(self.order)):
            axis = self.order[later]
            for n in range(1, self.wires.sizes[axis]):
                there = {**k, axis: n}
                number = slot_number(self.wires.sizes, there)
                copy = pltpu.make_async_remote_copy(
                    source, self.slot(there, k), self.send.at[number], self.recv.at[number],
                    device_id=self.wires.peer(axis, n), device_id_type=MESH,
                )
                copy.start()
                self.started.append((copy, number))

    def begin(self):
        k, stage = self.slots[0]
        self.forward(self.own, k, stage)

    def arrive(self, number):
        k, stage = self.slots[self.by_number[number]]
        here = self.slot(k, k)
        pltpu.make_async_remote_copy(
            here, here, self.send.at[number], self.recv.at[number],
            device_id=self.wires.peer("c", 1), device_id_type=MESH,
        ).wait_recv()
        self.forward(here, k, stage)

    def finish(self):
        for copy, _ in self.started:
            copy.wait_send()


FIRST = ("z", "x", "y", "c")
OTHER = ("z", "y", "x", "c")


def total(ref):
    rows = 8

    def body(i, part):
        x = ref[pl.ds(i * rows, rows)]
        return part + x * x

    part = lax.fori_loop(0, ref.shape[0] // rows, body, jnp.zeros((rows, ref.shape[1]), f32))
    return jnp.sum(part)


BLOCK = 256
TILE = 64
FAR = 1e12


def distances(dist, base, other_base, size):
    rows = dist.shape[1]

    def body(i, _):
        here = pl.ds(pl.multiple_of(i * TILE, TILE), TILE)
        down = lax.broadcasted_iota(jnp.int32, (TILE, rows), 0) + i * TILE
        key = jnp.where(down < rows, base + down, other_base + down - rows)
        query = base + lax.broadcasted_iota(jnp.int32, (TILE, rows), 1)
        dist[here] = jnp.where(key < size, jnp.abs(key - query).astype(f32), FAR)
        return 0

    lax.fori_loop(0, dist.shape[0] // TILE, body, 0)


def key_blocks(packed, other, m, col):
    rows = packed.shape[1]
    twin = m + 1 - 2 * (m % 2)
    for part, (ref, index) in enumerate(((packed, m), (other, twin))):
        for start in range(0, rows, BLOCK):
            k = ref[index, start : start + BLOCK, col + HEAD_DIM : col + 2 * HEAD_DIM]
            v = ref[index, start : start + BLOCK, col + 2 * HEAD_DIM : col + 3 * HEAD_DIM]
            yield part, start, part * rows + start, k, v


def attend(packed, other, dist, slopes, mixed, mixed_t, lse, score, m):
    heads = packed.shape[2] // (3 * HEAD_DIM)
    for j in range(heads):
        col = j * 3 * HEAD_DIM
        q = packed[m, :, col : col + HEAD_DIM] * bf(SCALE)
        slope = slopes[m * heads + j]
        top = None
        for _, _, at, k, _ in key_blocks(packed, other, m, col):
            s = rdot(k, q) - slope * dist[at : at + BLOCK]
            score[at : at + BLOCK] = s
            peak = jnp.max(s, axis=0, keepdims=True)
            top = peak if top is None else jnp.maximum(top, peak)
        total_e = jnp.zeros_like(top)
        acc = None
        for _, _, at, _, v in key_blocks(packed, other, m, col):
            e = jnp.exp(score[at : at + BLOCK] - top)
            total_e = total_e + jnp.sum(e, axis=0, keepdims=True)
            part = tdot(v, e.astype(bf))
            acc = part if acc is None else acc + part
        out = acc / total_e
        row = (m * heads + j) * HEAD_DIM
        mixed_t[pl.ds(pl.multiple_of(row, HEAD_DIM), HEAD_DIM)] = out
        mixed[m, :, j * HEAD_DIM : (j + 1) * HEAD_DIM] = out.T.astype(bf)
        lse[m * heads + j] = top + jnp.log(total_e)
        yield


def attend_back(packed, other, dist, slopes, mixed_t, lse, dmixed, down, dother, m):
    heads = packed.shape[2] // (3 * HEAD_DIM)
    for j in range(heads):
        col = j * 3 * HEAD_DIM
        q = packed[m, :, col : col + HEAD_DIM] * bf(SCALE)
        slope = slopes[m * heads + j]
        row = (m * heads + j) * HEAD_DIM
        mt = mixed_t[pl.ds(pl.multiple_of(row, HEAD_DIM), HEAD_DIM)]
        dm = dmixed[m, :, j * HEAD_DIM : (j + 1) * HEAD_DIM]
        delta = jnp.sum(dm.astype(f32).T * mt, axis=0, keepdims=True)
        level = lse[m * heads + j]
        dq = None
        for part, start, at, k, v in key_blocks(packed, other, m, col):
            p = jnp.exp(rdot(k, q) - slope * dist[at : at + BLOCK] - level)
            dv = dot(p.astype(bf), dm)
            t = (p * (rdot(v, dm) - delta)).astype(bf)
            dk = dot(t, q)
            more = tdot(k, t)
            dq = more if dq is None else dq + more
            here = slice(start, start + BLOCK)
            ref = dother if part else down.at[m]
            ref[here, col + HEAD_DIM : col + 2 * HEAD_DIM] = dk.astype(ref.dtype)
            ref[here, col + 2 * HEAD_DIM : col + 3 * HEAD_DIM] = dv.astype(ref.dtype)
        down[m, :, col : col + HEAD_DIM] = (dq * SCALE).T.astype(down.dtype)
        yield


def windows(x, count):
    for j in range(8):
        moved = x if j == 0 else pltpu.roll(x, x.shape[0] - j, 0)
        for far in range(0, count + 1, 8):
            if 1 <= far + j <= count:
                yield far + j, moved[far : far + TILE]


def convolve(hm, chan, conv, column):
    lanes = slice(column, column + 128)

    def body(r, _):
        start = pl.multiple_of(r * TILE, TILE)
        x = hm[pl.ds(start, TILE + 2 * PAD), lanes]
        acc = jnp.broadcast_to(chan[KERNEL + 7, lanes][None], (TILE, 128))
        for offset, moved in windows(x, KERNEL):
            acc = acc + chan[offset - 1, lanes][None] * moved
        conv[pl.ds(start, TILE), lanes] = acc
        return 0

    lax.fori_loop(0, conv.shape[0] // TILE, body, 0)


def convolve_back(dconv, hm, chan, back, gtaps, column):
    lanes = slice(column, column + 128)

    def body(r, _):
        start = pl.multiple_of(r * TILE, TILE)
        x = dconv[pl.ds(start, TILE + 2 * PAD), lanes]
        acc = jnp.zeros((TILE, 128), f32)
        for offset, moved in windows(x, KERNEL):
            acc = acc + chan[KERNEL - offset, lanes][None] * moved
        back[pl.ds(start, TILE), lanes] = acc
        here = x[PAD : PAD + TILE]
        y = hm[pl.ds(start, TILE + 2 * PAD), lanes]
        for offset, moved in windows(y, KERNEL):
            part = here * moved
            part = sum(part[i : i + 8] for i in range(8, TILE, 8)) + part[:8]
            rows_at = slice((offset - 1) * 8, offset * 8)
            gtaps[rows_at, lanes] = gtaps[rows_at, lanes] + part
        return 0

    lax.fori_loop(0, back.shape[0] // TILE, body, 0)


VMEM = pl.BlockSpec(memory_space=pltpu.VMEM)
SMEM = pl.BlockSpec(memory_space=pltpu.SMEM)


class Reduce:
    def __init__(self, wires, order, source, landing, out, send, recv):
        self.wires, self.order, self.source, self.landing = wires, order, source, landing
        self.out, self.send, self.recv = out, send, recv
        self.where = {}
        self.started = []
        sizes = {a: wires.sizes[a] if a in order else 1 for a in AXES}
        slots = [k for k, _ in spread(sizes, order[::-1])]
        self.stages = []
        for axis in order:
            self.stages.append([k for k in slots if k[axis]])
            slots = [k for k in slots if not k[axis]]
        self.by_number = {
            self.number(k): (stage, k) for stage, ks in enumerate(self.stages) for k in ks
        }
        self.summed = set()

    def number(self, k):
        return slot_number(self.wires.sizes, k)

    def now(self, k):
        n = self.number(k)
        return self.landing(self.where[n]) if n in self.where else self.source(k)

    def leave(self, stage, k):
        axis = self.order[stage]
        n = self.wires.sizes[axis]
        number = self.number(k)
        source = self.now(k)
        pltpu.make_async_remote_copy(
            source, self.landing(k), self.send.at[number], self.recv.at[number],
            device_id=self.wires.peer(axis, (n - k[axis]) % n), device_id_type=MESH,
        ).start()
        self.started.append((k, number))

    def keep(self):
        add_rows(self.out, self.source(dict.fromkeys(AXES, 0)), None)

    def depart(self, number):
        self.leave(0, self.by_number[number][1])

    def terms(self, stage, kept):
        return {
            self.number({**kept, axis: n})
            for axis in self.order[: stage + 1]
            for n in range(1, self.wires.sizes[axis])
        }

    def arrive(self, number):
        stage, k = self.by_number[number]
        self.summed.add(number)
        here = self.landing(k)
        axis = self.order[stage]
        pltpu.make_async_remote_copy(
            here, here, self.send.at[number], self.recv.at[number],
            device_id=self.wires.peer(axis, 1), device_id_type=MESH,
        ).wait_recv()
        kept = {**k, axis: 0}
        if not any(kept.values()):
            add_rows(self.out, self.out, here)
            return
        add_rows(here, self.now(kept), here)
        self.where[self.number(kept)] = k
        last = k[axis] == self.wires.sizes[axis] - 1
        if last and stage + 1 < len(self.order) and kept[self.order[stage + 1]]:
            assert self.terms(stage, kept) <= self.summed
            self.leave(stage + 1, kept)

    def finish(self):
        for k, number in self.started:
            here = self.landing(k)
            pltpu.make_async_remote_copy(
                here, here, self.send.at[number], self.recv.at[number],
                device_id=self.wires.peer("c", 1), device_id_type=MESH,
            ).wait_send()


class Crossing:
    def __init__(self, *parts):
        self.parts = parts

    def make(self):
        (src, *s), (dst, *d), send, recv, i, wires = self.parts
        return pltpu.make_async_remote_copy(
            src.at[s[0]] if s else src, dst.at[d[0]] if d else dst, send.at[i], recv.at[i],
            device_id=wires.peer("c", 1), device_id_type=MESH,
        )

    def wait_send(self):
        self.make().wait_send()

    def wait_recv(self):
        self.make().wait_recv()


def add_rows(out, left, right):
    step = 16

    def body(i, _):
        here = pl.ds(pl.multiple_of(i * step, step), step)
        value = left[here].astype(f32)
        if right is not None:
            value = value + right[here].astype(f32)
        out[here] = value.astype(out.dtype)
        return 0

    lax.fori_loop(0, out.shape[0] // step, body, 0)


def gelu_slope(v):
    cube = 0.044715 * v * v * v
    t = jnp.tanh(0.7978845608028654 * (v + cube))
    inner = 0.7978845608028654 * (1.0 + 3.0 * 0.044715 * v * v)
    return 0.5 * (1.0 + t) + 0.5 * v * (1.0 - t * t) * inner


THIN_CHAN = 384
THIN_HEAD = 512
THIN = 640


class BackIn(NamedTuple):
    places: Any
    slopes: Any
    loss: Any
    g_up: Any
    g_down: Any
    dattn: Any
    mixed: Any
    extra: Any
    g_head: Any
    chan: Any
    packed: Any
    other: Any
    mixed_t: Any
    lse: Any
    dmixed: Any
    w_qkv: Any
    first: Any
    conv: Any
    dsecond: Any
    hm: Any
    features: Any


class BackRefs(NamedTuple):
    places: Any
    slopes: Any
    loss: Any
    g_up: Any
    g_down: Any
    dattn: Any
    mixed: Any
    extra: Any
    g_head: Any
    chan: Any
    packed: Any
    other: Any
    mixed_t: Any
    lse: Any
    dmixed: Any
    w_qkv: Any
    first: Any
    conv: Any
    dsecond: Any
    hm: Any
    features: Any
    o_thin: Any
    o_up: Any
    o_down: Any
    o_qkv: Any
    o_out: Any
    sums: Any
    g_qkv: Any
    g_out: Any
    thin: Any
    l_up0: Any
    l_up1: Any
    l_down0: Any
    l_down1: Any
    l_qkv0: Any
    l_qkv1: Any
    l_out0: Any
    l_out1: Any
    l_thin: Any
    down: Any
    dother: Any
    l_other: Any
    a1: Any
    l_a1: Any
    l_dattn: Any
    l_mixed: Any
    l_dpack: Any
    halo: Any
    edge: Any
    parts: Any
    w_buf: Any
    rows_buf: Any
    send: Any
    recv: Any
    c_send: Any
    c_recv: Any
    local: Any
    near_send: Any
    near_recv: Any
    far_send: Any
    far_recv: Any
    again: Any


COLS = 256


def by_tiles(count, size, body):
    def step(i, _):
        body(pl.ds(pl.multiple_of(i * size, size), size))
        return 0

    lax.fori_loop(0, count // size, step, 0)


def fold(x):
    return jnp.sum(x, axis=0, keepdims=True)


def norm_turn(da, xhat, scale, gain):
    dx = da * gain
    return scale * (
        dx
        - jnp.mean(dx, axis=-1, keepdims=True)
        - xhat * jnp.mean(dx * xhat, axis=-1, keepdims=True)
    )


FORE_TURNS = (
    (
        1, 8, 4, 2, 9, 16, 5, 3, 24, 17, 25, 12, 10, 6, 20, 13, 11, 28, 18, 7, 21, 26, 29, 19, 14, 27, 22,
        15, 30, 23, 31, 33, 65, 36, 34, 68, 66, 40, 48,
    ),
    (56, 72, 37, 35, 69, 67, 41, 49, 38),
    (97, 70, 129),
    (),
    (80, 42, 44),
    (),
    (88, 50),
    (52, 57, 73),
    (39,),
    (71,),
    (98,),
    (100, 81, 43, 45),
    (89, 51),
    (53, 130),
    (132, 104),
    (58, 99, 60),
    (101, 74),
    (76, 112),
    (131, 82, 84, 120, 133, 105),
    (46, 59, 92, 61),
    (75, 90),
    (77, 113),
    (
        54, 83, 85, 47, 93, 91, 55, 78, 79, 62, 63, 86, 87, 94, 95, 134, 121, 136, 108, 102, 144, 106, 152,
        116, 114, 124,
    ),
    (122,),
    (),
    (135, 137),
    (109, 103, 145, 107, 153, 117, 115, 125),
    (138, 140, 123),
    (110, 148),
    (),
    (161, 146, 156, 193),
    (139, 141, 164),
    (154, 111, 149, 168),
    (196, 118),
    (147, 157, 176, 142, 184, 165),
    (126, 155),
    (169, 150),
    (162, 197, 119),
    (177, 143, 185, 194, 158, 200),
    (127, 166, 172, 208, 151),
    (216, 163),
    (170, 180, 195, 159),
    (201, 178, 188, 167, 173),
    (),
    (209, 186, 198, 217, 171, 181, 202, 204, 179, 189),
    (174, 212, 210, 220),
    (187, 199, 203, 205, 218, 206, 182),
    (175, 213, 211, 221, 190, 214),
    (219, 207, 183, 222),
    (191, 215, 223),
)
BACK_TURNS = (
    (34, 100, 42, 108, 50, 116, 58, 124, 38, 102),
    (46, 110),
    (54, 118, 62, 126),
    (162, 228),
    (170, 236, 2, 68),
    (178, 244, 10, 76),
    (186, 252, 18, 84, 166, 230),
    (174, 238, 26, 92, 6, 70),
    (14, 78),
    (22, 86),
    (30, 94),
    (130, 182, 246, 196, 138, 204),
    (190, 254, 146, 212),
    (290, 356, 298, 364, 306, 372, 154, 220, 314, 380),
    (294, 358, 302, 366, 310, 374, 318, 382, 134, 198, 142, 206),
    (66, 4),
    (74, 12),
    (82, 20),
    (90, 28),
    (150, 214),
    (158, 222, 258, 324),
    (266, 332, 274, 340, 282, 348, 72, 262, 326, 270, 334),
    (418, 484, 426, 492, 434, 500, 442, 508, 422, 486, 430, 494, 278, 342, 286, 350, 8),
    (194, 132, 438, 502),
    (),
    (446, 510, 202, 140, 80),
    (210, 148),
    (218, 156, 16, 322, 260, 330, 268),
    (88, 386, 452),
    (394, 460, 24),
    (402, 468, 200),
    (410, 476, 136, 390, 454),
    (398, 462, 338, 276),
    (346, 284, 208),
    (406, 470, 414, 478),
    (
        545, 553, 561, 569, 549, 557, 565, 573, 547, 555, 563, 571, 551, 559, 567, 575, 144, 388, 450, 216,
        396, 458, 152, 328, 264, 336, 404, 466, 272, 344, 513, 521, 529, 412, 537, 517, 525, 474, 280, 533,
        541, 515, 523, 531, 539, 519, 527, 535, 543, 392, 456, 514, 522, 530, 538, 518, 400, 526, 534, 516,
        542, 524, 532, 464, 540, 408, 472, 520, 528, 536,
    ),
)


class ForeIn(NamedTuple):
    places: Any
    slopes: Any
    thin_own: Any
    near_own: Any
    mid_own: Any
    down_own: Any
    features: Any


class ForeOut(NamedTuple):
    thin: Any
    near: Any
    mid: Any
    down: Any
    hm: Any
    conv: Any
    first: Any
    packed: Any
    other: Any
    mixed: Any
    mixed_t: Any
    lse: Any
    chan: Any
    second: Any
    a2: Any
    active: Any
    slope: Any


class ForeRefs(NamedTuple):
    places: Any
    slopes: Any
    thin_own: Any
    near_own: Any
    mid_own: Any
    down_own: Any
    features: Any
    o_thin: Any
    o_near: Any
    mid: Any
    down: Any
    o_hm: Any
    o_conv: Any
    o_first: Any
    o_packed: Any
    o_other: Any
    o_mixed: Any
    o_mixed_t: Any
    o_lse: Any
    o_chan: Any
    o_second: Any
    o_a2: Any
    o_active: Any
    o_slope: Any
    thin: Any
    near: Any
    hm: Any
    conv: Any
    first: Any
    packed: Any
    other: Any
    mixed: Any
    mixed_t: Any
    lse: Any
    chan: Any
    second: Any
    a2: Any
    active: Any
    slope: Any
    a1: Any
    dist: Any
    score: Any
    w: Any
    send: Any
    recv: Any
    local: Any
    c_send: Any
    c_recv: Any
    again: Any


def fore_kernel(ndp, nmp, *refs):
    r = ForeRefs(*refs)
    wires = Wires(ndp, nmp)
    wires.align(r.again)
    sizes = wires.sizes
    thin_rows = r.thin_own.shape[0]
    rows, model = r.first.shape
    size = r.places[2]

    def thin_slot(k, sent):
        block = (k["z"] * sizes["x"] + k["x"]) * nmp + wires.owner_mp(sent["y"], sent["c"])
        return r.thin.at[pl.ds(pl.multiple_of(block * thin_rows, thin_rows), thin_rows)]

    flows = [Gather(wires, FIRST, r.thin_own, thin_slot, r.send.at[0], r.recv.at[0])]

    def wide_flow(own, out, half, order):
        height = own.shape[0] // 2

        def slot(k, sent):
            start = (k["z"] * sizes["x"] + k["x"]) * 2 * height + half * height
            return out.at[k["y"] * sizes["c"] + k["c"], pl.ds(start, height)]

        n = len(flows)
        part = own.at[pl.ds(half * height, height)]
        flows.append(Gather(wires, order, part, slot, r.send.at[n], r.recv.at[n]))
        return flows[-1]

    near = [wide_flow(r.near_own, r.near, h, o) for h, o in enumerate((FIRST, OTHER))]
    mid = [wide_flow(r.mid_own, r.mid, h, o) for h, o in enumerate((FIRST, OTHER))]
    down = [wide_flow(r.down_own, r.down, h, o) for h, o in enumerate((FIRST, OTHER))]
    zero = dict.fromkeys(AXES, 0)
    kept = [
        pltpu.make_async_copy(f.own, f.slot(zero, zero), r.local.at[i])
        for i, f in enumerate(flows)
    ]
    for copy in kept:
        copy.start()
    for f in flows[:1] + near:
        f.begin()
    turns = iter(FORE_TURNS)
    slots = ndp * nmp
    saves = []

    def save(src, dst):
        copy = pltpu.make_async_copy(src, dst, r.local.at[len(flows) + nmp + len(saves)])
        copy.start()
        saves.append(copy)

    def turn():
        for code in next(turns):
            flows[code // slots].arrive(code % slots)

    turn()
    for f in mid:
        f.begin()
    for copy in kept:
        copy.wait()

    for i in range(0, model, 128):
        cols = r.thin[i : i + 128, THIN_CHAN:THIN_HEAD].astype(f32)
        r.chan[:, i : i + 128] = cols.T
    save(r.chan, r.o_chan)
    save(r.thin, r.o_thin)
    distances(r.dist, r.places[0], r.places[1], size)
    turn()

    for column in range(0, model, 128):
        cols = slice(column, column + 128)
        h = rdot(r.features[...], r.thin[cols, :THIN_CHAN])
        h = h + r.chan[KERNEL + 6, cols][None]
        place = r.places[0] - PAD + lax.broadcasted_iota(jnp.int32, (h.shape[0], 1), 0)
        r.first[:, cols] = h[PAD : PAD + rows]
        r.hm[:, cols] = jnp.where((place >= 0) & (place < size), h, 0.0)
        turn()
    for c in range(0, model, 128):
        convolve(r.hm, r.chan, r.conv, c)
        turn()

    def norm(i, _):
        here = pl.ds(pl.multiple_of(i * TILE, TILE), TILE)
        v = r.conv[here]
        inner = 0.7978845608028654 * v * (1.0 + 0.044715 * v * v)
        first = r.first[here] + v * (0.5 + 0.5 * jnp.tanh(inner))
        r.first[here] = first
        xhat, _ = norm_parts(first)
        r.a1[here] = (xhat * r.chan[KERNEL][None] + r.chan[KERNEL + 1][None]).astype(bf)

        return 0

    save(r.hm, r.o_hm)
    save(r.conv, r.o_conv)
    for i in range(0, rows // TILE, 2):
        lax.fori_loop(i, i + 2, norm, 0)
        turn()
    save(r.first, r.o_first)
    turn()
    crossings = []
    width = r.packed.shape[2]
    for m in range(nmp):
        def expand(cols):
            r.packed[m, :, cols] = dot(r.a1[...], r.near[m, :, cols]).astype(bf)

        by_tiles(width, 3 * COLS, expand)
        copy = pltpu.make_async_remote_copy(
            r.packed.at[m], r.other.at[m], r.c_send.at[m], r.c_recv.at[m],
            device_id=wires.peer("c", 1), device_id_type=MESH,
        )
        copy.start()
        crossings.append(copy)
        turn()
    for f in down:
        f.begin()
    save(r.near, r.o_near)
    save(r.packed, r.o_packed)
    for m in range(nmp):
        crossings[m + 1 - 2 * (m % 2)].wait_recv()
        for _ in attend(
            r.packed, r.other, r.dist, r.slopes, r.mixed, r.mixed_t, r.lse,
            r.score, m,
        ):
            turn()
    turn()
    for src, dst in (
        (r.other, r.o_other), (r.mixed, r.o_mixed), (r.mixed_t, r.o_mixed_t), (r.lse, r.o_lse)
    ):
        save(src, dst)
    loads = [
        pltpu.make_async_copy(r.mid.at[m], r.w.at[m], r.local.at[len(flows) + m])
        for m in range(nmp)
    ]
    for copy in loads:
        copy.start()
    c_out = r.mixed.shape[2]
    hid = r.active.shape[2]
    w_out = [r.w.at[m, :, pl.ds(0, c_out)] for m in range(nmp)]
    w_up = [r.w.at[m, :, pl.ds(c_out, hid)] for m in range(nmp)]
    for copy in loads:
        copy.wait()

    def project(cols):
        acc = r.first[:, cols]
        for m in range(nmp):
            acc = acc + rdot(r.mixed[m], w_out[m][cols, :])
        r.second[:, cols] = acc

    by_tiles(model, 4 * COLS, project)

    def second_norm(here):
        xhat, _ = norm_parts(r.second[here])
        gain, bias = r.chan[KERNEL + 2][None], r.chan[KERNEL + 3][None]
        r.a2[here] = (xhat * gain + bias).astype(bf)

    by_tiles(rows, TILE, second_norm)
    save(r.second, r.o_second)
    save(r.a2, r.o_a2)
    turn()
    for m in range(nmp):

        def gelu_pair(v, cols):
            square = v * v
            t = jnp.tanh(0.7978845608028654 * v * (1.0 + 0.044715 * square))
            half = 0.5 + 0.5 * t
            r.active[m, :, cols] = (v * half).astype(bf)
            inner = 0.3989422804014327 * (1.0 + 0.134145 * square)
            r.slope[m, :, cols] = (half + v * (1.0 - t * t) * inner).astype(bf)

        def expand(i, _):
            cols = [pl.ds(pl.multiple_of((2 * i + n) * COLS, COLS), COLS) for n in range(2)]
            values = [dot(r.a2[...], w_up[m][:, c]) for c in cols]
            for v, c in zip(values, cols):
                gelu_pair(v, c)
            return 0

        lax.fori_loop(0, hid // COLS // 2, expand, 0)
        save(r.active.at[m], r.o_active.at[m])
        save(r.slope.at[m], r.o_slope.at[m])
        turn()
    turn()
    assert next(turns, None) is None
    for copy in saves:
        copy.wait()
    for f in flows:
        f.finish()
    for copy in crossings:
        copy.wait_send()


def fore_all(ndp, nmp, given):
    model = given.near_own.shape[0] * ndp
    width = given.near_own.shape[1]
    hid = given.down_own.shape[1]
    wide = HEADS * HEAD_DIM
    rows = given.features.shape[0] - 2 * PAD
    struct = jax.ShapeDtypeStruct
    dma = pltpu.SemaphoreType.DMA
    anywhere = pl.BlockSpec(memory_space=pl.ANY)
    outs = [
        struct((model, THIN), bf),
        struct((nmp, model, width), bf),
        struct((nmp, model, given.mid_own.shape[1]), bf),
        struct((nmp, model, hid), bf),
        struct((rows + 2 * PAD, model), f32),
        struct((rows, model), f32),
        struct((rows, model), f32),
        struct((nmp, rows, width), bf),
        struct((nmp, rows, width), bf),
        struct((nmp, rows, wide // nmp), bf),
        struct((wide, rows), f32),
        struct((HEADS, 1, rows), f32),
        struct((128, model), f32),
        struct((rows, model), f32),
        struct((rows, model), bf),
        struct((nmp, rows, hid), bf),
        struct((nmp, rows, hid), bf),
    ]
    outs = pl.pallas_call(
        functools.partial(fore_kernel, ndp, nmp),
        name="fore",
        out_shape=outs,
        in_specs=[SMEM] * 2 + [anywhere] * 4 + [VMEM],
        out_specs=[anywhere] * len(outs),
        scratch_shapes=[pltpu.VMEM(o.shape, o.dtype) for o in outs[:2] + outs[4:]]
        + [
            pltpu.VMEM((rows, model), bf),
            pltpu.VMEM((2 * rows, rows), f32),
            pltpu.VMEM((2 * rows, rows), f32),
            pltpu.VMEM((nmp, model, given.mid_own.shape[1]), bf),
            dma((7, ndp * nmp)),
            dma((7, ndp * nmp)),
            dma((7 + nmp + 13 + 2 * nmp,)),
            dma((nmp,)),
            dma((nmp,)),
            pltpu.SemaphoreType.REGULAR,
        ],
        compiler_params=pltpu.CompilerParams(
            collective_id=0, has_side_effects=True, vmem_limit_bytes=62 << 20
        ),
    )(*given)
    return ForeOut(*outs)


class MiddleIn(NamedTuple):
    places: Any
    second: Any
    a2: Any
    active: Any
    slope: Any
    chan: Any
    thin: Any
    target: Any
    mid: Any
    down: Any


class MiddleOut(NamedTuple):
    g_up: Any
    g_down: Any
    dsecond: Any
    dattn: Any
    dmixed: Any
    extra: Any
    g_head: Any
    loss: Any


class MiddleRefs(NamedTuple):
    places: Any
    second: Any
    a2: Any
    active: Any
    slope: Any
    chan: Any
    thin: Any
    target: Any
    mid: Any
    down: Any
    g_up: Any
    g_down: Any
    dsecond: Any
    dattn: Any
    dmixed: Any
    extra: Any
    g_head: Any
    loss: Any
    ffn: Any
    l_a2: Any
    dffn: Any
    l_dffn: Any
    l_active: Any
    l_dhid: Any
    dhid: Any
    a3: Any
    stage: Any
    w: Any
    w_down: Any
    c_send: Any
    c_recv: Any
    local: Any


def middle_kernel(ndp, nmp, *refs):
    r = MiddleRefs(*refs)
    wires = Wires(ndp, nmp)
    partner = wires.peer("c", 1)
    wires.greet([partner])
    rows, model = r.second.shape
    ny = nmp // 2
    theirs = list(range(1, nmp, 2))
    mine = list(range(0, nmp, 2))
    hid = r.active.shape[2]
    c_out = r.mid.shape[2] - hid
    w_out = [r.w.at[m, :, pl.ds(0, c_out)] for m in range(nmp)]
    w_up = [r.w.at[m, :, pl.ds(c_out, hid)] for m in range(nmp)]
    loads = [
        [
            pltpu.make_async_copy(src.at[m], dst.at[m], r.local.at[i * nmp + m])
            for m in range(nmp)
        ]
        for i, (src, dst) in enumerate(((r.down, r.w_down), (r.mid, r.w)))
    ]
    for group in loads:
        for m in theirs + mine:
            group[m].start()
    w_down = [r.w_down.at[m] for m in range(nmp)]
    crossings = []

    def cross(src, dst):
        i = len(crossings)
        copy = pltpu.make_async_remote_copy(
            src, dst, r.c_send.at[i], r.c_recv.at[i],
            device_id=partner, device_id_type=MESH,
        )
        copy.start()
        crossings.append(copy)
        return copy

    def row(i):
        return r.chan[KERNEL + i][None]

    got_a2 = cross(r.a2, r.l_a2)
    got_active = [cross(r.active.at[m], r.l_active.at[m // 2]) for m in theirs]
    for m in theirs + mine:
        loads[0][m].wait()

        def shrink(cols):
            part = rdot(r.active[m], w_down[m][cols, :])
            r.ffn[:, cols] = part if m == theirs[0] else r.ffn[:, cols] + part

        by_tiles(model, 4 * COLS, shrink)

    def third_norm(here):
        xhat, _ = norm_parts(r.second[here] + r.ffn[here])
        r.a3[here] = (xhat * row(4) + row(5)).astype(bf)

    by_tiles(rows, TILE, third_norm)
    mel = r.places[6]
    lanes = lax.broadcasted_iota(jnp.int32, (16, 128), 1)
    digits = jnp.zeros((16, 128), f32)
    for d in range(ndp):
        start = d * (model // ndp)
        digits = digits + r.thin[start : start + 16, THIN_HEAD:].astype(f32)
    first_digit = mel + 2 * r.places[5]
    scale = jnp.where(lanes == first_digit, 32.0, jnp.where(lanes == first_digit + 1, 1.0, 0.0))
    count = jnp.sum(digits[0:1] * scale[0:1], axis=1, keepdims=True)
    place = r.places[0] + lax.broadcasted_iota(jnp.int32, (rows, 1), 0)
    weights = jnp.where((place >= r.places[3]) & (place < r.places[4]), 1.0, 0.0) / count
    head_lanes = lax.broadcasted_iota(jnp.int32, (model, 128), 1)
    head = jnp.where(head_lanes < mel, r.thin[:, THIN_HEAD:].astype(f32), 0.0).astype(bf)
    error = dot(r.a3[...], head) - r.target[...]
    weighted = weights * error
    lanes = lanes[:8]
    r.loss[...] = jnp.where(lanes == 0, jnp.sum(weighted * error), 0.0)
    dpred = (2.0 * weighted).astype(bf)
    r.g_head[...] = tdot(r.a3[...], dpred).astype(bf)
    r.dsecond[...] = rdot(dpred, head)

    zero = jnp.zeros((1, model), f32)

    def third_back(i, acc):
        here = pl.ds(pl.multiple_of(i * TILE, TILE), TILE)
        xhat, scale = norm_parts(r.second[here] + r.ffn[here])
        da = r.dsecond[here]
        dv = norm_turn(da, xhat, scale, row(4))
        r.ffn[here] = dv
        r.dffn[here] = dv.astype(bf)
        return acc[0] + fold(da * xhat), acc[1] + fold(da)

    dgain, dbias = lax.fori_loop(0, rows // TILE, third_back, (zero, zero))
    r.extra[...] = jnp.zeros_like(r.extra)
    r.extra[2:3] = dgain
    r.extra[3:4] = dbias
    got_dffn = cross(r.dffn, r.l_dffn)
    got_dhid = []
    stored = []

    def store(out, y, left, right, left_other, right_other):
        slot = len(stored) % 2
        if len(stored) >= 2:
            stored[-2].wait()

        def body(cols):
            part = tdot(left[:, cols], right[...]) + tdot(left_other[:, cols], right_other[...])
            r.stage[slot, cols] = part.astype(bf)

        by_tiles(model, 4 * COLS, body)
        copy = pltpu.make_async_copy(r.stage.at[slot], out.at[y], r.local.at[2 * nmp + len(stored)])
        copy.start()
        stored.append(copy)

    got_a2.wait_recv()
    for m in theirs + mine:
        loads[1][m].wait()

        def contract(cols):
            dact = dot(r.dffn[...], w_down[m][:, cols])
            r.dhid[m, :, cols] = (dact * r.slope[m, :, cols].astype(f32)).astype(bf)

        by_tiles(hid, 4 * COLS, contract)
        if m in theirs:
            got_dhid.append(cross(r.dhid.at[m], r.l_dhid.at[m // 2]))

        def gather_da2(cols):
            part = rdot(r.dhid[m], w_up[m][cols, :])
            r.dsecond[:, cols] = part if m == theirs[0] else r.dsecond[:, cols] + part

        by_tiles(model, 4 * COLS, gather_da2)
    got_dffn.wait_recv()
    for y in range(ny):
        got_active[y].wait_recv()
        store(r.g_down, y, r.dffn, r.active.at[2 * y], r.l_dffn, r.l_active.at[y])
    for y in range(ny):
        got_dhid[y].wait_recv()
        store(r.g_up, y, r.a2, r.dhid.at[2 * y], r.l_a2, r.l_dhid.at[y])

    def second_back(i, acc):
        here = pl.ds(pl.multiple_of(i * TILE, TILE), TILE)
        xhat, scale = norm_parts(r.second[here])
        da = r.dsecond[here]
        dsecond = r.ffn[here] + norm_turn(da, xhat, scale, row(2))
        r.dsecond[here] = dsecond
        r.dattn[here] = dsecond.astype(bf)
        return acc[0] + fold(da * xhat), acc[1] + fold(da)

    dgain, dbias = lax.fori_loop(0, rows // TILE, second_back, (zero, zero))
    r.extra[0:1] = dgain
    r.extra[1:2] = dbias
    for m in range(nmp):
        r.dmixed[m] = dot(r.dattn[...], w_out[m][...]).astype(bf)
    for copy in stored[-2:]:
        copy.wait()
    for copy in crossings:
        copy.wait_send()


def middle_all(ndp, nmp, given):
    rows, model = given.second.shape
    ny = nmp // 2
    hid = given.active.shape[2]
    c_out = given.mid.shape[2] - hid
    dma = pltpu.SemaphoreType.DMA
    anywhere = pl.BlockSpec(memory_space=pl.ANY)
    struct = jax.ShapeDtypeStruct
    outs = [
        struct((ny, model, hid), bf),
        struct((ny, model, hid), bf),
        struct((rows, model), f32),
        struct((rows, model), bf),
        struct((nmp, rows, c_out), bf),
        struct((8, model), f32),
        struct((model, 128), bf),
        struct((8, 128), f32),
    ]
    flat, tall = pltpu.VMEM((rows, model), f32), pltpu.VMEM((rows, model), bf)
    scratch = [
        flat,
        tall,
        tall,
        tall,
        pltpu.VMEM((ny, rows, hid), bf),
        pltpu.VMEM((ny, rows, hid), bf),
        pltpu.VMEM((nmp, rows, hid), bf),
        tall,
        pltpu.VMEM((2, model, hid), bf),
        pltpu.VMEM(given.mid.shape, bf),
        pltpu.VMEM(given.down.shape, bf),
        dma((8,)),
        dma((8,)),
        dma((2 * nmp + 2 * ny,)),
    ]
    outs = pl.pallas_call(
        functools.partial(middle_kernel, ndp, nmp),
        name="middle",
        out_shape=outs,
        in_specs=[SMEM] + [VMEM] * 7 + [anywhere] * 2,
        out_specs=[anywhere] * 2 + [VMEM] * 6,
        scratch_shapes=scratch,
        compiler_params=pltpu.CompilerParams(
            collective_id=2, has_side_effects=True, vmem_limit_bytes=62 << 20
        ),
    )(*given)
    return MiddleOut(*outs)


def back_kernel(ndp, nmp, *refs):
    r = BackRefs(*refs)
    wires = Wires(ndp, nmp)
    sizes = wires.sizes
    rows, model = r.dattn.shape
    ny = sizes["y"]
    seq = wires.at["c"]
    nears = [wires.near(k) for k in range(1, nmp)]
    fars = [wires.far(k) for k in range(1, ndp)]
    wires.align(r.again)
    pending = []
    size = r.places[2]

    count = iter(range(16))

    def cross(src, dst):
        i = next(count)
        copy = Crossing(src, dst, r.c_send, r.c_recv, i, wires)
        copy.make().start()
        pending.append(copy)
        return copy

    def sent(copy):
        copy.wait_send()
        pending[:] = [c for c in pending if c is not copy]

    locals_used = []

    def fetch(src, dst):
        copy = pltpu.make_async_copy(src, dst, r.local.at[len(locals_used)])
        copy.start()
        locals_used.append(copy)
        return copy

    flows = []

    def wide_flow(term, out, box, half, order):
        height = term.shape[1] // ndp // 2
        n = len(flows)

        def source(k):
            start = (k["z"] * sizes["x"] + k["x"]) * 2 * height + half * height
            return term.at[k["y"], pl.ds(start, height)]

        def landing(k):
            return box.at[slot_number(sizes, k) // sizes["c"] - 1]

        here = out.at[pl.ds(half * height, height)]
        flows.append(
            Reduce(wires, order, source, landing, here, r.send.at[n], r.recv.at[n])
        )
        return flows[-1]

    def both(term, out, *boxes):
        orders = (("y", "x", "z"), ("x", "y", "z"))
        return [wide_flow(term, out, boxes[h], h, order) for h, order in enumerate(orders)]

    def thin_source(k):
        height = r.o_thin.shape[0]
        block = (k["z"] * sizes["x"] + k["x"]) * nmp + wires.owner_mp(k["y"], k["c"])
        return r.thin.at[pl.ds(pl.multiple_of(block * height, height), height)]

    down_flows = both(r.g_down, r.o_down, r.l_down0, r.l_down1)
    up_flows = both(r.g_up, r.o_up, r.l_up0, r.l_up1)
    out_flows = both(r.g_out, r.o_out, r.l_out0, r.l_out1)
    qkv_flows = both(r.g_qkv, r.o_qkv, r.l_qkv0, r.l_qkv1)
    n = len(flows)
    thin_flow = Reduce(
        wires, ("c", "y", "x", "z"), thin_source,
        lambda k: r.l_thin.at[slot_number(sizes, k) - 1],
        r.o_thin, r.send.at[n], r.recv.at[n],
    )
    flows.append(thin_flow)
    turns = iter(BACK_TURNS)
    slots = ndp * nmp

    def turn():
        for code in next(turns):
            flow = flows[code // (2 * slots)]
            if code // slots % 2:
                flow.depart(code % slots)
            else:
                flow.arrive(code % slots)

    mine = [m for m in range(nmp) if m % 2 == 0]
    theirs = [m for m in range(nmp) if m % 2]
    for f in down_flows + up_flows:
        f.keep()
    turn()
    got_dattn = cross((r.dattn,), (r.l_dattn,))
    got_mixed = [cross((r.mixed, m), (r.l_mixed, m // 2)) for m in theirs]

    got_other = {}
    loads = {m: fetch(r.w_qkv.at[m], r.w_buf.at[m]) for m in range(2)}

    def attention(packed, other, mixed_t, dmixed, dist):
        copies = [
            fetch(src, ref)
            for src, ref in (
                (r.packed, packed), (r.other, other), (r.mixed_t, mixed_t), (r.dmixed, dmixed)
            )
        ]
        distances(dist, r.places[0], r.places[1], size)
        turn()
        got_dattn.wait_recv()
        for copy in got_mixed:
            copy.wait_recv()
        for y in range(ny):
            g = tdot(r.dattn[...], r.mixed[2 * y])
            r.g_out[y] = (g + tdot(r.l_dattn[...], r.l_mixed[y])).astype(bf)
        for f in out_flows:
            f.keep()
        for copy in copies:
            copy.wait()
        leaving = []
        for m in theirs + mine:
            slot = len(leaving) % 2
            if len(leaving) >= 2:
                sent(leaving[-2])
            for _ in attend_back(
                packed, other, dist, r.slopes, mixed_t, r.lse, dmixed,
                r.down, r.dother.at[slot], m,
            ):
                turn()
            twin = m + 1 - 2 * (m % 2)
            leaving.append(cross((r.dother, slot), (r.l_other, twin)))
            got_other[twin] = leaving[-1]

    chunks, _, width = r.packed.shape
    pl.run_scoped(
        attention,
        pltpu.VMEM(r.packed.shape, bf),
        pltpu.VMEM(r.other.shape, bf),
        pltpu.VMEM(r.mixed_t.shape, f32),
        pltpu.VMEM(r.dmixed.shape, bf),
        pltpu.VMEM((2 * rows, rows), f32),
    )

    lane = lax.broadcasted_iota(jnp.int32, (TILE, width), 1)
    is_query = lax.rem(lane, 3 * HEAD_DIM) < HEAD_DIM

    def front(first, conv, back, hm, features, dconv, gtaps):
        copies = [
            fetch(src, ref)
            for src, ref in (
                (r.first, first), (r.conv, conv), (r.dsecond, back), (r.hm, hm),
                (r.features.at[pl.ds(PAD, rows)], features),
            )
        ]
        copies[0].wait()
        gain = r.chan[KERNEL][None]
        bias = r.chan[KERNEL + 1][None]

        def act(i, _):
            here = pl.ds(pl.multiple_of(i * TILE, TILE), TILE)
            xhat, _ = norm_parts(first[here])
            r.a1[here] = (xhat * gain + bias).astype(bf)
            return 0

        lax.fori_loop(0, rows // TILE, act, 0)
        got_a1 = cross((r.a1,), (r.l_a1,))
        turn()

        def combine(m):
            got_other[m].wait_recv()

            def body(i, _):
                here = pl.ds(pl.multiple_of(i * TILE, TILE), TILE)
                own = r.down[m, here].astype(f32)
                more = own + r.l_other[m, here].astype(f32)
                r.down[m, here] = jnp.where(is_query, own, more).astype(bf)
                return 0

            lax.fori_loop(0, rows // TILE, body, 0)

        got_pack = []
        for m in theirs:
            combine(m)
            got_pack.append(cross((r.down, m), (r.l_dpack, m // 2)))
        for m in mine:
            combine(m)
        turn()
        got_a1.wait_recv()
        for y in range(ny):
            got_pack[y].wait_recv()
            g = tdot(r.a1[...], r.down[2 * y])
            r.g_qkv[y] = (g + tdot(r.l_a1[...], r.l_dpack[y])).astype(bf)
            turn()
        for f in qkv_flows:
            f.keep()
        inner = pl.ds(PAD, rows)
        for m in range(chunks):
            loads[m].wait()
            part = rdot(r.down[m], r.w_buf[m % 2])
            dconv[inner] = part if m == 0 else dconv[inner] + part
            if m + 2 < chunks:
                loads[m + 2] = fetch(r.w_qkv.at[m + 2], r.w_buf.at[m % 2])
            turn()
        for copy in copies[1:]:
            copy.wait()
        r.rows_buf[...] = jnp.zeros_like(r.rows_buf)
        r.rows_buf[KERNEL + 2 : KERNEL + 6] = r.extra[0:4]

        def norm(i, sums_in):
            here = pl.ds(pl.multiple_of(i * TILE, TILE), TILE)
            xhat, scale = norm_parts(first[here])
            shifted = pl.ds(pl.multiple_of(i * TILE + PAD, PAD), TILE)
            da = dconv[shifted]
            dx = da * gain
            dv = scale * (
                dx
                - jnp.mean(dx, axis=-1, keepdims=True)
                - xhat * jnp.mean(dx * xhat, axis=-1, keepdims=True)
            )
            dfirst = back[here] + dv
            first[here] = dfirst
            dc = dfirst * gelu_slope(conv[here])
            dconv[shifted] = dc
            return tuple(a + fold(b) for a, b in zip(sums_in, (da * xhat, da, dc)))

        zero = jnp.zeros((1, model), f32)
        dgain, dbias, dcsum = lax.fori_loop(0, rows // TILE, norm, (zero, zero, zero))
        r.rows_buf[KERNEL : KERNEL + 1] = dgain
        r.rows_buf[KERNEL + 1 : KERNEL + 2] = dbias
        r.rows_buf[KERNEL + 7 : KERNEL + 8] = dcsum
        r.edge[0] = dconv[PAD : 2 * PAD]
        r.edge[1] = dconv[rows : rows + PAD]
        got_edge = cross((r.edge,), (r.halo,))
        turn()
        got_edge.wait_recv()
        dconv[0:PAD] = jnp.where(seq == 0, 0.0, r.halo[1])
        dconv[rows + PAD :] = jnp.where(seq == 0, r.halo[0], 0.0)
        gtaps[...] = jnp.zeros_like(gtaps)
        for c in range(0, model, 128):
            convolve_back(dconv, hm, r.chan, back, gtaps, c)
            turn()

        def finish(i, acc):
            here = pl.ds(pl.multiple_of(i * TILE, TILE), TILE)
            place = r.places[0] + i * TILE + lax.broadcasted_iota(jnp.int32, (TILE, 1), 0)
            dstart = first[here] + jnp.where(place < size, back[here], 0.0)
            r.a1[here] = dstart.astype(bf)
            return acc + fold(dstart)

        sent(got_a1)
        r.rows_buf[KERNEL + 6 : KERNEL + 7] = lax.fori_loop(0, rows // TILE, finish, zero)
        for k in range(KERNEL):
            r.rows_buf[k : k + 1] = fold(gtaps[8 * k : 8 * k + 8])
        r.thin[:, :THIN_CHAN] = tdot(r.a1[...], features[...]).astype(bf)
        for i in range(0, model, 128):
            r.thin[i : i + 128, THIN_CHAN:THIN_HEAD] = r.rows_buf[:, i : i + 128].T.astype(bf)
        r.thin[:, THIN_HEAD:] = r.g_head[...]

    pl.run_scoped(
        front,
        pltpu.VMEM((rows, model), f32),
        pltpu.VMEM((rows, model), f32),
        pltpu.VMEM((rows, model), f32),
        pltpu.VMEM((rows + 2 * PAD, model), f32),
        pltpu.VMEM((rows, r.features.shape[1]), bf),
        pltpu.VMEM((rows + 2 * PAD, model), f32),
        pltpu.VMEM((8 * KERNEL, model), f32),
    )
    thin_flow.keep()
    turn()
    assert next(turns, None) is None
    for f in flows:
        f.finish()
    for copy in pending:
        copy.wait_send()

    squares = None
    for out in (r.o_thin, r.o_up, r.o_down, r.o_qkv, r.o_out):
        part = total(out)
        squares = part if squares is None else squares + part
    lanes = lax.broadcasted_iota(jnp.int32, (8, 128), 1)
    block = jnp.where(lanes == 1, squares, r.loss[...])
    parts = r.parts
    for peers, sends, recvs, lower in (
        (nears, r.near_send, r.near_recv, 0),
        (fars, r.far_send, r.far_recv, nmp),
    ):
        parts[lower] = block
        copies = []
        for i, p in enumerate(peers):
            copy = pltpu.make_async_remote_copy(
                parts.at[lower], parts.at[lower + 1 + i], sends.at[i], recvs.at[i],
                device_id=p, device_id_type=MESH,
            )
            copy.start()
            copies.append(copy)
        for copy in copies:
            copy.wait()
        for i in range(len(peers)):
            block = block + parts[lower + 1 + i]
    r.sums[...] = block


def back_all(ndp, nmp, given):
    rows, model = given.dattn.shape
    ny = nmp // 2
    width = given.packed.shape[2]
    c_out = given.mixed.shape[2]
    c_up = given.g_up.shape[2]
    height = model // ndp
    pairs = (ndp * ny - 1, height // 2)
    dma = pltpu.SemaphoreType.DMA
    wide = (c_up, given.g_down.shape[2], width, c_out)
    outs = [jax.ShapeDtypeStruct((height // nmp, THIN), f32)]
    outs += [jax.ShapeDtypeStruct((height, n), f32) for n in wide]
    outs += [jax.ShapeDtypeStruct((8, 128), f32)]
    scratch = [
        pltpu.VMEM((ny, model, width), bf),
        pltpu.VMEM((ny, model, c_out), bf),
        pltpu.VMEM((model, THIN), bf),
    ]
    for n in wide:
        scratch += [pltpu.VMEM((*pairs, n), bf)] * 2
    scratch += [
        pltpu.VMEM((ndp * nmp - 1, height // nmp, THIN), bf),
        pltpu.VMEM((nmp, rows, width), bf),
        pltpu.VMEM((2, rows, width), bf),
        pltpu.VMEM((nmp, rows, width), bf),
        pltpu.VMEM((rows, model), bf),
        pltpu.VMEM((rows, model), bf),
        pltpu.VMEM((rows, model), bf),
        pltpu.VMEM((ny, rows, c_out), bf),
        pltpu.VMEM((ny, rows, width), bf),
        pltpu.VMEM((2, PAD, model), f32),
        pltpu.VMEM((2, PAD, model), f32),
        pltpu.VMEM((nmp + ndp, 8, 128), f32),
        pltpu.VMEM((2, model, width), bf),
        pltpu.VMEM((128, model), f32),
        dma((9, ndp * nmp)),
        dma((9, ndp * nmp)),
        dma((16,)),
        dma((16,)),
        dma((16,)),
        dma((nmp - 1,)),
        dma((nmp - 1,)),
        dma((ndp - 1,)),
        dma((ndp - 1,)),
        pltpu.SemaphoreType.REGULAR,
    ]
    anywhere = pl.BlockSpec(memory_space=pl.ANY)
    specs = [SMEM] * 2 + [VMEM] * 8 + [anywhere] * 3 + [VMEM] * 1 + [anywhere] * 7
    return pl.pallas_call(
        functools.partial(back_kernel, ndp, nmp),
        name="back",
        out_shape=outs,
        in_specs=specs,
        out_specs=[VMEM] * len(outs),
        scratch_shapes=scratch,
        compiler_params=pltpu.CompilerParams(
            collective_id=1, has_side_effects=True, vmem_limit_bytes=62 << 20
        ),
    )(*given)


def step_kernel(sums, g_thin, g_qkv, g_out, g_up, g_down, *refs):
    weights, firsts, seconds = refs[:7], refs[7:14], refs[14:21]
    loss, grad_norm = refs[21:23]
    outs = refs[23:]
    norm = jnp.sqrt(sums[0:1, 1:2])
    loss[...] = sums[0:1, 0:1]
    grad_norm[...] = norm
    factor = CLIP_AT / jnp.maximum(norm, CLIP_AT)

    def update(i, here, grad):
        new = adam_update(weights[i][here], firsts[i][here], seconds[i][here], grad, factor)
        for n in range(3):
            outs[3 * i + n][here] = new[n]

    inputs, channels = weights[0].shape[1], weights[1].shape[1]
    mel = weights[6].shape[1]
    every = slice(None)
    update(0, every, g_thin[:, :THIN_CHAN][:, :inputs])
    update(1, every, g_thin[:, THIN_CHAN:THIN_HEAD][:, :channels])
    update(6, every, g_thin[:, THIN_HEAD:][:, :mel])
    for i, grad in ((2, g_qkv), (4, g_up)):
        by_tiles(grad.shape[0], 16, lambda here, i=i, grad=grad: update(i, here, grad[here]))
    for i, grad in ((3, g_out), (5, g_down)):
        by_tiles(grad.shape[1], 128, lambda here, i=i, grad=grad: update(i, here, grad[:, here].T))


def step_all(sums, grads, state):
    state = [x.T if i % 7 < 2 else x for i, x in enumerate(state)]
    one = jax.ShapeDtypeStruct((1, 1), f32)
    outs = [jax.ShapeDtypeStruct(state[i].shape, f32) for i in range(7) for _ in range(3)]
    loss, norm, *new = pl.pallas_call(
        step_kernel,
        name="step",
        out_shape=[one, one] + outs,
        in_specs=[VMEM] * 27,
        out_specs=[VMEM] * 23,
        compiler_params=pltpu.CompilerParams(vmem_limit_bytes=62 << 20),
    )(sums, *grads, *state)
    return (loss[0, 0], norm[0, 0], *[x.T for x in new[:6]], *new[6:])


def shards(
    clean_mel,
    noise_mel,
    lengths,
    span_start,
    span_end,
    phone_ids,
    flow_steps,
    in_table,
    channel_rows,
    attn_qkv,
    attn_out,
    ffn_up,
    ffn_down,
    mel_head,
    table_first,
    channel_first,
    qkv_first,
    merge_first,
    upward_first,
    downward_first,
    head_first,
    table_second,
    channel_second,
    qkv_second,
    merge_second,
    upward_second,
    downward_second,
    head_second,
):
    micro, units, length, mel = clean_mel.shape
    nmp = lax.axis_size("mp")
    seqs = nmp // micro
    rows = length // seqs
    mp = lax.axis_index("mp")
    batch = mp // seqs
    seq = mp % seqs
    base = seq * rows
    width = in_table.shape[0]
    nch = channel_rows.shape[0]

    c_qkv = attn_qkv.shape[1]
    c_out = attn_out.shape[0]
    c_up = ffn_up.shape[1]

    ndp = lax.axis_size("dp")
    spans = jnp.sum(span_end - span_start, axis=1)
    digits = jnp.stack([spans // 32, spans % 32], axis=1).reshape(1, -1)
    digits = jnp.broadcast_to(digits, (mel_head.shape[0], 2 * micro))

    def columns(x, size):
        return jnp.pad(x.astype(bf), ((0, 0), (0, size - x.shape[1])))

    thin = jnp.concatenate(
        [
            columns(in_table.T, THIN_CHAN),
            columns(channel_rows.T, THIN_HEAD - THIN_CHAN),
            columns(jnp.concatenate([mel_head, digits.astype(f32)], axis=1), THIN - THIN_HEAD),
        ],
        axis=1,
    )
    mid = jnp.concatenate([attn_out.T, ffn_up], axis=1).astype(bf)
    own = (ndp, nmp, seqs) == (8, 4, 2)
    def mine(x):
        return lax.dynamic_index_in_dim(x, batch, 0, keepdims=False)[0]

    def widen(x):
        x = jnp.pad(mine(x), [(PAD, PAD)] + [(0, 0)] * (x.ndim - 3))
        return lax.dynamic_slice_in_dim(x, base, rows + 2 * PAD, 0)

    size = mine(lengths)
    first_frame = mine(span_start)
    last_frame = mine(span_end)
    place = base - PAD + jnp.arange(rows + 2 * PAD)
    valid_ext = ((place >= 0) & (place < size)).astype(f32)[:, None]
    masked_ext = ((place >= first_frame) & (place < last_frame)).astype(f32)[:, None]
    inside = slice(PAD, PAD + rows)
    valid = valid_ext[inside]
    masked = masked_ext[inside]
    tau = mine(flow_steps).astype(f32) / TSTEPS
    clean = widen(clean_mel).astype(f32)
    noise = widen(noise_mel).astype(f32)
    noisy = (1.0 - (1.0 - SIGMA) * tau) * noise + tau * clean
    context = clean * (valid_ext * (1.0 - masked_ext))
    target = (clean - (1.0 - SIGMA) * noise)[inside]
    onehot = (widen(phone_ids)[:, None] == jnp.arange(PHONES)).astype(bf)
    features_ext = jnp.concatenate([noisy.astype(bf), context.astype(bf), onehot], axis=-1)
    features = features_ext[inside]

    wires = Wires(ndp, nmp)
    owners = [wires.owner_mp(m // 2, m % 2) if own else m for m in range(nmp)]
    owners = jnp.stack(owners) if own else jnp.arange(nmp)
    heads = (owners[:, None] * (HEADS // nmp) + jnp.arange(HEADS // nmp)).reshape(-1)
    slopes = jnp.exp2(-8.0 * (heads + 1).astype(f32) / HEADS)
    if own:
        numbers = [base, (1 - seq) * rows, size, first_frame, last_frame, batch, mel]
        places = jnp.stack([jnp.asarray(n, jnp.int32) for n in numbers])
        features_wide = columns(features_ext, THIN_CHAN)
        fore = fore_all(
            ndp,
            nmp,
            ForeIn(
                places=places,
                slopes=slopes,
                thin_own=thin,
                near_own=attn_qkv.astype(bf),
                mid_own=mid,
                down_own=ffn_down.T.astype(bf),
                features=features_wide,
            ),
        )
        thin = fore.thin
    else:
        thin = lax.all_gather(thin, ("dp", "mp"), axis=0, tiled=True)
        w_qkv = lax.all_gather(attn_qkv.astype(bf), ("mp", "dp"), axis=0, tiled=True)
        w_qkv = w_qkv.reshape(nmp, -1, c_qkv)
        rest = jnp.concatenate([mid, ffn_down.T.astype(bf)], axis=1)
        rest = lax.all_gather(rest, ("mp", "dp"), axis=0, tiled=True)
        rest = rest.reshape(nmp, -1, rest.shape[1])
        owners = jnp.arange(nmp)
    model = thin.shape[0]
    if own:
        middle = middle_all(
            ndp,
            nmp,
            MiddleIn(
                places=places,
                second=fore.second,
                a2=fore.a2,
                active=fore.active,
                slope=fore.slope,
                chan=fore.chan,
                thin=fore.thin,
                target=jnp.pad(target, ((0, 0), (0, 128 - mel))),
                mid=fore.mid,
                down=fore.down,
            ),
        )
        given = BackIn(
            places=places,
            slopes=slopes,
            loss=middle.loss,
            g_up=middle.g_up,
            g_down=middle.g_down,
            dattn=middle.dattn,
            mixed=fore.mixed,
            extra=middle.extra,
            g_head=middle.g_head,
            chan=fore.chan,
            packed=fore.packed,
            other=fore.other,
            mixed_t=fore.mixed_t,
            lse=fore.lse,
            dmixed=middle.dmixed,
            w_qkv=fore.near,
            first=fore.first,
            conv=fore.conv,
            dsecond=middle.dsecond,
            hm=fore.hm,
            features=features_wide,
        )
        g_thin, g_up, g_down, g_qkv, g_out, sums = back_all(ndp, nmp, given)
        state = (
            in_table, channel_rows, attn_qkv, attn_out, ffn_up, ffn_down, mel_head,
            table_first, channel_first, qkv_first, merge_first, upward_first, downward_first,
            head_first, table_second, channel_second, qkv_second, merge_second, upward_second,
            downward_second, head_second,
        )
        return step_all(sums, (g_thin, g_qkv, g_out, g_up, g_down), state)
    else:
        digits = thin[:, THIN_HEAD + mel : THIN_HEAD + mel + 2 * micro]
        digits = jnp.sum(digits.reshape(ndp, -1, 2 * micro)[:, 0].astype(f32), axis=0)
        count = lax.dynamic_slice_in_dim(digits, 2 * batch, 2, 0)
        count = count[0] * 32.0 + count[1]
        w_out = rest[:, :, :c_out]
        w_up = rest[:, :, c_out : c_out + c_up]
        w_down = rest[:, :, c_out + c_up :]
        w_in = thin[:, :width]
        channel = thin[:, THIN_CHAN : THIN_CHAN + nch].T.astype(f32)
        w_head = thin[:, THIN_HEAD : THIN_HEAD + mel]
        taps = channel[:KERNEL]
        vecs = channel[KERNEL:]

        start_ext = rdot(features_ext, w_in) + vecs[6]
        hm = start_ext * valid_ext
        conv = jnp.zeros((rows, model), f32) + vecs[7]
        for k in range(KERNEL):
            conv = conv + taps[k] * hm[k + 1 : k + 1 + rows]
        first = start_ext[inside] + gelu(conv)
        x_one, r_one = norm_parts(first)
        act_one = (x_one * vecs[0] + vecs[1]).astype(bf)

        groups = [[g * seqs + s for s in range(seqs)] for g in range(micro)]

        def shift(x, i):
            pairs = [(g[(s + i) % seqs], g[s]) for g in groups for s in range(seqs)]
            return lax.ppermute(x, "mp", pairs)

        def unshift(x, i):
            pairs = [(g[s], g[(s + i) % seqs]) for g in groups for s in range(seqs)]
            return lax.ppermute(x, "mp", pairs)

        packed = jnp.einsum("rd,mdc->rmc", act_one, w_qkv, preferred_element_type=f32).astype(bf)
        packed = packed.reshape(rows, HEADS, 3, HEAD_DIM)
        query, key, value = packed[:, :, 0], packed[:, :, 1], packed[:, :, 2]
        both = jnp.stack([key, value])
        both = jnp.concatenate([both] + [shift(both, i) for i in range(1, seqs)], axis=1)
        keys, values = both[0], both[1]
        blocks = (seq + jnp.arange(seqs)) % seqs
        key_place = (blocks[:, None] * rows + jnp.arange(rows)).reshape(-1)
        query_place = base + jnp.arange(rows)
        distance = jnp.abs(query_place[:, None] - key_place[None, :]).astype(f32)
        raw = jnp.einsum("qhd,khd->hqk", query, keys, preferred_element_type=f32)
        score = raw * SCALE - slopes[:, None, None] * distance
        score = jnp.where((key_place < size)[None, None, :], score, -1000000000.0)
        top = jnp.max(score, axis=-1, keepdims=True)
        prob = jnp.exp(score - top)
        prob = prob / jnp.sum(prob, axis=-1, keepdims=True)
        prob_low = prob.astype(bf)
        mixed = jnp.einsum("hqk,khd->qhd", prob_low, values, preferred_element_type=f32)
        mixed = mixed.astype(bf).reshape(rows, nmp, c_out)
        mixed = [mixed[:, m] for m in range(nmp)]
        attn = jnp.zeros((rows, model), f32)
        for m in range(nmp):
            attn = attn + rdot(mixed[m], w_out[m])
        second = first + attn

        x_two, r_two = norm_parts(second)
        act_two = (x_two * vecs[2] + vecs[3]).astype(bf)
        ffn = jnp.zeros((rows, model), f32)
        hidden = []
        active = []
        for m in range(nmp):
            hidden.append(dot(act_two, w_up[m]))
            active.append(gelu(hidden[m]).astype(bf))
            ffn = ffn + rdot(active[m], w_down[m])
        third = second + ffn

        x_three, r_three = norm_parts(third)
        act_three = (x_three * vecs[4] + vecs[5]).astype(bf)
        error = dot(act_three, w_head) - target
        weight_rows = masked / count
        loss_local = jnp.sum(weight_rows * error * error)
        dpred = (2.0 * weight_rows * error).astype(bf)
        g_head = tdot(act_three, dpred)
        dthird, dg3, db3 = norm_back(rdot(dpred, w_head), x_three, r_three, vecs[4])

        dffn = dthird.astype(bf)
        da2 = jnp.zeros((rows, model), f32)
        dhids = []
        for m in range(nmp):
            dhid = gelu_back(hidden[m], dot(dffn, w_down[m])).astype(bf)
            dhids.append(dhid)
            da2 = da2 + rdot(dhid, w_up[m])
        dnorm, dg2, db2 = norm_back(da2, x_two, r_two, vecs[2])
        dsecond = dthird + dnorm

        dattn = dsecond.astype(bf)
        g_out = [tdot(dattn, mixed[m]).astype(bf) for m in range(nmp)]
        dmixed = [dot(dattn, w_out[m]).astype(bf) for m in range(nmp)]
        dmixed = jnp.stack(dmixed, axis=1).reshape(rows, HEADS, HEAD_DIM)
        dvalues = jnp.einsum("hqk,qhd->khd", prob_low, dmixed, preferred_element_type=f32)
        dprob = jnp.einsum("qhd,khd->hqk", dmixed, values, preferred_element_type=f32)
        dscore = prob * (dprob - jnp.sum(prob * dprob, axis=-1, keepdims=True))
        draw = (dscore * SCALE).astype(bf)
        dquery = jnp.einsum("hqk,khd->qhd", draw, keys, preferred_element_type=f32)
        dkeys = jnp.einsum("hqk,qhd->khd", draw, query, preferred_element_type=f32)
        dboth = jnp.stack([dkeys, dvalues])
        parts = [dboth[:, i * rows : (i + 1) * rows] for i in range(seqs)]
        dboth = parts[0]
        for i in range(1, seqs):
            dboth = dboth + unshift(parts[i].astype(bf), i).astype(f32)
        dpacked = jnp.stack([dquery, dboth[0], dboth[1]], axis=2).astype(bf)
        dpacked = dpacked.reshape(rows, nmp, c_qkv)
        dpacked = [dpacked[:, m] for m in range(nmp)]
        g_qkv = [tdot(act_one, dpacked[m]).astype(bf) for m in range(nmp)]
        da1 = jnp.zeros((rows, model), f32)
        for m in range(nmp):
            da1 = da1 + rdot(dpacked[m], w_qkv[m])

        dnorm, dg1, db1 = norm_back(da1, x_one, r_one, vecs[0])
        dfirst = dsecond + dnorm
        dconv = gelu_back(conv, dfirst)
        right = lax.ppermute(
            dconv[:PAD], "mp", [(g[s + 1], g[s]) for g in groups for s in range(seqs - 1)]
        )
        left = lax.ppermute(
            dconv[rows - PAD :], "mp", [(g[s], g[s + 1]) for g in groups for s in range(seqs - 1)]
        )
        dconv_ext = jnp.concatenate([left, dconv, right], axis=0)
        back = jnp.zeros((rows, model), f32)
        g_taps = []
        for k in range(KERNEL):
            back = back + taps[k] * dconv_ext[2 * PAD - 1 - k : 2 * PAD - 1 - k + rows]
            g_taps.append(jnp.sum(dconv * hm[k + 1 : k + 1 + rows], axis=0))
        dstart = dfirst + valid * back
        g_in = tdot(dstart.astype(bf), features)
        g_rows = g_taps + [dg1, db1, dg2, db2, dg3, db3, jnp.sum(dstart, axis=0), jnp.sum(dconv, axis=0)]
        g_chan = jnp.stack(g_rows, axis=1)

        g_thin = jnp.concatenate(
            [
                columns(g_in, THIN_CHAN),
                columns(g_chan, THIN_HEAD - THIN_CHAN),
                columns(g_head, THIN - THIN_HEAD),
            ],
            axis=1,
        )
        g_up = [tdot(act_two, dhids[m]).astype(bf) for m in range(nmp)]
        g_down = [tdot(dffn, active[m]).astype(bf) for m in range(nmp)]
        terms = [g_thin, jnp.stack(g_up), jnp.stack(g_down), jnp.stack(g_qkv), jnp.stack(g_out)]
        g_thin = lax.psum_scatter(g_thin, ("dp", "mp"), scatter_dimension=0, tiled=True)
        sums = [g_thin.astype(f32)] + [
            lax.psum_scatter(
                t.reshape(-1, t.shape[2]), ("mp", "dp"), scatter_dimension=0, tiled=True
            ).astype(f32)
            for t in terms[1:]
        ]
        g_thin, g_up, g_down, g_qkv, g_out = sums
        squares = sum(jnp.sum(g * g) for g in sums)
        sums = lax.psum(jnp.stack([loss_local, squares])[None], ("dp", "mp"))
    sums = sums[0]
    loss = sums[0]
    grad_norm = jnp.sqrt(sums[1])
    factor = CLIP_AT / jnp.maximum(grad_norm, CLIP_AT)

    tw, tm, tv = adam_update(in_table, table_first, table_second, g_thin[:, :width].T, factor)
    cw, cm, cv = adam_update(
        channel_rows, channel_first, channel_second, g_thin[:, THIN_CHAN : THIN_CHAN + nch].T, factor
    )
    hw, hm_, hv = adam_update(mel_head, head_first, head_second, g_thin[:, THIN_HEAD : THIN_HEAD + mel], factor)
    qw, qm, qv = adam_update(attn_qkv, qkv_first, qkv_second, g_qkv, factor)
    ow, om, ov = adam_update(attn_out, merge_first, merge_second, g_out.T, factor)
    uw, um, uv = adam_update(ffn_up, upward_first, upward_second, g_up, factor)
    dw, dm, dv = adam_update(ffn_down, downward_first, downward_second, g_down.T, factor)
    return (
        loss, grad_norm,
        tw, tm, tv, cw, cm, cv, qw, qm, qv, ow, om, ov, uw, um, uv, dw, dm, dv, hw, hm_, hv,
    )


def solution(mesh):
    wide = P(None, ("dp", "mp"))
    tall = P(("dp", "mp"), None)
    down = P("dp", "mp")
    flat = P("mp", "dp")
    weights = (wide, wide, down, flat, down, flat, tall)
    pair = P(None, "dp")
    data = (P(None, "dp", None, None), P(None, "dp", None, None), pair, pair, pair)
    data = data + (P(None, "dp", None), pair)
    return jax.shard_map(
        shards,
        mesh=mesh,
        in_specs=data + weights * 3,
        out_specs=(P(), P()) + tuple(w for w in weights for _ in range(3)),
        check_vma=False,
    )
```
